256 devices in a mesh: sample: 8 (over z), space: 32 (over y, x, core).
Axes of the slice: x: 4, y: 4, z: 8, core: 2. Of those that a mesh axis runs over, the one named last changes fastest.
Arguments:
- volume: bfloat16 [256, 8, 4, 16, 128], P(('sample', 'space')), may hold values from -6 to 6
- grad_out: bfloat16 [256, 1, 2, 16, 128], P(('sample', 'space')), may hold values from -6 to 6
- filter_one: bfloat16 [3, 3, 3, 4, 32], replicated, may hold values from -0.625 to 0.625
- filter_two: bfloat16 [3, 3, 3, 32, 64], replicated, may hold values from -0.21875 to 0.21875
- filter_three: bfloat16 [3, 3, 3, 64, 128], replicated, may hold values from -0.15625 to 0.15625
Outputs:
- grad_one: float32 [3, 3, 3, 4, 32], replicated
- grad_two: float32 [3, 3, 3, 32, 64], replicated
- grad_three: float32 [3, 3, 3, 64, 128], replicated
The draws below stay inside these ranges and needn't reach their ends.
All inputs are finite; a program needn't handle non-finite values.
Results may differ from the reference program's by a relative error of at most 0.011.
Values may be sent and summed in bfloat16 or wider, within the bound.
No kernel may reach another device: no remote copies, remote signals or barrier semaphores. Data moves between devices by JAX's collectives and lax.ppermute only.
A program may use at most 128 MiB of HBM per device.

```python
import jax
import jax.numpy as jnp
from jax import lax

CIN = 4
CH1 = 32
CH2 = 64
CH3 = 128
DEPTH = 256
HEIGHT = 16
WIDTH = 128
QUART = 32
BATCH = 8


def steps_of(rng, extent, shards, low, high):
    def one(axis_at, blocks):
        heights = jax.random.uniform(jax.random.fold_in(jax.random.fold_in(rng, 6), axis_at), (blocks,), jnp.float32, low / len(shards), high / len(shards))
        return jnp.repeat(jnp.exp(heights), extent[axis_at] // blocks).reshape((-1,) + (1,) * (len(extent) - axis_at - 1))

    gain = one(*shards[0])
    for cut in shards[1:]:
        gain = gain * one(*cut)
    return gain


def noise(key, extent, deviation, most, split=(), kind=jnp.bfloat16):
    values = jax.random.normal(key, extent, jnp.float32) * deviation
    if len(split) > 0:
        values = steps_of(key, extent, split, -0.22, 0.18) * values
    return jnp.clip(values, min=-most, max=most).astype(kind)


def setup_inputs(seed: int = 0) -> dict:
    key_list = jax.random.split(jax.random.key(seed), 6)
    return {
        "volume": noise(key_list[0], (BATCH * QUART, DEPTH // QUART, CIN, HEIGHT, WIDTH), 1.0, 6.0, ((0, 256),)),
        "grad_out": noise(key_list[1], (BATCH * QUART, DEPTH // (8 * QUART), HEIGHT // 8, WIDTH // 8, CH3), 1.0, 6.0, ((0, 256),)),
        "filter_one": noise(key_list[2], (3, 3, 3, CIN, CH1), (27 * CIN) ** -0.5, 0.625),
        "filter_two": noise(key_list[3], (3, 3, 3, CH1, CH2), (27 * CH1) ** -0.5, 0.21875),
        "filter_three": noise(key_list[4], (3, 3, 3, CH2, CH3), (27 * CH2) ** -0.5, 0.15625),
    }


def convolve(inputs, kernel, spec):
    return lax.conv_general_dilated(inputs, kernel, (1, 1, 1), 'SAME', dimension_numbers=(spec, 'DHWIO', 'NDHWC'), preferred_element_type=jnp.float32)

def reverse_kernel(kernel):
    return jnp.transpose(kernel[::-1, ::-1, ::-1], (0, 1, 2, 4, 3))

def pooled(values):
    nb, dd, hh, ww, cc = values.shape
    return values.reshape(nb, dd // 2, 2, hh // 2, 2, ww // 2, 2, cc).mean(axis=(2, 4, 6))

def expand(values):
    values = jnp.repeat(jnp.repeat(jnp.repeat(values, 2, axis=1), 2, axis=2), 2, axis=3)
    return values * 0.125

def slope(values):
    sig = jax.nn.sigmoid(values)
    return sig * (1.0 + values * (1.0 - sig))

def filter_grad(padded, delta, form):
    depth, rows, cols = (delta.shape[1], delta.shape[2], delta.shape[3])
    blocks = []
    for off_d in range(3):
        for off_h in range(3):
            for off_w in range(3):
                if form == 'last':
                    piece = padded[:, off_d:off_d + depth, off_h:off_h + rows, off_w:off_w + cols, :]
                    blocks.append(jnp.einsum('ndhwi,ndhwo->io', piece, delta, preferred_element_type=jnp.float32))
                else:
                    piece = padded[:, off_d:off_d + depth, :, off_h:off_h + rows, off_w:off_w + cols]
                    blocks.append(jnp.einsum('ndihw,ndhwo->io', piece, delta, preferred_element_type=jnp.float32))
    stacked = jnp.stack(blocks)
    return stacked.reshape(3, 3, 3, stacked.shape[1], stacked.shape[2])

def reference(volume, grad_out, filter_one, filter_two, filter_three):
    whole_vols = volume.reshape(BATCH, DEPTH, CIN, HEIGHT, WIDTH)
    placed = grad_out.reshape(BATCH, DEPTH // 8, HEIGHT // 8, WIDTH // 8, CH3)

    def one_volume(carry, item):
        sample_vol, sample_grad = item
        inputs = sample_vol[None]
        z_one = convolve(inputs, filter_one, 'NDCHW')
        p_one = pooled(jax.nn.silu(z_one)).astype(jnp.bfloat16)
        z_two = convolve(p_one, filter_two, 'NDHWC')
        p_two = pooled(jax.nn.silu(z_two)).astype(jnp.bfloat16)
        z_three = convolve(p_two, filter_three, 'NDHWC')
        d_three = (expand(sample_grad[None].astype(jnp.float32)) * slope(z_three)).astype(jnp.bfloat16)
        g_three = filter_grad(jnp.pad(p_two, ((0, 0), (1, 1), (1, 1), (1, 1), (0, 0))), d_three, 'last')
        q_two = convolve(d_three, reverse_kernel(filter_three), 'NDHWC').astype(jnp.bfloat16)
        q_two = lax.optimization_barrier(q_two).astype(jnp.float32)
        d_two = (expand(q_two) * slope(z_two)).astype(jnp.bfloat16)
        g_two = filter_grad(jnp.pad(p_one, ((0, 0), (1, 1), (1, 1), (1, 1), (0, 0))), d_two, 'last')
        q_one = convolve(d_two, reverse_kernel(filter_two), 'NDHWC')
        d_one = (expand(q_one) * slope(z_one)).astype(jnp.bfloat16)
        g_one = filter_grad(jnp.pad(inputs, ((0, 0), (1, 1), (0, 0), (1, 1), (1, 1))), d_one, 'first')
        return ((carry[0] + g_one, carry[1] + g_two, carry[2] + g_three), None)
    start = (jnp.zeros((3, 3, 3, CIN, CH1), jnp.float32), jnp.zeros((3, 3, 3, CH1, CH2), jnp.float32), jnp.zeros((3, 3, 3, CH2, CH3), jnp.float32))
    totals, unused = lax.scan(one_volume, start, (whole_vols, placed))
    cells = float(BATCH * DEPTH * HEIGHT * WIDTH)
    return (totals[0] / jnp.sqrt(jnp.float32(cells)), totals[1] / jnp.sqrt(jnp.float32(cells / 8.0)), totals[2] / jnp.sqrt(jnp.float32(cells / 64.0)))
```

```python
import jax
import jax.numpy as jnp
from jax import lax
from jax.sharding import PartitionSpec as P


def padded_2(shard, sides, width):
    for axis, dim in sides:
        size, length = (lax.axis_size(axis), shard.shape[dim])
        up = [(i, (i + 1) % size) for i in range(size - 1)]
        down = [(j, i) for i, j in up]
        last = lax.slice_in_dim(shard, length - width, length, axis=dim)
        initial = lax.slice_in_dim(shard, 0, width, axis=dim)
        before = lax.ppermute(last, axis, up)
        after = lax.ppermute(initial, axis, down)
        shard = jnp.concatenate([before, shard, after], axis=dim)
    return shard


def convolve(inputs, kernel, spec, padding):
    return lax.conv_general_dilated(
        inputs,
        kernel,
        (1, 1, 1),
        padding,
        dimension_numbers=(spec, "DHWIO", "NDHWC"),
        preferred_element_type=jnp.float32,
    )


def reverse_kernel(kernel):
    return jnp.transpose(kernel[::-1, ::-1, ::-1], (0, 1, 2, 4, 3))


def pooled(values):
    nb, dd, hh, ww, cc = values.shape
    return values.reshape(nb, dd // 2, 2, hh // 2, 2, ww // 2, 2, cc).mean(axis=(2, 4, 6))


def expand(values):
    values = jnp.repeat(jnp.repeat(jnp.repeat(values, 2, axis=1), 2, axis=2), 2, axis=3)
    return values * 0.125


def slope(values):
    sig = jax.nn.sigmoid(values)
    return sig * (1.0 + values * (1.0 - sig))


def filter_grad(padded, delta, form):
    depth, rows, cols = (delta.shape[1], delta.shape[2], delta.shape[3])
    blocks = []
    for off_d in range(3):
        for off_h in range(3):
            for off_w in range(3):
                if form == "last":
                    piece = padded[
                        :, off_d : off_d + depth, off_h : off_h + rows, off_w : off_w + cols, :
                    ]
                    blocks.append(
                        jnp.einsum(
                            "ndhwi,ndhwo->io", piece, delta, preferred_element_type=jnp.float32
                        )
                    )
                else:
                    piece = padded[
                        :, off_d : off_d + depth, :, off_h : off_h + rows, off_w : off_w + cols
                    ]
                    blocks.append(
                        jnp.einsum(
                            "ndihw,ndhwo->io", piece, delta, preferred_element_type=jnp.float32
                        )
                    )
    stacked = jnp.stack(blocks)
    return stacked.reshape(3, 3, 3, stacked.shape[1], stacked.shape[2])


def with_rims(values, first_block, last_block):
    extended = padded_2(values, (("space", 1),), 1)
    lower = jnp.where(first_block, jnp.zeros_like(extended[:, :1]), extended[:, :1])
    upper = jnp.where(last_block, jnp.zeros_like(extended[:, -1:]), extended[:, -1:])
    return jnp.concatenate([lower, extended[:, 1:-1], upper], axis=1)


def exchange(pieces, axis):
    return lax.all_to_all(pieces, axis, 0, 0, tiled=True)


def reduce_all(grads):
    spaces, samples = (lax.axis_size("space"), lax.axis_size("sample"))
    flat = jnp.concatenate([g.reshape(-1, 128).astype(jnp.bfloat16) for g in grads])
    rows = flat.shape[0]
    each = -(-rows // (16 * spaces)) * 16
    flat = jnp.pad(flat, ((0, each * spaces - rows), (0, 0)))
    got = exchange(flat.reshape(spaces, each, 128), "space")
    part = got.astype(jnp.float32).sum(axis=0).astype(jnp.bfloat16)
    got = exchange(jnp.broadcast_to(part[None], (samples, each, 128)), "sample")
    part = got.astype(jnp.float32).sum(axis=0).astype(jnp.bfloat16)
    got = exchange(jnp.broadcast_to(part[None], (spaces, each, 128)), "space")
    flat = got.reshape(-1, 128).astype(jnp.float32)
    totals, at = ([], 0)
    for g in grads:
        count = g.size // 128
        totals.append(flat[at : at + count].reshape(g.shape))
        at += count
    return totals


def per_device(volume, grad_out, filter_one, filter_two, filter_three):
    devices = lax.axis_size("space")
    place = lax.axis_index("space")
    first_block = place == 0
    last_block = place == devices - 1
    inner_pad = [(0, 0), (1, 1), (1, 1)]
    vol_ext = with_rims(volume, first_block, last_block)
    z_one = convolve(vol_ext, filter_one, "NDCHW", inner_pad)
    p_one = pooled(jax.nn.silu(z_one)).astype(jnp.bfloat16)
    p_one_ext = with_rims(p_one, first_block, last_block)
    z_two = convolve(p_one_ext, filter_two, "NDHWC", inner_pad)
    p_two = pooled(jax.nn.silu(z_two)).astype(jnp.bfloat16)
    p_two_ext = with_rims(p_two, first_block, last_block)
    z_three = convolve(p_two_ext, filter_three, "NDHWC", inner_pad)
    d_three = (expand(grad_out.astype(jnp.float32)) * slope(z_three)).astype(jnp.bfloat16)
    g_three = filter_grad(
        jnp.pad(p_two_ext, ((0, 0), (0, 0), (1, 1), (1, 1), (0, 0))), d_three, "last"
    )
    d_three_ext = with_rims(d_three, first_block, last_block)
    q_two = convolve(d_three_ext, reverse_kernel(filter_three), "NDHWC", inner_pad).astype(
        jnp.bfloat16
    )
    d_two = (expand(q_two.astype(jnp.float32)) * slope(z_two)).astype(jnp.bfloat16)
    g_two = filter_grad(jnp.pad(p_one_ext, ((0, 0), (0, 0), (1, 1), (1, 1), (0, 0))), d_two, "last")
    d_two_ext = with_rims(d_two, first_block, last_block)
    q_one = convolve(d_two_ext, reverse_kernel(filter_two), "NDHWC", inner_pad)
    d_one = (expand(q_one) * slope(z_one)).astype(jnp.bfloat16)
    g_one = filter_grad(jnp.pad(vol_ext, ((0, 0), (0, 0), (0, 0), (1, 1), (1, 1))), d_one, "first")
    cells = float(
        lax.axis_size("sample") * devices * volume.shape[1] * volume.shape[3] * volume.shape[4]
    )
    totals = reduce_all((g_one, g_two, g_three))
    return (
        totals[0] / jnp.sqrt(jnp.float32(cells)),
        totals[1] / jnp.sqrt(jnp.float32(cells / 8.0)),
        totals[2] / jnp.sqrt(jnp.float32(cells / 64.0)),
    )


def solution(mesh):
    return jax.shard_map(
        per_device,
        mesh=mesh,
        in_specs=(
            P(("sample", "space"), None, None, None, None),
            P(("sample", "space"), None, None, None, None),
            P(),
            P(),
            P(),
        ),
        out_specs=(P(), P(), P()),
        check_vma=False,
    )
```

```python
import jax
import jax.numpy as jnp
import numpy as np
from jax import lax
from jax.experimental import pallas as pl
from jax.experimental.pallas import tpu as pltpu
from jax.sharding import PartitionSpec as P

BF = jnp.bfloat16
F32 = jnp.float32
SLOT = 80


def one_hot_tables():
    def table(rows, cols):
        return np.zeros((rows, cols), np.float32)

    shift = table(128, 256)
    for w in range(128):
        if w >= 1:
            shift[w - 1, w] = 1.0
        if w + 1 < 128:
            shift[w + 1, 128 + w] = 1.0
    pair = table(256, 384)
    odd = table(256, 384)
    even = table(128, 384)
    for a in range(2):
        for kw in range(3):
            for w in range(64):
                src = w + kw - 1
                if 0 <= src < 64:
                    pair[128 * a + 2 * src, 128 * kw + 64 * a + w] = 1.0
                    odd[64 + 64 * a + src, 128 * kw + 64 * a + w] = 1.0
                    even[64 * a + src, 128 * kw + 64 * a + w] = 1.0
    squeeze = table(1024, 256)
    for m in range(8):
        for w in range(32):
            squeeze[128 * m + 2 * w, 32 * m + w] = 1.0
    spread3 = table(256, 2304)
    spread_b = table(256, 1152)
    for kd in range(3):
        for kw in range(3):
            at = 3 * kd + kw
            for w in range(32):
                src = w + kw - 1
                if 0 <= src < 32:
                    for n in range(6):
                        spread3[32 * (n + kd) + src, 256 * at + 32 * n + w] = 1.0
                    for n in range(4):
                        spread_b[32 * (n + kd) + src, 128 * at + 32 * n + w] = 1.0
    grow_g = table(48, 256)
    for b in range(3):
        for d in range(2):
            for w in range(32):
                grow_g[16 * b + w // 2, 32 * (2 * b + d) + w] = 1.0 / 16
    grow2 = table(128, 512)
    for n in range(4):
        for d in range(2):
            for w in range(64):
                grow2[32 * n + w // 2, 64 * (2 * n + d) + w] = 1.0 / 16
    grow1 = table(256, 512)
    for e in range(4):
        for w in range(128):
            grow1[64 * e + w // 2, 128 * e + w] = 1.0 / 16
    return [shift, pair, odd, even, squeeze, spread3, spread_b, grow_g, grow2, grow1]


def dot(a, b):
    return jnp.dot(a, b, preferred_element_type=F32)


def inside(index, count):
    return jnp.logical_and(index >= 0, index < count)


def body(
    place,
    vol_b2,
    vol_b1,
    vol_own,
    vol_a1,
    vol_a2,
    grad_own,
    base_one,
    filter_two,
    filter_three,
    shift,
    pair,
    odd,
    even,
    squeeze,
    spread3,
    spread_b,
    grow_g,
    grow2,
    grow1,
    out,
    t1,
    t2,
    t3,
    t3r,
    t2r,
    x1,
    pp,
    x2,
    q,
    x3,
    d3c,
    d2c,
    sl1,
    sl2,
    d2,
    d1,
    d2t,
    d3t,
):
    me = place[0]
    blocks = place[1]

    lane640 = lax.broadcasted_iota(jnp.int32, (32, 640), 1) % 16
    base = base_one[...]
    for h in range(16):
        moved = pltpu.roll(base, (h - 1) % 640, 1) if h != 1 else base
        if h == 0:
            moved = jnp.where(lane640 == 15, 0.0, moved)
        if h == 15:
            moved = jnp.where(lane640 == 0, 0.0, moved)
        t1[32 * h : 32 * h + 32, :] = moved[:, :576].astype(BF)

    def build(it, carry):
        kd = it // 3
        kw = it % 3
        taps = [kd * 9 + kh * 3 + kw for kh in range(3)]
        back = [(2 - kd) * 9 + (2 - kh) * 3 + (2 - kw) for kh in range(3)]
        w2 = [filter_two[k].astype(F32).T * 0.5 for k in taps]
        zero = jnp.zeros((64, 32), F32)
        for s in range(-6, 6):
            parts = [w2[s + j] if 0 <= s + j <= 2 else zero for j in range(4)]
            if -3 <= s <= 2:
                tile = jnp.concatenate(parts, axis=1).astype(BF)
            else:
                tile = jnp.zeros((64, 128), BF)
            for m in range(2):
                h = 4 * m + 1 - s
                if 0 <= h < 8:
                    t2[64 * h : 64 * h + 64, pl.ds(pl.multiple_of(it * 256 + 128 * m, 128), 128)] = tile
        w3 = [filter_three[k].astype(F32).T * 0.5 for k in taps]
        zero = jnp.zeros((128, 64), F32)
        for s in range(-2, 4):
            parts = [w3[s + j] if 0 <= s + j <= 2 else zero for j in range(2)]
            if -1 <= s <= 2:
                tile = jnp.concatenate(parts, axis=1).astype(BF)
            else:
                tile = jnp.zeros((128, 128), BF)
            for m in range(2):
                h = 2 * m + 1 - s
                if 0 <= h < 4:
                    t3[128 * h : 128 * h + 128, pl.ds(pl.multiple_of(it * 256 + 128 * m, 128), 128)] = tile
        v3 = [filter_three[k] for k in back]
        for hp in range(4):
            for h in range(4):
                kh = h - hp + 1
                tile = v3[kh] if 0 <= kh <= 2 else jnp.zeros((64, 128), BF)
                t3r[64 * hp : 64 * hp + 64, pl.ds(pl.multiple_of(it * 512 + 128 * h, 128), 128)] = tile
        v2 = [filter_two[k].astype(F32) for k in back]
        zero = jnp.zeros((32, 64), F32)
        for s in range(-6, 8):
            parts = [v2[s + j] if 0 <= s + j <= 2 else zero for j in range(2)]
            if -1 <= s <= 2:
                tile = jnp.concatenate(parts, axis=1).astype(BF)
            else:
                tile = jnp.zeros((32, 128), BF)
            for m in range(4):
                hp = 2 * m + 1 - s
                if 0 <= hp < 8:
                    t2r[32 * hp : 32 * hp + 32, pl.ds(pl.multiple_of(it * 512 + 128 * m, 128), 128)] = tile
        return carry

    lax.fori_loop(0, 9, build, 0)

    at = 0
    for ref, count in ((vol_b2, 7), (vol_b1, 8), (vol_own, 8), (vol_a1, 8), (vol_a2, 7)):
        rows = ref[: 64 * count, :]
        moved = dot(rows, shift[...]).astype(BF)
        for p in range(count):
            lanes = slice(128 * (at + p), 128 * (at + p) + 128)
            x1[0:64, lanes] = moved[64 * p : 64 * p + 64, :128]
            x1[64:128, lanes] = rows[64 * p : 64 * p + 64, :]
            x1[128:192, lanes] = moved[64 * p : 64 * p + 64, 128:]
        at += count

    def layer_one(j, own):
        rhs = jnp.concatenate(
            [x1[:, pl.ds(pl.multiple_of((2 * j + kd) * 128, 128), 256)] for kd in range(3)], axis=0
        )
        half = dot(t1[...], rhs)
        t = jnp.tanh(half)
        if own:
            slope = (1.0 + t) + half * (1.0 - t * t)
            sl1[:, pl.ds(pl.multiple_of((j - 7) * 256, 256), 256)] = slope.astype(BF)
        act = half + half * t
        act = act[:, :128] + act[:, 128:]
        act = act.reshape(8, 2, 32, 128)
        act = (act[:, 0] + act[:, 1]).reshape(256, 128)
        act = act + pltpu.roll(act, 127, 1)
        scale = jnp.where(inside(4 * me - 7 + j, 4 * blocks), 0.125, 0.0)
        pp[:, pl.ds(pl.multiple_of(j * 128, 128), 128)] = (act * scale).astype(BF)

    def loop_one(lo, hi, own):
        def step(j, carry):
            layer_one(j, own)
            return carry

        lax.fori_loop(lo, hi, step, 0)

    loop_one(0, 7, False)
    loop_one(7, 11, True)
    loop_one(11, 18, False)

    def gather_two(m, carry):
        for kd in range(3):
            got = dot(
                pp[:, pl.ds(pl.multiple_of((2 * m + kd) * 128, 128), 256)], pair[...]
            ).astype(BF)
            for kw in range(3):
                k = 3 * kd + kw
                x2[256 * k : 256 * k + 256, pl.ds(pl.multiple_of(m * 128, 128), 128)] = got[
                    :, 128 * kw : 128 * kw + 128
                ]
        return carry

    lax.fori_loop(0, 8, gather_two, 0)

    def layer_two(c, carry):
        lanes = pl.ds(pl.multiple_of(c * 256, 256), 256)
        half = dot(t2[...], x2[:, lanes])
        t = jnp.tanh(half)
        slope = (1.0 + t) + half * (1.0 - t * t)
        sl2[:, lanes] = slope.astype(BF)
        act = (half + half * t).reshape(4, 2, 64, 256)
        act = (act[:, 0] + act[:, 1]).reshape(256, 256)
        for u in range(2):
            tile = act[:, 128 * u : 128 * u + 128]
            tile = tile + pltpu.roll(tile, 64, 1)
            tile = tile + pltpu.roll(tile, 127, 1)
            m = 2 * c + u
            scale = jnp.where(inside(2 * me - 3 + m, 2 * blocks), 0.125, 0.0)
            q[:, pl.ds(pl.multiple_of(m * 128, 128), 128)] = (tile * scale).astype(BF)
        return carry

    lax.fori_loop(0, 4, layer_two, 0)

    packed = dot(q[...], squeeze[...]).astype(BF)
    for k in range(9):
        x3[256 * k : 256 * k + 256, :] = dot(
            packed, spread3[:, 256 * k : 256 * k + 256]
        ).astype(BF)
    half = dot(t3[...], x3[...])
    t = jnp.tanh(half)
    slope = (1.0 + t) + half * (1.0 - t * t)
    grown = []
    for hh in range(2):
        rows = jnp.concatenate(
            [
                vol_b1[512 + 16 * hh : 528 + 16 * hh, :],
                grad_own[16 * hh : 16 * hh + 16, :],
                vol_a1[512 + 16 * hh : 528 + 16 * hh, :],
            ],
            axis=0,
        )
        got = dot(rows.astype(F32).T.astype(BF), grow_g[...])
        grown += [got, got]
    delta = jnp.concatenate(grown, axis=0) * slope
    lane = lax.broadcasted_iota(jnp.int32, (512, 128), 1)
    d3t[...] = jnp.where(lane >= 64, delta[:, :128], 0.0).T.astype(BF)
    delta = delta.astype(BF)
    for k in range(9):
        d3c[512 * k : 512 * k + 512, :] = dot(
            delta, spread_b[:, 128 * k : 128 * k + 128]
        ).astype(BF)
    back = dot(t3r[...], d3c[...])
    lane = lax.broadcasted_iota(jnp.int32, (256, 128), 1)
    back = jnp.where(inside(2 * me - 1 + lane // 32, 2 * blocks), back, 0.0).astype(BF)
    back = dot(back, grow2[...])
    for h in range(8):
        rows = slice(64 * h, 64 * h + 64)
        delta = back[64 * (h // 2) : 64 * (h // 2) + 64, :] * sl2[rows, 256:768].astype(F32)
        d2t[:, rows] = delta[:, 128:384].T.astype(BF)
        d2[rows, :] = delta.astype(BF)

    for start in range(1, 6):
        u = start // 2
        if start % 2:
            got = dot(d2[:, 128 * u : 128 * u + 256], odd[...])
        else:
            got = dot(d2[:, 128 * u : 128 * u + 128], even[...])
        got = got.astype(BF)
        for kd in range(3):
            for m in range(2):
                if 1 + kd + 2 * m == start:
                    for kw in range(3):
                        k = 3 * kd + kw
                        d2c[512 * k : 512 * k + 512, 128 * m : 128 * m + 128] = got[
                            :, 128 * kw : 128 * kw + 128
                        ]
    back = dot(t2r[...], d2c[...]).astype(BF)
    back = dot(back, grow1[...])
    for h in range(16):
        rows = slice(32 * h, 32 * h + 32)
        source = back[32 * (h // 2) : 32 * (h // 2) + 32, :]
        for e in range(8):
            lanes = slice(128 * e, 128 * e + 128)
            delta = source[:, 128 * (e // 2) : 128 * (e // 2) + 128] * sl1[rows, lanes].astype(F32)
            d1[rows, lanes] = delta.astype(BF)

    def grad_three(it, carry):
        kd = it // 3
        kw = it % 3
        got = dot(x3[pl.ds(pl.multiple_of(it * 256, 256), 256), 0:128], d3t[...])
        for kh in range(3):
            total = None
            for h in range(4):
                hp = h + kh - 1
                if 0 <= hp < 4:
                    part = got[64 * hp : 64 * hp + 64, 128 * h : 128 * h + 128]
                    total = part if total is None else total + part
            k = kd * 9 + kh * 3 + kw
            out[pl.ds(pl.multiple_of(k * 64, 64), 64), :] = total.astype(BF)
        return carry

    lax.fori_loop(0, 9, grad_three, 0)

    lane16 = lax.broadcasted_iota(jnp.int32, (16, 128), 1)

    def grad_two(it, carry):
        kd = it // 3
        kw = it % 3
        got = dot(x2[pl.ds(pl.multiple_of(it * 256, 256), 256), 384:640], d2t[...])
        for kh in range(3):
            totals = [None, None]
            for h in range(8):
                hp = h + kh - 1
                if 0 <= hp < 8:
                    part = got[32 * hp : 32 * hp + 32, 128 * (h // 2) : 128 * (h // 2) + 128]
                    now = totals[h % 2]
                    totals[h % 2] = part if now is None else now + part
            low = totals[0] + pltpu.roll(totals[1], 64, 1)
            high = pltpu.roll(totals[0], 64, 1) + totals[1]
            k = kd * 9 + kh * 3 + kw
            out[pl.ds(pl.multiple_of(1728 + k * 16, 16), 16), :] = jnp.where(
                lane16 < 64, low[:16], high[16:]
            ).astype(BF)
        return carry

    lax.fori_loop(0, 9, grad_two, 0)

    lhs = jnp.concatenate([x1[:, 128 * (14 + kd) : 128 * (14 + kd) + 1024] for kd in range(3)], axis=0)
    got = lax.dot_general(lhs, d1[...], (((1,), (1,)), ((), ())), preferred_element_type=F32)
    row = lax.broadcasted_iota(jnp.int32, (576, 128), 0) % 16
    col = lax.broadcasted_iota(jnp.int32, (576, 128), 1) // 32
    lane36 = lax.broadcasted_iota(jnp.int32, (36, 128), 1)
    packed = jnp.zeros((36, 128), F32)
    for kh in range(3):
        total = jnp.zeros((576, 128), F32)
        for u in range(4):
            keep = row == col + (4 * u + kh - 1)
            total = total + jnp.where(keep, got[:, 128 * u : 128 * u + 128], 0.0)
        total = total.reshape(36, 16, 128).sum(axis=1)
        total = total + pltpu.roll(total, 64, 1)
        total = total + pltpu.roll(total, 32, 1)
        packed = packed + jnp.where(lane36 // 32 == kh, total, 0.0)
    out[2160:2208, :] = jnp.concatenate([packed, jnp.zeros((12, 128), F32)], axis=0).astype(BF)
    out[2208:, :] = jnp.zeros((out.shape[0] - 2208, 128), BF)


def local_grads(place, volumes, grad_own, base_one, filter_two, filter_three, rows):
    tables = [jnp.asarray(t, BF) for t in one_hot_tables()]
    vmem = pl.BlockSpec(memory_space=pltpu.VMEM)
    args = [*volumes, grad_own, base_one, filter_two, filter_three, *tables]
    return pl.pallas_call(
        body,
        out_shape=jax.ShapeDtypeStruct((rows, 128), BF),
        in_specs=[pl.BlockSpec(memory_space=pltpu.SMEM)] + [vmem] * len(args),
        out_specs=vmem,
        scratch_shapes=[
            pltpu.VMEM((512, 576), BF),
            pltpu.VMEM((512, 2304), BF),
            pltpu.VMEM((512, 2304), BF),
            pltpu.VMEM((256, 4608), BF),
            pltpu.VMEM((256, 4608), BF),
            pltpu.VMEM((192, 38 * 128), BF),
            pltpu.VMEM((256, 18 * 128), BF),
            pltpu.VMEM((2304, 1024), BF),
            pltpu.VMEM((256, 1024), BF),
            pltpu.VMEM((2304, 256), BF),
            pltpu.VMEM((4608, 128), BF),
            pltpu.VMEM((4608, 256), BF),
            pltpu.VMEM((512, 1024), BF),
            pltpu.VMEM((512, 1024), BF),
            pltpu.VMEM((512, 512), BF),
            pltpu.VMEM((512, 1024), BF),
            pltpu.VMEM((256, 512), BF),
            pltpu.VMEM((128, 512), BF),
        ],
        compiler_params=pltpu.CompilerParams(vmem_limit_bytes=58 * 1024 * 1024),
        name="local_grads",
    )(place, *args)


def exchange(pieces, axis):
    return lax.all_to_all(pieces, axis, 0, 0, tiled=True)


def total_of(got):
    return got.astype(F32).sum(axis=0).astype(BF)


def per_device(volume, grad_out, filter_one, filter_two, filter_three):
    spaces, samples = (lax.axis_size("space"), lax.axis_size("sample"))
    place = jnp.stack([lax.axis_index("space"), jnp.int32(spaces)]).astype(jnp.int32)
    vol = volume.reshape(512, 128)
    grad = grad_out.reshape(32, 128)
    both = jnp.concatenate([vol, grad], axis=0)

    def move(values, step):
        return lax.ppermute(
            values, "space", [(i, i + step) for i in range(spaces) if 0 <= i + step < spaces]
        )

    before1, after1 = (move(both, 1), move(both, -1))
    before2, after2 = (move(vol[64:], 2), move(vol[:448], -2))
    base_one = jnp.transpose(filter_one, (4, 0, 2, 3, 1)).astype(F32) * 0.5
    base_one = jnp.pad(base_one, ((0, 0), (0, 0), (0, 0), (0, 0), (0, 13))).reshape(32, 576)
    base_one = jnp.pad(base_one, ((0, 0), (0, 64)))
    flat = local_grads(
        place,
        (before2, before1, vol, after1, after2),
        grad,
        base_one,
        filter_two.reshape(27, 32, 64),
        filter_three.reshape(27, 64, 128),
        spaces * SLOT,
    )
    part = total_of(exchange(flat.reshape(spaces, SLOT, 128), "space"))
    part = total_of(exchange(jnp.broadcast_to(part[None], (samples, SLOT, 128)), "sample"))
    flat = exchange(jnp.broadcast_to(part[None], (spaces, SLOT, 128)), "space")
    flat = flat.reshape(-1, 128).astype(F32)
    cells = float(samples * spaces * volume.shape[1] * volume.shape[3] * volume.shape[4])
    g_three = flat[:1728].reshape(3, 3, 3, 64, 128)
    g_two = flat[1728:2160].reshape(3, 3, 3, 16, 128)
    g_two = jnp.concatenate([g_two[..., :64], g_two[..., 64:]], axis=3)
    g_one = jnp.transpose(flat[2160:2196, :96].reshape(3, 3, 4, 3, 32), (0, 3, 1, 2, 4))
    return (
        g_one / jnp.sqrt(jnp.float32(cells)),
        g_two / jnp.sqrt(jnp.float32(cells / 8.0)),
        g_three / jnp.sqrt(jnp.float32(cells / 64.0)),
    )


def solution(mesh):
    return jax.shard_map(
        per_device,
        mesh=mesh,
        in_specs=(
            P(("sample", "space"), None, None, None, None),
            P(("sample", "space"), None, None, None, None),
            P(),
            P(),
            P(),
        ),
        out_specs=(P(), P(), P()),
        check_vma=False,
    )
```

```python
import jax
import jax.numpy as jnp
import numpy as np
from jax import lax
from jax.experimental import pallas as pl
from jax.experimental.pallas import tpu as pltpu
from jax.sharding import PartitionSpec as P

BF = jnp.bfloat16
F32 = jnp.float32
SLOT = 80
G_TWO = 1728
G_ONE = 2160
NT = (((1,), (1,)), ((), ()))
TN = (((0,), (0,)), ((), ()))


def table(rows, cols):
    return np.zeros((rows, cols), np.float32)


def build_tables():
    perm = table(108, 640)
    for kd in range(3):
        for kh in range(3):
            for kw in range(3):
                for c in range(4):
                    row = ((kd * 3 + kh) * 3 + kw) * 4 + c
                    perm[row, ((kd * 3 + kw) * 4 + c) * 16 + kh] = 0.5
    return [perm]


def forward_tables():
    shift = table(128, 256)
    for w in range(128):
        if w >= 1:
            shift[w - 1, w] = 1.0
        if w + 1 < 128:
            shift[w + 1, 128 + w] = 1.0
    pair = table(256, 384)
    for a in range(2):
        for kw in range(3):
            for w in range(64):
                src = w + kw - 1
                if 0 <= src < 64:
                    pair[128 * a + 2 * src, 128 * kw + 64 * a + w] = 1.0
    squeeze = table(512, 128)
    for m in range(4):
        for w in range(32):
            squeeze[128 * m + 2 * w, 32 * m + w] = 1.0
    spread = table(128, 1152)
    for kd in range(3):
        for kw in range(3):
            at = 3 * kd + kw
            for w in range(32):
                src = w + kw - 1
                if 0 <= src < 32:
                    for n in range(2):
                        spread[32 * (n + kd) + src, 128 * at + 32 * n + w] = 1.0
    grow = table(16, 128)
    for d in range(2):
        for w in range(32):
            grow[w // 2, 32 * d + w] = 1.0 / 16
    return [shift, pair, squeeze, spread, grow]


def backward_tables():
    odd = table(256, 384)
    even = table(128, 384)
    for a in range(2):
        for kw in range(3):
            for w in range(64):
                src = w + kw - 1
                if 0 <= src < 64:
                    odd[64 + 64 * a + src, 128 * kw + 64 * a + w] = 1.0
                    even[64 * a + src, 128 * kw + 64 * a + w] = 1.0
    spread = table(256, 1152)
    for kd in range(3):
        for kw in range(3):
            at = 3 * kd + kw
            for w in range(32):
                src = w + kw - 1
                if 0 <= src < 32:
                    for n in range(4):
                        spread[32 * (n + kd) + src, 128 * at + 32 * n + w] = 1.0
    grow2 = table(128, 512)
    for n in range(4):
        for d in range(2):
            for w in range(64):
                grow2[32 * n + w // 2, 64 * (2 * n + d) + w] = 1.0 / 16
    grow1 = table(256, 512)
    for e in range(4):
        for w in range(128):
            grow1[64 * e + w // 2, 128 * e + w] = 1.0 / 16
    return [odd, even, spread, grow2, grow1]


def dot(a, b):
    return jnp.dot(a, b, preferred_element_type=F32)


def inside(index, count):
    return jnp.logical_and(index >= 0, index < count)


def position():
    return lax.axis_index("space"), lax.axis_size("space")


def taps_of(it):
    kd, kw = (it // 3, it % 3)
    return [kd * 9 + kh * 3 + kw for kh in range(3)]


def taps_back(it):
    kd, kw = (2 - it // 3, 2 - it % 3)
    return [kd * 9 + (2 - kh) * 3 + kw for kh in range(3)]


def build_forward(filter_one, filter_two, filter_three, perm, t1, t2, t3, s2, s3, sems):
    for it in range(9):
        w2 = [filter_two[k].astype(F32).T * 0.5 for k in taps_of(it)]
        zero = jnp.zeros((64, 32), F32)
        for s in range(-6, 6):
            if -3 <= s <= 2:
                parts = [w2[s + j] if 0 <= s + j <= 2 else zero for j in range(4)]
                tile = jnp.concatenate(parts, axis=1).astype(BF)
            else:
                tile = jnp.zeros((64, 128), BF)
            for m in range(2):
                h = 4 * m + 1 - s
                if 0 <= h < 8:
                    s2[64 * h : 64 * h + 64, it * 256 + 128 * m : it * 256 + 128 * m + 128] = tile
    copy2 = pltpu.make_async_copy(s2, t2, sems.at[0])
    copy2.start()
    for it in range(9):
        w3 = [filter_three[k].astype(F32).T * 0.5 for k in taps_of(it)]
        zero = jnp.zeros((128, 64), F32)
        for s in range(-2, 4):
            if -1 <= s <= 2:
                parts = [w3[s + j] if 0 <= s + j <= 2 else zero for j in range(2)]
                tile = jnp.concatenate(parts, axis=1).astype(BF)
            else:
                tile = jnp.zeros((128, 128), BF)
            for m in range(2):
                h = 2 * m + 1 - s
                if 0 <= h < 4:
                    s3[128 * h : 128 * h + 128, it * 256 + 128 * m : it * 256 + 128 * m + 128] = tile
    copy3 = pltpu.make_async_copy(s3, t3, sems.at[1])
    copy3.start()
    lane = lax.broadcasted_iota(jnp.int32, (32, 640), 1) % 16
    base = lax.dot_general(filter_one[...], perm[...], TN, preferred_element_type=F32)
    for h in range(16):
        moved = pltpu.roll(base, (h - 1) % 640, 1) if h != 1 else base
        if h == 0:
            moved = jnp.where(lane == 15, 0.0, moved)
        if h == 15:
            moved = jnp.where(lane == 0, 0.0, moved)
        t1[32 * h : 32 * h + 32, :] = moved[:, :576].astype(BF)
    copy2.wait()
    copy3.wait()


def build_backward(filter_two, filter_three, t3r, t2r, s3, s2, sems):
    for it in range(9):
        v3 = [filter_three[k] for k in taps_back(it)]
        for hp in range(4):
            for h in range(4):
                kh = h - hp + 1
                tile = v3[kh] if 0 <= kh <= 2 else jnp.zeros((64, 128), BF)
                s3[64 * hp : 64 * hp + 64, it * 512 + 128 * h : it * 512 + 128 * h + 128] = tile
    copy3 = pltpu.make_async_copy(s3, t3r, sems.at[0])
    copy3.start()
    for it in range(9):
        v2 = [filter_two[k].astype(F32) for k in taps_back(it)]
        zero = jnp.zeros((32, 64), F32)
        for s in range(-6, 8):
            if -1 <= s <= 2:
                parts = [v2[s + j] if 0 <= s + j <= 2 else zero for j in range(2)]
                tile = jnp.concatenate(parts, axis=1).astype(BF)
            else:
                tile = jnp.zeros((32, 128), BF)
            for m in range(4):
                hp = 2 * m + 1 - s
                if 0 <= hp < 8:
                    s2[32 * hp : 32 * hp + 32, it * 512 + 128 * m : it * 512 + 128 * m + 128] = tile
    copy2 = pltpu.make_async_copy(s2, t2r, sems.at[1])
    copy2.start()
    copy3.wait()
    copy2.wait()


def forward(
    vol_before,
    vol_own,
    vol_after,
    grad_own,
    t1,
    t2_far,
    t3_far,
    shift,
    pair,
    squeeze,
    spread,
    grow,
    d3p,
    d3t,
    x3,
    sl1,
    sl2,
    x1_own,
    x2_own,
    t2,
    t3,
    x1,
    pp,
    x2,
    q,
    sems,
):
    me, blocks = position()
    copy2 = pltpu.make_async_copy(t2_far, t2, sems.at[0])
    copy2.start()
    copy3 = pltpu.make_async_copy(t3_far, t3, sems.at[1])
    copy3.start()

    at = 0
    for ref, first, count in ((vol_before, 1, 7), (vol_own, 0, 8), (vol_after, 0, 7)):
        rows = ref[64 * first : 64 * (first + count), :]
        moved = dot(rows, shift[...]).astype(BF)
        for p in range(count):
            lanes = slice(128 * (at + p), 128 * (at + p) + 128)
            x1[0:64, lanes] = moved[64 * p : 64 * p + 64, :128]
            x1[64:128, lanes] = rows[64 * p : 64 * p + 64, :]
            x1[128:192, lanes] = moved[64 * p : 64 * p + 64, 128:]
        at += count

    for j in range(10):
        rhs = jnp.concatenate(
            [x1[:, (2 * j + kd) * 128 : (2 * j + kd) * 128 + 256] for kd in range(3)], axis=0
        )
        half = dot(t1[...], rhs)
        t = jnp.tanh(half)
        if 3 <= j < 7:
            slope = (1.0 + t) + half * (1.0 - t * t)
            sl1[:, (j - 3) * 256 : (j - 3) * 256 + 256] = slope.astype(BF)
        act = half + half * t
        act = act[:, :128] + act[:, 128:]
        act = act.reshape(8, 2, 32, 128)
        act = (act[:, 0] + act[:, 1]).reshape(256, 128)
        act = act + pltpu.roll(act, 127, 1)
        scale = jnp.where(inside(4 * me - 3 + j, 4 * blocks), 0.125, 0.0)
        pp[:, j * 128 : j * 128 + 128] = (act * scale).astype(BF)

    for first in range(9):
        got = dot(pp[:, first * 128 : first * 128 + 256], pair[...]).astype(BF)
        for kd in range(3):
            m = (first - kd) // 2
            if (first - kd) % 2 == 0 and 0 <= m < 4:
                for kw in range(3):
                    k = 3 * kd + kw
                    x2[256 * k : 256 * k + 256, m * 128 : m * 128 + 128] = got[
                        :, 128 * kw : 128 * kw + 128
                    ]

    copy2.wait()
    for c in range(2):
        lanes = slice(c * 256, c * 256 + 256)
        half = dot(t2[...], x2[:, lanes])
        t = jnp.tanh(half)
        slope = (1.0 + t) + half * (1.0 - t * t)
        sl2[:, lanes] = slope.astype(BF)
        act = (half + half * t).reshape(4, 2, 64, 256)
        act = (act[:, 0] + act[:, 1]).reshape(256, 256)
        for u in range(2):
            tile = act[:, 128 * u : 128 * u + 128]
            tile = tile + pltpu.roll(tile, 64, 1)
            tile = tile + pltpu.roll(tile, 127, 1)
            m = 2 * c + u
            scale = jnp.where(inside(2 * me - 1 + m, 2 * blocks), 0.125, 0.0)
            q[:, m * 128 : m * 128 + 128] = (tile * scale).astype(BF)
    x1_own[...] = x1[:, 6 * 128 : 16 * 128]
    x2_own[...] = x2[:, 128:384]

    packed = dot(q[...], squeeze[...]).astype(BF)
    got = dot(packed, spread[...]).astype(BF)
    for k in range(9):
        x3[256 * k : 256 * k + 256, :] = got[:, 128 * k : 128 * k + 128]
    copy3.wait()
    half = dot(t3[...], x3[...])
    t = jnp.tanh(half)
    slope = (1.0 + t) + half * (1.0 - t * t)
    grown = []
    for hh in range(2):
        rows = grad_own[16 * hh : 16 * hh + 16, :]
        got = lax.dot_general(rows, grow[...], TN, preferred_element_type=F32)
        grown += [got, got]
    delta = jnp.concatenate(grown, axis=0) * slope
    d3t[...] = delta.T.astype(BF)
    d3p[...] = (delta[:256] + pltpu.roll(delta[256:], 64, 1)).astype(BF)


def grad_three(x3, d3t, out):
    for it in range(9):
        got = dot(x3[256 * it : 256 * it + 256, :], d3t[...])
        for kh, k in enumerate(taps_of(it)):
            total = None
            for h in range(4):
                hp = h + kh - 1
                if 0 <= hp < 4:
                    part = got[64 * hp : 64 * hp + 64, 128 * h : 128 * h + 128]
                    total = part if total is None else total + part
            out[k * 64 : k * 64 + 64, :] = total.astype(BF)


def backward(
    d3_before,
    d3_own,
    d3_after,
    g3,
    sl2,
    t3r_far,
    t2r_far,
    sl1_far,
    x2_far,
    x1_far,
    odd,
    even,
    spread,
    grow2,
    grow1,
    out,
    t3r,
    t2r,
    sl1,
    x2,
    x1,
    d3c,
    d2c,
    d2,
    d1,
    d2t,
    sems,
):
    me, blocks = position()
    copies = []
    for i, (far, near) in enumerate(
        ((t3r_far, t3r), (t2r_far, t2r), (x2_far, x2), (sl1_far, sl1), (x1_far, x1))
    ):
        copies.append(pltpu.make_async_copy(far, near, sems.at[i]))
        copies[-1].start()
    out[:G_TWO, :] = g3[...]

    before, own, after = (ref[...].astype(F32) for ref in (d3_before, d3_own, d3_after))
    low = lax.broadcasted_iota(jnp.int32, (256, 128), 1) < 64
    top = jnp.where(low, before, pltpu.roll(own, 64, 1))
    bottom = jnp.where(low, pltpu.roll(before, 64, 1), own)
    delta = jnp.concatenate(
        [
            jnp.concatenate([top, after], axis=1),
            jnp.concatenate([bottom, pltpu.roll(after, 64, 1)], axis=1),
        ],
        axis=0,
    ).astype(BF)
    got = dot(delta, spread[...]).astype(BF)
    for k in range(9):
        d3c[512 * k : 512 * k + 512, :] = got[:, 128 * k : 128 * k + 128]
    copies[0].wait()
    back = dot(t3r[...], d3c[...])
    lane = lax.broadcasted_iota(jnp.int32, (256, 128), 1)
    back = jnp.where(inside(2 * me - 1 + lane // 32, 2 * blocks), back, 0.0).astype(BF)
    back = dot(back, grow2[...])
    for h in range(8):
        rows = slice(64 * h, 64 * h + 64)
        delta = back[64 * (h // 2) : 64 * (h // 2) + 64, :] * sl2[rows, :].astype(F32)
        d2t[:, rows] = delta[:, 128:384].T.astype(BF)
        d2[rows, :] = delta.astype(BF)

    for start in range(1, 6):
        u = start // 2
        if start % 2:
            got = dot(d2[:, 128 * u : 128 * u + 256], odd[...])
        else:
            got = dot(d2[:, 128 * u : 128 * u + 128], even[...])
        got = got.astype(BF)
        for kd in range(3):
            for m in range(2):
                if 1 + kd + 2 * m == start:
                    for kw in range(3):
                        k = 3 * kd + kw
                        d2c[512 * k : 512 * k + 512, 128 * m : 128 * m + 128] = got[
                            :, 128 * kw : 128 * kw + 128
                        ]
    copies[1].wait()
    back = dot(t2r[...], d2c[...]).astype(BF)

    copies[2].wait()
    lane16 = lax.broadcasted_iota(jnp.int32, (16, 128), 1)
    for it in range(9):
        got = dot(x2[256 * it : 256 * it + 256, :], d2t[...])
        for kh, k in enumerate(taps_of(it)):
            totals = [None, None]
            for h in range(8):
                hp = h + kh - 1
                if 0 <= hp < 8:
                    part = got[32 * hp : 32 * hp + 32, 128 * (h // 2) : 128 * (h // 2) + 128]
                    now = totals[h % 2]
                    totals[h % 2] = part if now is None else now + part
            low = totals[0] + pltpu.roll(totals[1], 64, 1)
            high = pltpu.roll(totals[0], 64, 1) + totals[1]
            out[G_TWO + k * 16 : G_TWO + k * 16 + 16, :] = jnp.where(
                lane16 < 64, low[:16], high[16:]
            ).astype(BF)

    copies[3].wait()
    back = dot(back, grow1[...])
    for h in range(16):
        rows = slice(32 * h, 32 * h + 32)
        source = back[32 * (h // 2) : 32 * (h // 2) + 32, :]
        for e in range(8):
            lanes = slice(128 * e, 128 * e + 128)
            delta = source[:, 128 * (e // 2) : 128 * (e // 2) + 128] * sl1[rows, lanes].astype(F32)
            d1[rows, lanes] = delta.astype(BF)

    copies[4].wait()
    lhs = jnp.concatenate([x1[:, 128 * kd : 128 * kd + 1024] for kd in range(3)], axis=0)
    got = lax.dot_general(lhs, d1[...], NT, preferred_element_type=F32)
    row = lax.broadcasted_iota(jnp.int32, (576, 128), 0) % 16
    col = lax.broadcasted_iota(jnp.int32, (576, 128), 1) // 32
    lane36 = lax.broadcasted_iota(jnp.int32, (36, 128), 1)
    packed = jnp.zeros((36, 128), F32)
    for kh in range(3):
        total = jnp.zeros((576, 128), F32)
        for u in range(4):
            keep = row == col + (4 * u + kh - 1)
            total = total + jnp.where(keep, got[:, 128 * u : 128 * u + 128], 0.0)
        total = total.reshape(36, 16, 128).sum(axis=1)
        total = total + pltpu.roll(total, 64, 1)
        total = total + pltpu.roll(total, 32, 1)
        packed = packed + jnp.where(lane36 // 32 == kh, total, 0.0)
    out[G_ONE : G_ONE + 48, :] = jnp.concatenate(
        [packed, jnp.zeros((12, 128), F32)], axis=0
    ).astype(BF)
    out[G_ONE + 48 :, :] = jnp.zeros((out.shape[0] - G_ONE - 48, 128), BF)


def finish(scales, flat, one, two, three):
    for k in range(27):
        three[k] = flat[64 * k : 64 * k + 64, :].astype(F32) * scales[2]
        got = flat[G_TWO + 16 * k : G_TWO + 16 * k + 16, :].astype(F32) * scales[1]
        two[k, 0:16, :] = got[:, :64]
        two[k, 16:32, :] = got[:, 64:]
    got = flat[G_ONE : G_ONE + 48, :].astype(F32) * scales[0]
    for it in range(9):
        for kh, k in enumerate(taps_of(it)):
            one[k] = got[4 * it : 4 * it + 4, 32 * kh : 32 * kh + 32]


VMEM = pl.BlockSpec(memory_space=pltpu.VMEM)
FAR = pl.BlockSpec(memory_space=pl.ANY)


def call(kernel, name, args, far, outs, far_outs, scratch, flops):
    shapes = [jax.ShapeDtypeStruct(shape, kind) for shape, kind in outs]
    moved = sum(a.size * a.dtype.itemsize for a in list(args) + shapes)
    return pl.pallas_call(
        kernel,
        out_shape=shapes,
        in_specs=[FAR if i in far else VMEM for i in range(len(args))],
        out_specs=[FAR if i in far_outs else VMEM for i in range(len(outs))],
        scratch_shapes=scratch,
        compiler_params=pltpu.CompilerParams(vmem_limit_bytes=58 * 1024 * 1024),
        cost_estimate=pl.CostEstimate(flops=flops, bytes_accessed=moved, transcendentals=0),
        name=name,
    )(*args)


def near(*shape):
    return pltpu.VMEM(shape, BF)


def constants(tables):
    return [jnp.asarray(t, BF) for t in tables]


def run_build_forward(filter_one, filter_two, filter_three):
    return call(
        build_forward,
        "build_forward",
        [filter_one, filter_two, filter_three, *constants(build_tables())],
        (),
        [((512, 576), BF), ((512, 2304), BF), ((512, 2304), BF)],
        (1, 2),
        [near(512, 2304), near(512, 2304), pltpu.SemaphoreType.DMA((2,))],
        10**9,
    )


def run_build_backward(filter_two, filter_three):
    return call(
        build_backward,
        "build_backward",
        [filter_two, filter_three],
        (),
        [((256, 4608), BF), ((256, 4608), BF)],
        (0, 1),
        [near(256, 4608), near(256, 4608), pltpu.SemaphoreType.DMA((2,))],
        10**9,
    )


def run_forward(volumes, grad_own, t1, t2, t3):
    args = [*volumes, grad_own, t1, t2, t3, *constants(forward_tables())]
    return call(
        forward,
        "forward",
        args,
        (5, 6),
        [
            ((256, 128), BF),
            ((128, 512), BF),
            ((2304, 128), BF),
            ((512, 1024), BF),
            ((512, 512), BF),
            ((192, 1280), BF),
            ((2304, 256), BF),
        ],
        (),
        [
            near(512, 2304),
            near(512, 2304),
            near(192, 22 * 128),
            near(256, 10 * 128),
            near(2304, 512),
            near(256, 512),
            pltpu.SemaphoreType.DMA((2,)),
        ],
        7 * 10**9,
    )


def run_grad_three(x3, d3t):
    return call(grad_three, "grad_three", [x3, d3t], (), [((G_TWO, 128), BF)], (), [], 10**9)[0]


def run_backward(deltas, g3, sl2, t3r, t2r, sl1, x2, x1, rows):
    args = [*deltas, g3, sl2, t3r, t2r, sl1, x2, x1, *constants(backward_tables())]
    return call(
        backward,
        "backward",
        args,
        (5, 6, 7, 8, 9),
        [((rows, 128), BF)],
        (),
        [
            near(256, 4608),
            near(256, 4608),
            near(512, 1024),
            near(2304, 256),
            near(192, 1280),
            near(4608, 128),
            near(4608, 256),
            near(512, 512),
            near(512, 1024),
            near(256, 512),
            pltpu.SemaphoreType.DMA((5,)),
        ],
        4 * 10**9,
    )[0]


def run_finish(flat, cells):
    scales = 1.0 / jnp.sqrt(jnp.array([cells, cells / 8.0, cells / 64.0], F32))
    shapes = [(27, 4, 32), (27, 32, 64), (27, 64, 128)]
    outs = pl.pallas_call(
        finish,
        out_shape=[jax.ShapeDtypeStruct(shape, F32) for shape in shapes],
        in_specs=[pl.BlockSpec(memory_space=pltpu.SMEM), VMEM],
        out_specs=[VMEM] * 3,
        name="finish",
    )(scales, flat)
    return tuple(o.reshape(3, 3, 3, *o.shape[1:]) for o in outs)


def exchange(pieces, axis):
    return lax.all_to_all(pieces, axis, 0, 0, tiled=True)


def total_of(got):
    return got.astype(F32).sum(axis=0).astype(BF)


def move(values, step):
    size = lax.axis_size("space")
    pairs = [(i, i + step) for i in range(size) if 0 <= i + step < size]
    return lax.ppermute(values, "space", pairs)


def per_device(volume, grad_out, filter_one, filter_two, filter_three):
    spaces, samples = (lax.axis_size("space"), lax.axis_size("sample"))
    own = volume.reshape(512, 128)
    f1 = filter_one.reshape(108, 32)
    f2 = filter_two.reshape(27, 32, 64)
    f3 = filter_three.reshape(27, 64, 128)

    before = move(own, 1)
    t1, t2, t3 = run_build_forward(f1, f2, f3)
    sent, t1 = lax.optimization_barrier((own, t1))
    after = move(sent, -1)
    d3p, d3t, x3, sl1, sl2, x1, x2 = run_forward(
        (before, own, after), grad_out.reshape(32, 128), t1, t2, t3
    )
    d3_before = move(d3p, 1)
    g3 = run_grad_three(x3, d3t)
    t3r, t2r = run_build_backward(*lax.optimization_barrier((f2, f3, d3t))[:2])
    sent, g3, t2r = lax.optimization_barrier((d3p, g3, t2r))
    d3_after = move(sent, -1)
    flat = run_backward(
        (d3_before, d3p, d3_after), g3, sl2, t3r, t2r, sl1, x2, x1, spaces * SLOT
    )
    part = total_of(exchange(flat.reshape(spaces, SLOT, 128), "space"))
    part = total_of(exchange(jnp.broadcast_to(part[None], (samples, SLOT, 128)), "sample"))
    flat = exchange(jnp.broadcast_to(part[None], (spaces, SLOT, 128)), "space")
    cells = float(samples * spaces * volume.shape[1] * volume.shape[3] * volume.shape[4])
    return run_finish(flat.reshape(-1, 128), cells)


def solution(mesh):
    return jax.shard_map(
        per_device,
        mesh=mesh,
        in_specs=(
            P(("sample", "space"), None, None, None, None),
            P(("sample", "space"), None, None, None, None),
            P(),
            P(),
            P(),
        ),
        out_specs=(P(), P(), P()),
        check_vma=False,
    )
```

```python
import jax
import jax.numpy as jnp
import numpy as np
from jax import lax
from jax.experimental import pallas as pl
from jax.experimental.pallas import tpu as pltpu
from jax.sharding import PartitionSpec as P

BF = jnp.bfloat16
F32 = jnp.float32
SLOT = 80
G_TWO = 1728
G_ONE = 2160
NT = (((1,), (1,)), ((), ()))
TN = (((0,), (0,)), ((), ()))


def table(rows, cols):
    return np.zeros((rows, cols), np.float32)


def one_hot_tables():
    perm = table(108, 640)
    for kd in range(3):
        for kh in range(3):
            for kw in range(3):
                for c in range(4):
                    row = ((kd * 3 + kh) * 3 + kw) * 4 + c
                    perm[row, ((kd * 3 + kw) * 4 + c) * 16 + kh] = 0.5
    shift = table(128, 256)
    for w in range(128):
        if w >= 1:
            shift[w - 1, w] = 1.0
        if w + 1 < 128:
            shift[w + 1, 128 + w] = 1.0
    pair = table(256, 384)
    odd = table(256, 384)
    even = table(128, 384)
    for a in range(2):
        for kw in range(3):
            for w in range(64):
                src = w + kw - 1
                if 0 <= src < 64:
                    pair[128 * a + 2 * src, 128 * kw + 64 * a + w] = 1.0
                    odd[64 + 64 * a + src, 128 * kw + 64 * a + w] = 1.0
                    even[64 * a + src, 128 * kw + 64 * a + w] = 1.0
    squeeze = table(512, 128)
    spread = table(128, 1152)
    grow_g = table(96, 768)
    grow2 = table(128, 512)
    for h in range(4):
        for w in range(32):
            squeeze[128 * h + 2 * w, 32 * h + w] = 1.0
            for kh in range(3):
                for kw in range(3):
                    if 0 <= h + kh - 1 < 4 and 0 <= w + kw - 1 < 32:
                        src = 32 * (h + kh - 1) + w + kw - 1
                        spread[src, 128 * (3 * kh + kw) + 32 * h + w] = 1.0
            for n in range(6):
                src = 32 * (n // 2) + 16 * (h // 2) + w // 2
                grow_g[src, 128 * n + 32 * h + w] = 1.0 / 16
            for d in range(2):
                for u in range(2):
                    grow2[32 * h + w, 128 * h + 64 * d + 2 * w + u] = 1.0 / 16
    grow1 = table(256, 512)
    for e in range(4):
        for w in range(128):
            grow1[64 * e + w // 2, 128 * e + w] = 1.0 / 16
    return [perm, shift, pair, odd, even, squeeze, spread, grow_g, grow2, grow1]


def dot(a, b):
    return jnp.dot(a, b, preferred_element_type=F32)


def inside(index, count):
    return jnp.logical_and(index >= 0, index < count)


def position():
    return lax.axis_index("space"), lax.axis_size("space")


def taps_of(it):
    kd, kw = (it // 3, it % 3)
    return [kd * 9 + kh * 3 + kw for kh in range(3)]


def taps_back(it):
    kd, kw = (2 - it // 3, 2 - it % 3)
    return [kd * 9 + (2 - kh) * 3 + kw for kh in range(3)]


def body(
    vol_own,
    grad_own,
    swap_core,
    swap_chip,
    swap_chip2,
    swap_core2,
    filter_one,
    filter_two,
    filter_three,
    perm,
    shift,
    pair,
    odd,
    even,
    squeeze,
    spread,
    grow_g,
    grow2,
    grow1,
    out,
    t1,
    t2,
    t2r,
    w3t,
    x1,
    pp,
    x2,
    q,
    x3,
    d2c,
    sl1,
    sl2,
    d2,
    d1,
):
    me, blocks = position()
    first_core = me % 2 == 0

    lane = lax.broadcasted_iota(jnp.int32, (32, 640), 1) % 16
    base = lax.dot_general(filter_one[...], perm[...], TN, preferred_element_type=F32)
    for h in range(16):
        moved = pltpu.roll(base, (h - 1) % 640, 1) if h != 1 else base
        if h == 0:
            moved = jnp.where(lane == 15, 0.0, moved)
        if h == 15:
            moved = jnp.where(lane == 0, 0.0, moved)
        t1[32 * h : 32 * h + 32, :] = moved[:, :576].astype(BF)
    for it in range(9):
        w2 = [filter_two[k].astype(F32).T * 0.5 for k in taps_of(it)]
        zero = jnp.zeros((64, 32), F32)
        for s in range(-6, 6):
            if -3 <= s <= 2:
                parts = [w2[s + j] if 0 <= s + j <= 2 else zero for j in range(4)]
                tile = jnp.concatenate(parts, axis=1).astype(BF)
            else:
                tile = jnp.zeros((64, 128), BF)
            for m in range(2):
                h = 4 * m + 1 - s
                if 0 <= h < 8:
                    t2[64 * h : 64 * h + 64, it * 256 + 128 * m : it * 256 + 128 * m + 128] = tile
    for it in range(9):
        v2 = [filter_two[k].astype(F32) for k in taps_back(it)]
        zero = jnp.zeros((32, 64), F32)
        for s in range(-6, 8):
            if -1 <= s <= 2:
                parts = [v2[s + j] if 0 <= s + j <= 2 else zero for j in range(2)]
                tile = jnp.concatenate(parts, axis=1).astype(BF)
            else:
                tile = jnp.zeros((32, 128), BF)
            for m in range(4):
                hp = 2 * m + 1 - s
                if 0 <= hp < 8:
                    t2r[32 * hp : 32 * hp + 32, it * 512 + 128 * m : it * 512 + 128 * m + 128] = tile
    w3t[...] = (filter_three[...].astype(F32).T * 0.5).astype(BF)

    def either(a, b, lo, hi):
        return jnp.where(first_core, a[lo:hi, :], b[lo:hi, :])

    at = 0
    for rows in (
        either(swap_chip2, swap_core2, 64, 512),
        either(swap_chip, swap_core, 0, 512),
        vol_own[...],
        either(swap_core, swap_chip, 0, 512),
        either(swap_core2, swap_chip2, 0, 448),
    ):
        moved = dot(rows, shift[...]).astype(BF)
        count = rows.shape[0] // 64
        for p in range(count):
            lanes = slice(128 * (at + p), 128 * (at + p) + 128)
            x1[0:64, lanes] = moved[64 * p : 64 * p + 64, :128]
            x1[64:128, lanes] = rows[64 * p : 64 * p + 64, :]
            x1[128:192, lanes] = moved[64 * p : 64 * p + 64, 128:]
        at += count

    for j in range(18):
        rhs = jnp.concatenate(
            [x1[:, (2 * j + kd) * 128 : (2 * j + kd) * 128 + 256] for kd in range(3)], axis=0
        )
        half = dot(t1[...], rhs)
        t = jnp.tanh(half)
        if 7 <= j < 11:
            slope = (1.0 + t) + half * (1.0 - t * t)
            sl1[:, (j - 7) * 256 : (j - 7) * 256 + 256] = slope.astype(BF)
        act = half + half * t
        act = act[:, :128] + act[:, 128:]
        act = act.reshape(8, 2, 32, 128)
        act = (act[:, 0] + act[:, 1]).reshape(256, 128)
        act = act + pltpu.roll(act, 127, 1)
        scale = jnp.where(inside(4 * me - 7 + j, 4 * blocks), 0.125, 0.0)
        pp[:, j * 128 : j * 128 + 128] = (act * scale).astype(BF)

    for first in range(17):
        got = dot(pp[:, first * 128 : first * 128 + 256], pair[...]).astype(BF)
        for kd in range(3):
            m = (first - kd) // 2
            if (first - kd) % 2 == 0 and 0 <= m < 8:
                for kw in range(3):
                    k = 3 * kd + kw
                    x2[256 * k : 256 * k + 256, m * 128 : m * 128 + 128] = got[
                        :, 128 * kw : 128 * kw + 128
                    ]

    for c in range(4):
        lanes = slice(c * 256, c * 256 + 256)
        half = dot(t2[...], x2[:, lanes])
        t = jnp.tanh(half)
        if 1 <= c < 3:
            slope = (1.0 + t) + half * (1.0 - t * t)
            sl2[:, c * 256 - 256 : c * 256] = slope.astype(BF)
        act = (half + half * t).reshape(4, 2, 64, 256)
        act = (act[:, 0] + act[:, 1]).reshape(256, 256)
        for u in range(2):
            tile = act[:, 128 * u : 128 * u + 128]
            tile = tile + pltpu.roll(tile, 64, 1)
            tile = tile + pltpu.roll(tile, 127, 1)
            m = 2 * c + u
            scale = jnp.where(inside(2 * me - 3 + m, 2 * blocks), 0.125, 0.0)
            tile = (tile * scale).astype(BF)
            for h in range(4):
                q[64 * m : 64 * m + 64, 128 * h : 128 * h + 128] = tile[64 * h : 64 * h + 64, :]

    packed = dot(q[...], squeeze[...]).astype(BF)
    got = dot(packed, spread[...]).astype(BF)
    for kd in range(3):
        for s in range(9):
            k = 9 * kd + s
            for n in range(6):
                x3[64 * k : 64 * k + 64, 128 * n : 128 * n + 128] = got[
                    64 * (n + kd) : 64 * (n + kd) + 64, 128 * s : 128 * s + 128
                ]
    rows = jnp.concatenate(
        [
            either(swap_chip, swap_core, 512, 544),
            grad_own[...],
            either(swap_core, swap_chip, 512, 544),
        ],
        axis=0,
    )
    grown = dot(rows.astype(F32).T.astype(BF), grow_g[...])
    half = dot(w3t[...], x3[...])
    t = jnp.tanh(half)
    d3 = (grown * ((1.0 + t) + half * (1.0 - t * t))).astype(BF)

    out[:G_TWO, :] = lax.dot_general(
        x3[:, 256:512], d3[:, 256:512], NT, preferred_element_type=F32
    ).astype(BF)

    lane = lax.broadcasted_iota(jnp.int32, (64, 128), 1)
    col, line = (lane % 32, lane // 32)
    masks = []
    for b in range(3):
        for c in range(3):
            keep = inside(col + 1 - c, 32)
            masks.append(jnp.logical_and(keep, inside(line + 1 - b, 4)))
    grown = []
    for n in range(4):
        total = None
        for b in range(3):
            for c in range(3):
                part = None
                for a in range(3):
                    k = 9 * a + 3 * b + c
                    plane = n + 2 - a
                    got = dot(
                        filter_three[64 * k : 64 * k + 64, :], d3[:, 128 * plane : 128 * plane + 128]
                    )
                    part = got if part is None else part + got
                move_by = -(32 * (1 - b) + 1 - c) % 128
                if move_by:
                    part = jnp.where(masks[3 * b + c], pltpu.roll(part, move_by, 1), 0.0)
                total = part if total is None else total + part
        scale = jnp.where(inside(2 * me - 1 + n, 2 * blocks), 1.0, 0.0)
        grown.append((total * scale).astype(BF))
    back = dot(jnp.concatenate(grown, axis=0), grow2[...])
    for h in range(8):
        rows = slice(64 * h, 64 * h + 64)
        for n in range(4):
            lanes = slice(128 * n, 128 * n + 128)
            source = back[64 * n : 64 * n + 64, 128 * (h // 2) : 128 * (h // 2) + 128]
            d2[rows, lanes] = (source * sl2[rows, lanes].astype(F32)).astype(BF)

    for start in range(1, 6):
        u = start // 2
        if start % 2:
            got = dot(d2[:, 128 * u : 128 * u + 256], odd[...])
        else:
            got = dot(d2[:, 128 * u : 128 * u + 128], even[...])
        got = got.astype(BF)
        for kd in range(3):
            for m in range(2):
                if 1 + kd + 2 * m == start:
                    for kw in range(3):
                        k = 3 * kd + kw
                        d2c[512 * k : 512 * k + 512, 128 * m : 128 * m + 128] = got[
                            :, 128 * kw : 128 * kw + 128
                        ]
    back = dot(t2r[...], d2c[...]).astype(BF)
    back = dot(back, grow1[...])
    for h in range(16):
        rows = slice(32 * h, 32 * h + 32)
        source = back[32 * (h // 2) : 32 * (h // 2) + 32, :]
        for e in range(8):
            lanes = slice(128 * e, 128 * e + 128)
            delta = source[:, 128 * (e // 2) : 128 * (e // 2) + 128] * sl1[rows, lanes].astype(F32)
            d1[rows, lanes] = delta.astype(BF)

    lane16 = lax.broadcasted_iota(jnp.int32, (16, 128), 1)
    all_two = lax.dot_general(
        x2[:, 384:640], d2[:, 128:384], NT, preferred_element_type=F32
    )
    for it in range(9):
        got = all_two[256 * it : 256 * it + 256, :]
        for kh, k in enumerate(taps_of(it)):
            totals = [None, None]
            for h in range(8):
                hp = h + kh - 1
                if 0 <= hp < 8:
                    part = got[32 * hp : 32 * hp + 32, 128 * (h // 2) : 128 * (h // 2) + 128]
                    now = totals[h % 2]
                    totals[h % 2] = part if now is None else now + part
            low = totals[0] + pltpu.roll(totals[1], 64, 1)
            high = pltpu.roll(totals[0], 64, 1) + totals[1]
            out[G_TWO + k * 16 : G_TWO + k * 16 + 16, :] = jnp.where(
                lane16 < 64, low[:16], high[16:]
            ).astype(BF)

    lhs = jnp.concatenate([x1[:, 128 * (14 + kd) : 128 * (14 + kd) + 1024] for kd in range(3)], axis=0)
    got = lax.dot_general(lhs, d1[...], NT, preferred_element_type=F32)
    row = lax.broadcasted_iota(jnp.int32, (576, 128), 0) % 16
    col = lax.broadcasted_iota(jnp.int32, (576, 128), 1) // 32
    lane36 = lax.broadcasted_iota(jnp.int32, (36, 128), 1)
    packed = jnp.zeros((36, 128), F32)
    for kh in range(3):
        total = jnp.zeros((576, 128), F32)
        for u in range(4):
            keep = row == col + (4 * u + kh - 1)
            total = total + jnp.where(keep, got[:, 128 * u : 128 * u + 128], 0.0)
        total = total.reshape(36, 16, 128).sum(axis=1)
        total = total + pltpu.roll(total, 64, 1)
        total = total + pltpu.roll(total, 32, 1)
        packed = packed + jnp.where(lane36 // 32 == kh, total, 0.0)
    out[G_ONE : G_ONE + 48, :] = jnp.concatenate(
        [packed, jnp.zeros((12, 128), F32)], axis=0
    ).astype(BF)
    out[G_ONE + 48 :, :] = jnp.zeros((out.shape[0] - G_ONE - 48, 128), BF)


def finish(scales, flat, one, two, three):
    for k in range(27):
        three[k] = flat[64 * k : 64 * k + 64, :].astype(F32) * scales[2]
        got = flat[G_TWO + 16 * k : G_TWO + 16 * k + 16, :].astype(F32) * scales[1]
        two[k, 0:16, :] = got[:, :64]
        two[k, 16:32, :] = got[:, 64:]
    got = flat[G_ONE : G_ONE + 48, :].astype(F32) * scales[0]
    for it in range(9):
        for kh, k in enumerate(taps_of(it)):
            one[k] = got[4 * it : 4 * it + 4, 32 * kh : 32 * kh + 32]


VMEM = pl.BlockSpec(memory_space=pltpu.VMEM)


def near(*shape):
    return pltpu.VMEM(shape, BF)


def local_grads(volume, grad, swaps, filter_one, filter_two, filter_three, rows):
    tables = [jnp.asarray(t, BF) for t in one_hot_tables()]
    args = [volume, grad, *swaps, filter_one, filter_two, filter_three, *tables]
    return pl.pallas_call(
        body,
        out_shape=jax.ShapeDtypeStruct((rows, 128), BF),
        in_specs=[VMEM] * len(args),
        out_specs=VMEM,
        scratch_shapes=[
            near(512, 576),
            near(512, 2304),
            near(256, 4608),
            near(128, 1728),
            near(192, 38 * 128),
            near(256, 18 * 128),
            near(2304, 1024),
            near(512, 512),
            near(1728, 768),
            near(4608, 256),
            near(512, 1024),
            near(512, 512),
            near(512, 512),
            near(512, 1024),
        ],
        compiler_params=pltpu.CompilerParams(vmem_limit_bytes=58 * 1024 * 1024),
        name="local_grads",
    )(*args)


def run_finish(flat, cells):
    scales = 1.0 / jnp.sqrt(jnp.array([cells, cells / 8.0, cells / 64.0], F32))
    shapes = [(27, 4, 32), (27, 32, 64), (27, 64, 128)]
    outs = pl.pallas_call(
        finish,
        out_shape=[jax.ShapeDtypeStruct(shape, F32) for shape in shapes],
        in_specs=[pl.BlockSpec(memory_space=pltpu.SMEM), VMEM],
        out_specs=[VMEM] * 3,
        name="finish",
    )(scales, flat)
    return tuple(o.reshape(3, 3, 3, *o.shape[1:]) for o in outs)


def exchange(pieces, axis):
    return lax.all_to_all(pieces, axis, 0, 0, tiled=True)


def total_of(got):
    return got.astype(F32).sum(axis=0).astype(BF)


def swap(values, first):
    size = lax.axis_size("space")
    pairs = [(i, i + 1) for i in range(first, size - 1, 2)]
    return lax.ppermute(values, "space", pairs + [(j, i) for i, j in pairs])


def per_device(volume, grad_out, filter_one, filter_two, filter_three):
    spaces, samples = (lax.axis_size("space"), lax.axis_size("sample"))
    own = volume.reshape(512, 128)
    grad = grad_out.reshape(32, 128)
    both = jnp.concatenate([own, grad], axis=0)
    swap_core = swap(both, 0)
    swap_chip = swap(both, 1)
    swap_chip2 = swap(swap_core, 1)
    swap_core2 = swap(swap_chip, 0)
    flat = local_grads(
        own,
        grad,
        (swap_core, swap_chip, swap_chip2, swap_core2),
        filter_one.reshape(108, 32),
        filter_two.reshape(27, 32, 64),
        filter_three.reshape(1728, 128),
        spaces * SLOT,
    )
    part = total_of(exchange(flat.reshape(spaces, SLOT, 128), "space"))
    part = total_of(exchange(jnp.broadcast_to(part[None], (samples, SLOT, 128)), "sample"))
    flat = exchange(jnp.broadcast_to(part[None], (spaces, SLOT, 128)), "space")
    cells = float(samples * spaces * volume.shape[1] * volume.shape[3] * volume.shape[4])
    return run_finish(flat.reshape(-1, 128), cells)


def solution(mesh):
    return jax.shard_map(
        per_device,
        mesh=mesh,
        in_specs=(
            P(("sample", "space"), None, None, None, None),
            P(("sample", "space"), None, None, None, None),
            P(),
            P(),
            P(),
        ),
        out_specs=(P(), P(), P()),
        check_vma=False,
    )
```

```python
import jax
import jax.numpy as jnp
import numpy as np
from jax import lax
from jax.experimental import pallas as pl
from jax.experimental.pallas import tpu as pltpu
from jax.sharding import PartitionSpec as P

BF = jnp.bfloat16
F32 = jnp.float32
SLOT = 80
LIMIT = 44
G_TWO = 1728
G_ONE = 2160
NT = (((1,), (1,)), ((), ()))
TN = (((0,), (0,)), ((), ()))


def table(rows, cols):
    return np.zeros((rows, cols), np.float32)


def one_hot_tables():
    perm = table(108, 640)
    for kd in range(3):
        for kh in range(3):
            for kw in range(3):
                for c in range(4):
                    row = ((kd * 3 + kh) * 3 + kw) * 4 + c
                    perm[row, ((kd * 3 + kw) * 4 + c) * 16 + kh] = 0.5
    shift = table(128, 256)
    for w in range(128):
        if w >= 1:
            shift[w - 1, w] = 1.0
        if w + 1 < 128:
            shift[w + 1, 128 + w] = 1.0
    pair = table(256, 384)
    odd = table(256, 384)
    even = table(128, 384)
    for a in range(2):
        for kw in range(3):
            for w in range(64):
                src = w + kw - 1
                if 0 <= src < 64:
                    pair[128 * a + 2 * src, 128 * kw + 64 * a + w] = 1.0
                    odd[64 + 64 * a + src, 128 * kw + 64 * a + w] = 1.0
                    even[64 * a + src, 128 * kw + 64 * a + w] = 1.0
    squeeze = table(512, 128)
    spread = table(128, 1152)
    grow_g = table(96, 768)
    grow2 = table(128, 512)
    for h in range(4):
        for w in range(32):
            squeeze[128 * h + 2 * w, 32 * h + w] = 1.0
            for kh in range(3):
                for kw in range(3):
                    if 0 <= h + kh - 1 < 4 and 0 <= w + kw - 1 < 32:
                        src = 32 * (h + kh - 1) + w + kw - 1
                        spread[src, 128 * (3 * kh + kw) + 32 * h + w] = 1.0
            for n in range(6):
                src = 32 * (n // 2) + 16 * (h // 2) + w // 2
                grow_g[src, 128 * n + 32 * h + w] = 1.0 / 16
            for d in range(2):
                for u in range(2):
                    grow2[32 * h + w, 128 * h + 64 * d + 2 * w + u] = 1.0 / 16
    grow1 = table(256, 512)
    for e in range(4):
        for w in range(128):
            grow1[64 * e + w // 2, 128 * e + w] = 1.0 / 16
    return [perm, shift, pair, odd, even, squeeze, spread, grow_g, grow2, grow1]


def dot(a, b):
    return jnp.dot(a, b, preferred_element_type=F32)


def inside(index, count):
    return jnp.logical_and(index >= 0, index < count)


def position():
    return lax.axis_index("space"), lax.axis_size("space")


def taps_of(it):
    kd, kw = (it // 3, it % 3)
    return [kd * 9 + kh * 3 + kw for kh in range(3)]


def taps_back(it):
    kd, kw = (2 - it // 3, 2 - it % 3)
    return [kd * 9 + (2 - kh) * 3 + kw for kh in range(3)]


def build(filter_one, filter_two, filter_three, perm, t1, t2, w3t, t2r, s1, s2, s3, s2r, sems):
    copies = [
        pltpu.make_async_copy(near_ref, far_ref, sems.at[i])
        for i, (near_ref, far_ref) in enumerate(((s1, t1), (s2, t2), (s3, w3t), (s2r, t2r)))
    ]
    for it in range(9):
        v2 = [filter_two[k].astype(F32) for k in taps_back(it)]
        zero = jnp.zeros((32, 64), F32)
        for s in range(-6, 8):
            if -1 <= s <= 2:
                parts = [v2[s + j] if 0 <= s + j <= 2 else zero for j in range(2)]
                tile = jnp.concatenate(parts, axis=1).astype(BF)
            else:
                tile = jnp.zeros((32, 128), BF)
            for m in range(4):
                hp = 2 * m + 1 - s
                if 0 <= hp < 8:
                    s2r[32 * hp : 32 * hp + 32, it * 512 + 128 * m : it * 512 + 128 * m + 128] = tile
    copies[3].start()
    taps = []
    for kh in range(3):
        rows = jnp.concatenate([filter_two[taps_of(it)[kh]] for it in range(9)], axis=0)
        taps.append(rows.astype(F32).T * 0.5)
    zero = jnp.zeros((64, 288), F32)
    for s in range(5):
        parts = [taps[p - s + 1] if 0 <= p - s + 1 < 3 else zero for p in range(5)]
        s2[64 * s : 64 * s + 64, :] = jnp.concatenate(parts, axis=1).astype(BF)
    copies[1].start()
    s3[...] = (filter_three[...].astype(F32).T * 0.5).astype(BF)
    copies[2].start()
    lane = lax.broadcasted_iota(jnp.int32, (32, 640), 1) % 16
    base = lax.dot_general(filter_one[...], perm[...], TN, preferred_element_type=F32)
    for h in range(16):
        moved = pltpu.roll(base, (h - 1) % 640, 1) if h != 1 else base
        if h == 0:
            moved = jnp.where(lane == 15, 0.0, moved)
        if h == 15:
            moved = jnp.where(lane == 0, 0.0, moved)
        s1[32 * h : 32 * h + 32, :] = moved[:, :576].astype(BF)
    copies[0].start()
    for copy in copies:
        copy.wait()


def body(
    vol_own,
    grad_own,
    swap_core,
    swap_chip,
    swap_chip2,
    swap_core2,
    filter_three,
    t1_far,
    t2_far,
    w3t_far,
    t2r_far,
    shift,
    pair,
    odd,
    even,
    squeeze,
    spread,
    grow_g,
    grow2,
    grow1,
    out,
    t1,
    t2,
    w3t,
    t2r,
    x1,
    pp,
    x2,
    q,
    x3,
    d2c,
    sl1,
    sl2,
    d2,
    d1,
    sems,
):
    me, blocks = position()
    first_core = me % 2 == 0
    copies = []
    for i, (far_ref, near_ref) in enumerate(
        ((t1_far, t1), (t2_far, t2), (w3t_far, w3t), (t2r_far, t2r))
    ):
        copies.append(pltpu.make_async_copy(far_ref, near_ref, sems.at[i]))
        copies[-1].start()

    def either(a, b, lo, hi):
        return jnp.where(first_core, a[lo:hi, :], b[lo:hi, :])

    at = 0
    for rows in (
        either(swap_chip2, swap_core2, 0, 448),
        either(swap_chip, swap_core, 0, 512),
        vol_own[...],
        either(swap_core, swap_chip, 0, 512),
        either(swap_core2, swap_chip2, 0, 448),
    ):
        moved = dot(rows, shift[...]).astype(BF)
        count = rows.shape[0] // 64
        for p in range(count):
            lanes = slice(128 * (at + p), 128 * (at + p) + 128)
            x1[0:64, lanes] = moved[64 * p : 64 * p + 64, :128]
            x1[64:128, lanes] = rows[64 * p : 64 * p + 64, :]
            x1[128:192, lanes] = moved[64 * p : 64 * p + 64, 128:]
        at += count

    copies[0].wait()
    for j in range(18):
        rhs = jnp.concatenate(
            [x1[:, (2 * j + kd) * 128 : (2 * j + kd) * 128 + 256] for kd in range(3)], axis=0
        )
        half = dot(t1[...], rhs)
        t = jnp.tanh(half)
        if 7 <= j < 11:
            slope = (1.0 + t) + half * (1.0 - t * t)
            sl1[:, (j - 7) * 256 : (j - 7) * 256 + 256] = slope.astype(BF)
        act = half + half * t
        act = act[:, :128] + act[:, 128:]
        act = act.reshape(8, 2, 32, 128)
        act = (act[:, 0] + act[:, 1]).reshape(256, 128)
        act = act + pltpu.roll(act, 127, 1)
        scale = jnp.where(inside(4 * me - 7 + j, 4 * blocks), 0.125, 0.0)
        pp[:, j * 128 : j * 128 + 128] = (act * scale).astype(BF)

    for first in range(17):
        got = dot(pp[:, first * 128 : first * 128 + 256], pair[...]).astype(BF)
        for kd in range(3):
            m = (first - kd) // 2
            if (first - kd) % 2 == 0 and 0 <= m < 8:
                for kw in range(3):
                    k = 3 * kd + kw
                    x2[256 * k : 256 * k + 256, m * 128 : m * 128 + 128] = got[
                        :, 128 * kw : 128 * kw + 128
                    ]

    copies[1].wait()
    for c in range(4):
        lanes = slice(c * 256, c * 256 + 256)
        for g in range(2):
            rhs = jnp.concatenate(
                [
                    x2[256 * it + 32 * p : 256 * it + 32 * p + 32, lanes]
                    for p in range(3 * g, 3 * g + 5)
                    for it in range(9)
                ],
                axis=0,
            )
            half = dot(t2[64 * g : 64 * g + 256, :], rhs)
            t = jnp.tanh(half)
            if 1 <= c < 3:
                slope = (1.0 + t) + half * (1.0 - t * t)
                sl2[256 * g : 256 * g + 256, c * 256 - 256 : c * 256] = slope.astype(BF)
            act = (half + half * t).reshape(2, 2, 64, 256)
            act = (act[:, 0] + act[:, 1]).reshape(128, 256)
            for u in range(2):
                tile = act[:, 128 * u : 128 * u + 128]
                tile = tile + pltpu.roll(tile, 64, 1)
                tile = tile + pltpu.roll(tile, 127, 1)
                m = 2 * c + u
                scale = jnp.where(inside(2 * me - 3 + m, 2 * blocks), 0.125, 0.0)
                tile = (tile * scale).astype(BF)
                for h in range(2):
                    lo = 128 * (2 * g + h)
                    q[64 * m : 64 * m + 64, lo : lo + 128] = tile[64 * h : 64 * h + 64, :]

    packed = dot(q[...], squeeze[...]).astype(BF)
    got = dot(packed, spread[...]).astype(BF)
    for kd in range(3):
        for s in range(9):
            k = 9 * kd + s
            for n in range(6):
                x3[64 * k : 64 * k + 64, 128 * n : 128 * n + 128] = got[
                    64 * (n + kd) : 64 * (n + kd) + 64, 128 * s : 128 * s + 128
                ]
    rows = jnp.concatenate(
        [
            either(swap_chip2, swap_core2, 448, 480),
            grad_own[...],
            either(swap_core2, swap_chip2, 448, 480),
        ],
        axis=0,
    )
    grown = dot(rows.astype(F32).T.astype(BF), grow_g[...])
    copies[2].wait()
    half = dot(w3t[...], x3[...])
    t = jnp.tanh(half)
    d3 = (grown * ((1.0 + t) + half * (1.0 - t * t))).astype(BF)

    out[:G_TWO, :] = lax.dot_general(
        x3[:, 256:512], d3[:, 256:512], NT, preferred_element_type=F32
    ).astype(BF)

    lane = lax.broadcasted_iota(jnp.int32, (64, 128), 1)
    col, line = (lane % 32, lane // 32)
    masks = []
    for b in range(3):
        for c in range(3):
            keep = inside(col + 1 - c, 32)
            masks.append(jnp.logical_and(keep, inside(line + 1 - b, 4)))
    lhs = jnp.concatenate([filter_three[576 * a : 576 * a + 576, :] for a in range(3)], axis=1)
    grown = []
    for pair_at in range(2):
        rhs = jnp.concatenate(
            [
                d3[:, 128 * (2 * pair_at + 2 - a) : 128 * (2 * pair_at + 2 - a) + 256]
                for a in range(3)
            ],
            axis=0,
        )
        got = dot(lhs, rhs)
        for u in range(2):
            total = None
            for b in range(3):
                for c in range(3):
                    s = 3 * b + c
                    part = got[64 * s : 64 * s + 64, 128 * u : 128 * u + 128]
                    move_by = -(32 * (1 - b) + 1 - c) % 128
                    if move_by:
                        part = jnp.where(masks[s], pltpu.roll(part, move_by, 1), 0.0)
                    total = part if total is None else total + part
            n = 2 * pair_at + u
            scale = jnp.where(inside(2 * me - 1 + n, 2 * blocks), 1.0, 0.0)
            grown.append((total * scale).astype(BF))
    back = dot(jnp.concatenate(grown, axis=0), grow2[...])
    for h in range(8):
        rows = slice(64 * h, 64 * h + 64)
        for n in range(4):
            lanes = slice(128 * n, 128 * n + 128)
            source = back[64 * n : 64 * n + 64, 128 * (h // 2) : 128 * (h // 2) + 128]
            d2[rows, lanes] = (source * sl2[rows, lanes].astype(F32)).astype(BF)

    for start in range(1, 6):
        u = start // 2
        if start % 2:
            got = dot(d2[:, 128 * u : 128 * u + 256], odd[...])
        else:
            got = dot(d2[:, 128 * u : 128 * u + 128], even[...])
        got = got.astype(BF)
        for kd in range(3):
            for m in range(2):
                if 1 + kd + 2 * m == start:
                    for kw in range(3):
                        k = 3 * kd + kw
                        d2c[512 * k : 512 * k + 512, 128 * m : 128 * m + 128] = got[
                            :, 128 * kw : 128 * kw + 128
                        ]
    copies[3].wait()
    back = dot(t2r[...], d2c[...]).astype(BF)
    back = dot(back, grow1[...])
    for h in range(16):
        rows = slice(32 * h, 32 * h + 32)
        source = back[32 * (h // 2) : 32 * (h // 2) + 32, :]
        for e in range(8):
            lanes = slice(128 * e, 128 * e + 128)
            delta = source[:, 128 * (e // 2) : 128 * (e // 2) + 128] * sl1[rows, lanes].astype(F32)
            d1[rows, lanes] = delta.astype(BF)

    lane16 = lax.broadcasted_iota(jnp.int32, (16, 128), 1)
    all_two = lax.dot_general(
        x2[:, 384:640], d2[:, 128:384], NT, preferred_element_type=F32
    )
    for it in range(9):
        got = all_two[256 * it : 256 * it + 256, :]
        for kh, k in enumerate(taps_of(it)):
            totals = [None, None]
            for h in range(8):
                hp = h + kh - 1
                if 0 <= hp < 8:
                    part = got[32 * hp : 32 * hp + 32, 128 * (h // 2) : 128 * (h // 2) + 128]
                    now = totals[h % 2]
                    totals[h % 2] = part if now is None else now + part
            low = totals[0] + pltpu.roll(totals[1], 64, 1)
            high = pltpu.roll(totals[0], 64, 1) + totals[1]
            out[G_TWO + k * 16 : G_TWO + k * 16 + 16, :] = jnp.where(
                lane16 < 64, low[:16], high[16:]
            ).astype(BF)

    lhs = jnp.concatenate([x1[:, 128 * (14 + kd) : 128 * (14 + kd) + 1024] for kd in range(3)], axis=0)
    got = lax.dot_general(lhs, d1[...], NT, preferred_element_type=F32)
    row = lax.broadcasted_iota(jnp.int32, (576, 128), 0) % 16
    col = lax.broadcasted_iota(jnp.int32, (576, 128), 1) // 32
    lane36 = lax.broadcasted_iota(jnp.int32, (36, 128), 1)
    packed = jnp.zeros((36, 128), F32)
    for kh in range(3):
        total = jnp.zeros((576, 128), F32)
        for u in range(4):
            keep = row == col + (4 * u + kh - 1)
            total = total + jnp.where(keep, got[:, 128 * u : 128 * u + 128], 0.0)
        total = total.reshape(36, 16, 128).sum(axis=1)
        total = total + pltpu.roll(total, 64, 1)
        total = total + pltpu.roll(total, 32, 1)
        packed = packed + jnp.where(lane36 // 32 == kh, total, 0.0)
    out[G_ONE : G_ONE + 48, :] = jnp.concatenate(
        [packed, jnp.zeros((12, 128), F32)], axis=0
    ).astype(BF)
    out[G_ONE + 48 :, :] = jnp.zeros((out.shape[0] - G_ONE - 48, 128), BF)


def finish(scales, flat, one, two, three):
    for k in range(27):
        three[k] = flat[64 * k : 64 * k + 64, :].astype(F32) * scales[2]
        got = flat[G_TWO + 16 * k : G_TWO + 16 * k + 16, :].astype(F32) * scales[1]
        two[k, 0:16, :] = got[:, :64]
        two[k, 16:32, :] = got[:, 64:]
    got = flat[G_ONE : G_ONE + 48, :].astype(F32) * scales[0]
    for it in range(9):
        for kh, k in enumerate(taps_of(it)):
            one[k] = got[4 * it : 4 * it + 4, 32 * kh : 32 * kh + 32]


VMEM = pl.BlockSpec(memory_space=pltpu.VMEM)


def near(*shape):
    return pltpu.VMEM(shape, BF)


FAR = pl.BlockSpec(memory_space=pl.ANY)
BANDED = ((512, 576), (320, 1440), (128, 1728), (256, 4608))


def run_build(filter_one, filter_two, filter_three):
    args = [filter_one, filter_two, filter_three, jnp.asarray(one_hot_tables()[0], BF)]
    return pl.pallas_call(
        build,
        out_shape=[jax.ShapeDtypeStruct(shape, BF) for shape in BANDED],
        in_specs=[VMEM] * len(args),
        out_specs=[FAR] * 4,
        scratch_shapes=[near(*shape) for shape in BANDED] + [pltpu.SemaphoreType.DMA((4,))],
        compiler_params=pltpu.CompilerParams(vmem_limit_bytes=24 * 1024 * 1024),
        cost_estimate=pl.CostEstimate(flops=10**9, bytes_accessed=6 * 10**6, transcendentals=0),
        name="build",
    )(*args)


def local_grads(volume, grad, swaps, filter_three, banded, rows):
    tables = [jnp.asarray(t, BF) for t in one_hot_tables()[1:]]
    args = [volume, grad, *swaps, filter_three, *banded, *tables]
    far = range(7, 11)
    return pl.pallas_call(
        body,
        out_shape=jax.ShapeDtypeStruct((rows, 128), BF),
        in_specs=[FAR if i in far else VMEM for i in range(len(args))],
        out_specs=VMEM,
        scratch_shapes=[near(*shape) for shape in BANDED]
        + [
            near(192, 38 * 128),
            near(256, 18 * 128),
            near(2304, 1024),
            near(512, 512),
            near(1728, 768),
            near(4608, 256),
            near(512, 1024),
            near(512, 512),
            near(512, 512),
            near(512, 1024),
            pltpu.SemaphoreType.DMA((4,)),
        ],
        compiler_params=pltpu.CompilerParams(vmem_limit_bytes=LIMIT * 1024 * 1024),
        cost_estimate=pl.CostEstimate(flops=10**10, bytes_accessed=10**7, transcendentals=0),
        name="local_grads",
    )(*args)


def run_finish(flat, cells):
    scales = 1.0 / jnp.sqrt(jnp.array([cells, cells / 8.0, cells / 64.0], F32))
    shapes = [(27, 4, 32), (27, 32, 64), (27, 64, 128)]
    outs = pl.pallas_call(
        finish,
        out_shape=[jax.ShapeDtypeStruct(shape, F32) for shape in shapes],
        in_specs=[pl.BlockSpec(memory_space=pltpu.SMEM), VMEM],
        out_specs=[VMEM] * 3,
        name="finish",
    )(scales, flat)
    return tuple(o.reshape(3, 3, 3, *o.shape[1:]) for o in outs)


def exchange(pieces, axis):
    return lax.all_to_all(pieces, axis, 0, 0, tiled=True)


def total_of(got):
    return got.astype(F32).sum(axis=0).astype(BF)


def swap(values, first):
    size = lax.axis_size("space")
    pairs = [(i, i + 1) for i in range(first, size - 1, 2)]
    return lax.ppermute(values, "space", pairs + [(j, i) for i, j in pairs])


def per_device(volume, grad_out, filter_one, filter_two, filter_three):
    spaces, samples = (lax.axis_size("space"), lax.axis_size("sample"))
    own = volume.reshape(512, 128)
    grad = grad_out.reshape(32, 128)
    f1 = filter_one.reshape(108, 32)
    f2 = filter_two.reshape(27, 32, 64)
    f3 = filter_three.reshape(1728, 128)
    core = lax.axis_index("space") % 2

    def second(block, flip=0):
        planes = lax.dynamic_slice(block, (64 * (core ^ flip), 0), (448, 128))
        return jnp.concatenate([planes, grad], axis=0)

    swap_core = swap(own, 0)
    swap_chip = swap(own, 1)
    relay = second(swap_core)
    swap_chip2 = swap(relay, 1)
    f2_later = lax.optimization_barrier((f2, relay))[0]
    banded = run_build(f1, f2_later, f3)
    swap_chip, *banded = lax.optimization_barrier((swap_chip, *banded))
    swap_core2 = swap(second(swap_chip, 1), 0)
    flat = local_grads(
        own,
        grad,
        (swap_core, swap_chip, swap_chip2, swap_core2),
        f3,
        banded,
        spaces * SLOT,
    )
    part = total_of(exchange(flat.reshape(spaces, SLOT, 128), "space"))
    part = total_of(exchange(jnp.broadcast_to(part[None], (samples, SLOT, 128)), "sample"))
    flat = exchange(jnp.broadcast_to(part[None], (spaces, SLOT, 128)), "space")
    cells = float(samples * spaces * volume.shape[1] * volume.shape[3] * volume.shape[4])
    return run_finish(flat.reshape(-1, 128), cells)


def solution(mesh):
    return jax.shard_map(
        per_device,
        mesh=mesh,
        in_specs=(
            P(("sample", "space"), None, None, None, None),
            P(("sample", "space"), None, None, None, None),
            P(),
            P(),
            P(),
        ),
        out_specs=(P(), P(), P()),
        check_vma=False,
    )
```

```python
import jax
import jax.numpy as jnp
import numpy as np
from jax import lax
from jax.experimental import pallas as pl
from jax.experimental.pallas import tpu as pltpu
from jax.sharding import PartitionSpec as P

BF = jnp.bfloat16
F32 = jnp.float32
SLOT = 80
LIMIT = 44
G_TWO = 1728
G_ONE = 2160
NT = (((1,), (1,)), ((), ()))
TN = (((0,), (0,)), ((), ()))


def table(rows, cols):
    return np.zeros((rows, cols), np.float32)


def one_hot_tables():
    perm = table(108, 640)
    for kd in range(3):
        for kh in range(3):
            for kw in range(3):
                for c in range(4):
                    row = ((kd * 3 + kh) * 3 + kw) * 4 + c
                    perm[row, ((kd * 3 + kw) * 4 + c) * 16 + kh] = 0.5
    shift = table(128, 256)
    for w in range(128):
        if w >= 1:
            shift[w - 1, w] = 1.0
        if w + 1 < 128:
            shift[w + 1, 128 + w] = 1.0
    pair = table(256, 384)
    odd = table(256, 384)
    even = table(128, 384)
    for a in range(2):
        for kw in range(3):
            for w in range(64):
                src = w + kw - 1
                if 0 <= src < 64:
                    pair[128 * a + 2 * src, 128 * kw + 64 * a + w] = 1.0
                    odd[64 + 64 * a + src, 128 * kw + 64 * a + w] = 1.0
                    even[64 * a + src, 128 * kw + 64 * a + w] = 1.0
    squeeze = table(512, 128)
    spread = table(128, 1152)
    grow_g = table(96, 768)
    grow2 = table(128, 512)
    for h in range(4):
        for w in range(32):
            squeeze[128 * h + 2 * w, 32 * h + w] = 1.0
            for kh in range(3):
                for kw in range(3):
                    if 0 <= h + kh - 1 < 4 and 0 <= w + kw - 1 < 32:
                        src = 32 * (h + kh - 1) + w + kw - 1
                        spread[src, 128 * (3 * kh + kw) + 32 * h + w] = 1.0
            for n in range(6):
                src = 32 * (n // 2) + 16 * (h // 2) + w // 2
                grow_g[src, 128 * n + 32 * h + w] = 1.0 / 16
            for d in range(2):
                for u in range(2):
                    grow2[32 * h + w, 128 * h + 64 * d + 2 * w + u] = 1.0 / 16
    grow1 = table(256, 512)
    for e in range(4):
        for w in range(128):
            grow1[64 * e + w // 2, 128 * e + w] = 1.0 / 16
    return [perm, shift, pair, odd, even, squeeze, spread, grow_g, grow2, grow1]


def dot(a, b):
    return jnp.dot(a, b, preferred_element_type=F32)


def inside(index, count):
    return jnp.logical_and(index >= 0, index < count)


def position():
    return lax.axis_index("space"), lax.axis_size("space")


def taps_of(it):
    kd, kw = (it // 3, it % 3)
    return [kd * 9 + kh * 3 + kw for kh in range(3)]


def taps_back(it):
    kd, kw = (2 - it // 3, 2 - it % 3)
    return [kd * 9 + (2 - kh) * 3 + kw for kh in range(3)]


def build(filter_two, t2, t2r, s2, s2r, sems):
    copy2r = pltpu.make_async_copy(s2r, t2r, sems.at[0])
    copy2 = pltpu.make_async_copy(s2, t2, sems.at[1])
    for it in range(9):
        v2 = [filter_two[k].astype(F32) for k in taps_back(it)]
        zero = jnp.zeros((32, 64), F32)
        for s in range(-6, 8):
            if -1 <= s <= 2:
                parts = [v2[s + j] if 0 <= s + j <= 2 else zero for j in range(2)]
                tile = jnp.concatenate(parts, axis=1).astype(BF)
            else:
                tile = jnp.zeros((32, 128), BF)
            for m in range(4):
                hp = 2 * m + 1 - s
                if 0 <= hp < 8:
                    s2r[32 * hp : 32 * hp + 32, it * 512 + 128 * m : it * 512 + 128 * m + 128] = tile
    copy2r.start()
    taps = []
    for kh in range(3):
        rows = jnp.concatenate([filter_two[taps_of(it)[kh]] for it in range(9)], axis=0)
        taps.append(rows.astype(F32).T * 0.5)
    zero = jnp.zeros((64, 288), F32)
    for s in range(5):
        parts = [taps[p - s + 1] if 0 <= p - s + 1 < 3 else zero for p in range(5)]
        s2[64 * s : 64 * s + 64, :] = jnp.concatenate(parts, axis=1).astype(BF)
    copy2.start()
    copy2r.wait()
    copy2.wait()


def body(
    vol_own,
    grad_own,
    swap_core,
    swap_chip,
    swap_chip2,
    swap_core2,
    filter_one,
    filter_three,
    t2_far,
    t2r_far,
    perm,
    shift,
    pair,
    odd,
    even,
    squeeze,
    spread,
    grow_g,
    grow2,
    grow1,
    kept,
    sent,
    t1,
    t2,
    w3t,
    t2r,
    x1,
    pp,
    x2,
    q,
    x3,
    d2c,
    sl1,
    sl2,
    d2,
    d1,
    out,
    sems,
):
    me, blocks = position()
    first_core = me % 2 == 0
    copies = [
        pltpu.make_async_copy(far_ref, near_ref, sems.at[i])
        for i, (far_ref, near_ref) in enumerate(((t2_far, t2), (t2r_far, t2r)))
    ]
    for copy in copies:
        copy.start()

    lane = lax.broadcasted_iota(jnp.int32, (32, 640), 1) % 16
    rows = filter_one[...].astype(F32).reshape(108, 32).astype(BF)
    base = lax.dot_general(rows, perm[...], TN, preferred_element_type=F32)
    for h in range(16):
        moved = pltpu.roll(base, (h - 1) % 640, 1) if h != 1 else base
        if h == 0:
            moved = jnp.where(lane == 15, 0.0, moved)
        if h == 15:
            moved = jnp.where(lane == 0, 0.0, moved)
        t1[32 * h : 32 * h + 32, :] = moved[:, :576].astype(BF)
    w3t[...] = (filter_three[...].astype(F32).T * 0.5).astype(BF)

    def either(a, b, lo, hi):
        return jnp.where(first_core, a[lo:hi, :], b[lo:hi, :])

    at = 0
    for rows in (
        either(swap_chip2, swap_core2, 0, 448),
        either(swap_chip, swap_core, 0, 512),
        vol_own[...],
        either(swap_core, swap_chip, 0, 512),
        either(swap_core2, swap_chip2, 0, 448),
    ):
        moved = dot(rows, shift[...]).astype(BF)
        count = rows.shape[0] // 64
        for p in range(count):
            lanes = slice(128 * (at + p), 128 * (at + p) + 128)
            x1[0:64, lanes] = moved[64 * p : 64 * p + 64, :128]
            x1[64:128, lanes] = rows[64 * p : 64 * p + 64, :]
            x1[128:192, lanes] = moved[64 * p : 64 * p + 64, 128:]
        at += count

    for j in range(18):
        rhs = jnp.concatenate(
            [x1[:, (2 * j + kd) * 128 : (2 * j + kd) * 128 + 256] for kd in range(3)], axis=0
        )
        half = dot(t1[...], rhs)
        t = jnp.tanh(half)
        if 7 <= j < 11:
            slope = (1.0 + t) + half * (1.0 - t * t)
            sl1[:, (j - 7) * 256 : (j - 7) * 256 + 256] = slope.astype(BF)
        act = half + half * t
        act = act[:, :128] + act[:, 128:]
        act = act.reshape(8, 2, 32, 128)
        act = (act[:, 0] + act[:, 1]).reshape(256, 128)
        act = act + pltpu.roll(act, 127, 1)
        scale = jnp.where(inside(4 * me - 7 + j, 4 * blocks), 0.125, 0.0)
        pp[:, j * 128 : j * 128 + 128] = (act * scale).astype(BF)

    for first in range(17):
        got = dot(pp[:, first * 128 : first * 128 + 256], pair[...]).astype(BF)
        for kd in range(3):
            m = (first - kd) // 2
            if (first - kd) % 2 == 0 and 0 <= m < 8:
                for kw in range(3):
                    k = 3 * kd + kw
                    x2[256 * k : 256 * k + 256, m * 128 : m * 128 + 128] = got[
                        :, 128 * kw : 128 * kw + 128
                    ]

    copies[0].wait()
    for c in range(4):
        lanes = slice(c * 256, c * 256 + 256)
        for g in range(2):
            rhs = jnp.concatenate(
                [
                    x2[256 * it + 32 * p : 256 * it + 32 * p + 32, lanes]
                    for p in range(3 * g, 3 * g + 5)
                    for it in range(9)
                ],
                axis=0,
            )
            half = dot(t2[64 * g : 64 * g + 256, :], rhs)
            t = jnp.tanh(half)
            if 1 <= c < 3:
                slope = (1.0 + t) + half * (1.0 - t * t)
                sl2[256 * g : 256 * g + 256, c * 256 - 256 : c * 256] = slope.astype(BF)
            act = (half + half * t).reshape(2, 2, 64, 256)
            act = (act[:, 0] + act[:, 1]).reshape(128, 256)
            for u in range(2):
                tile = act[:, 128 * u : 128 * u + 128]
                tile = tile + pltpu.roll(tile, 64, 1)
                tile = tile + pltpu.roll(tile, 127, 1)
                m = 2 * c + u
                scale = jnp.where(inside(2 * me - 3 + m, 2 * blocks), 0.125, 0.0)
                tile = (tile * scale).astype(BF)
                for h in range(2):
                    lo = 128 * (2 * g + h)
                    q[64 * m : 64 * m + 64, lo : lo + 128] = tile[64 * h : 64 * h + 64, :]

    packed = dot(q[...], squeeze[...]).astype(BF)
    got = dot(packed, spread[...]).astype(BF)
    for kd in range(3):
        for s in range(9):
            k = 9 * kd + s
            for n in range(6):
                x3[64 * k : 64 * k + 64, 128 * n : 128 * n + 128] = got[
                    64 * (n + kd) : 64 * (n + kd) + 64, 128 * s : 128 * s + 128
                ]
    rows = jnp.concatenate(
        [
            either(swap_chip2, swap_core2, 448, 480),
            grad_own[...],
            either(swap_core2, swap_chip2, 448, 480),
        ],
        axis=0,
    )
    grown = dot(rows.astype(F32).T.astype(BF), grow_g[...])
    half = dot(w3t[...], x3[...])
    t = jnp.tanh(half)
    d3 = (grown * ((1.0 + t) + half * (1.0 - t * t))).astype(BF)

    out[:G_TWO, :] = lax.dot_general(
        x3[:, 256:512], d3[:, 256:512], NT, preferred_element_type=F32
    ).astype(BF)

    lane = lax.broadcasted_iota(jnp.int32, (64, 128), 1)
    col, line = (lane % 32, lane // 32)
    masks = []
    for b in range(3):
        for c in range(3):
            keep = inside(col + 1 - c, 32)
            masks.append(jnp.logical_and(keep, inside(line + 1 - b, 4)))
    lhs = jnp.concatenate([filter_three[576 * a : 576 * a + 576, :] for a in range(3)], axis=1)
    grown = []
    for pair_at in range(2):
        rhs = jnp.concatenate(
            [
                d3[:, 128 * (2 * pair_at + 2 - a) : 128 * (2 * pair_at + 2 - a) + 256]
                for a in range(3)
            ],
            axis=0,
        )
        got = dot(lhs, rhs)
        for u in range(2):
            total = None
            for b in range(3):
                for c in range(3):
                    s = 3 * b + c
                    part = got[64 * s : 64 * s + 64, 128 * u : 128 * u + 128]
                    move_by = -(32 * (1 - b) + 1 - c) % 128
                    if move_by:
                        part = jnp.where(masks[s], pltpu.roll(part, move_by, 1), 0.0)
                    total = part if total is None else total + part
            n = 2 * pair_at + u
            scale = jnp.where(inside(2 * me - 1 + n, 2 * blocks), 1.0, 0.0)
            grown.append((total * scale).astype(BF))
    back = dot(jnp.concatenate(grown, axis=0), grow2[...])
    for h in range(8):
        rows = slice(64 * h, 64 * h + 64)
        for n in range(4):
            lanes = slice(128 * n, 128 * n + 128)
            source = back[64 * n : 64 * n + 64, 128 * (h // 2) : 128 * (h // 2) + 128]
            d2[rows, lanes] = (source * sl2[rows, lanes].astype(F32)).astype(BF)

    for start in range(1, 6):
        u = start // 2
        if start % 2:
            got = dot(d2[:, 128 * u : 128 * u + 256], odd[...])
        else:
            got = dot(d2[:, 128 * u : 128 * u + 128], even[...])
        got = got.astype(BF)
        for kd in range(3):
            for m in range(2):
                if 1 + kd + 2 * m == start:
                    for kw in range(3):
                        k = 3 * kd + kw
                        d2c[512 * k : 512 * k + 512, 128 * m : 128 * m + 128] = got[
                            :, 128 * kw : 128 * kw + 128
                        ]
    copies[1].wait()
    back = dot(t2r[...], d2c[...]).astype(BF)
    back = dot(back, grow1[...])
    for h in range(16):
        rows = slice(32 * h, 32 * h + 32)
        source = back[32 * (h // 2) : 32 * (h // 2) + 32, :]
        for e in range(8):
            lanes = slice(128 * e, 128 * e + 128)
            delta = source[:, 128 * (e // 2) : 128 * (e // 2) + 128] * sl1[rows, lanes].astype(F32)
            d1[rows, lanes] = delta.astype(BF)

    lane16 = lax.broadcasted_iota(jnp.int32, (16, 128), 1)
    all_two = lax.dot_general(
        x2[:, 384:640], d2[:, 128:384], NT, preferred_element_type=F32
    )
    for it in range(9):
        got = all_two[256 * it : 256 * it + 256, :]
        for kh, k in enumerate(taps_of(it)):
            totals = [None, None]
            for h in range(8):
                hp = h + kh - 1
                if 0 <= hp < 8:
                    part = got[32 * hp : 32 * hp + 32, 128 * (h // 2) : 128 * (h // 2) + 128]
                    now = totals[h % 2]
                    totals[h % 2] = part if now is None else now + part
            low = totals[0] + pltpu.roll(totals[1], 64, 1)
            high = pltpu.roll(totals[0], 64, 1) + totals[1]
            out[G_TWO + k * 16 : G_TWO + k * 16 + 16, :] = jnp.where(
                lane16 < 64, low[:16], high[16:]
            ).astype(BF)

    lhs = jnp.concatenate([x1[:, 128 * (14 + kd) : 128 * (14 + kd) + 1024] for kd in range(3)], axis=0)
    got = lax.dot_general(lhs, d1[...], NT, preferred_element_type=F32)
    row = lax.broadcasted_iota(jnp.int32, (576, 128), 0) % 16
    col = lax.broadcasted_iota(jnp.int32, (576, 128), 1) // 32
    lane36 = lax.broadcasted_iota(jnp.int32, (36, 128), 1)
    packed = jnp.zeros((36, 128), F32)
    for kh in range(3):
        total = jnp.zeros((576, 128), F32)
        for u in range(4):
            keep = row == col + (4 * u + kh - 1)
            total = total + jnp.where(keep, got[:, 128 * u : 128 * u + 128], 0.0)
        total = total.reshape(36, 16, 128).sum(axis=1)
        total = total + pltpu.roll(total, 64, 1)
        total = total + pltpu.roll(total, 32, 1)
        packed = packed + jnp.where(lane36 // 32 == kh, total, 0.0)
    out[G_ONE : G_ONE + 48, :] = jnp.concatenate(
        [packed, jnp.zeros((12, 128), F32)], axis=0
    ).astype(BF)
    out[G_ONE + 48 :, :] = jnp.zeros((out.shape[0] - G_ONE - 48, 128), BF)
    half_rows = kept.shape[0]
    mine = pl.multiple_of(me % 2 * half_rows, half_rows)
    kept[...] = out[pl.ds(mine, half_rows), :]
    sent[...] = out[pl.ds(half_rows - mine, half_rows), :]


def finish(scales, mine, other, one, two, three):
    first_core = position()[0] % 2 == 0

    def rows(at, count):
        half_rows = mine.shape[0]
        parts = []
        while count:
            use = min(count, half_rows - at % half_rows)
            here = slice(at % half_rows, at % half_rows + use)
            flag = first_core if at < half_rows else jnp.logical_not(first_core)
            parts.append(jnp.where(flag, mine[here, :], other[here, :]).astype(F32))
            at, count = (at + use, count - use)
        return parts[0] if len(parts) == 1 else jnp.concatenate(parts, axis=0)

    for k in range(27):
        three[k] = rows(64 * k, 64) * scales[2]
        got = rows(G_TWO + 16 * k, 16) * scales[1]
        two[k, 0:16, :] = got[:, :64]
        two[k, 16:32, :] = got[:, 64:]
    got = rows(G_ONE, 48) * scales[0]
    for it in range(9):
        for kh, k in enumerate(taps_of(it)):
            one[k] = got[4 * it : 4 * it + 4, 32 * kh : 32 * kh + 32]


VMEM = pl.BlockSpec(memory_space=pltpu.VMEM)


def near(*shape):
    return pltpu.VMEM(shape, BF)


FAR = pl.BlockSpec(memory_space=pl.ANY)
BANDED = ((320, 1440), (256, 4608))


def run_build(filter_two):
    return pl.pallas_call(
        build,
        out_shape=[jax.ShapeDtypeStruct(shape, BF) for shape in BANDED],
        in_specs=[VMEM],
        out_specs=[FAR] * 2,
        scratch_shapes=[near(*shape) for shape in BANDED] + [pltpu.SemaphoreType.DMA((2,))],
        compiler_params=pltpu.CompilerParams(vmem_limit_bytes=16 * 1024 * 1024),
        cost_estimate=pl.CostEstimate(flops=10**9, bytes_accessed=6 * 10**6, transcendentals=0),
        name="build",
    )(filter_two)


def local_grads(volume, grad, swaps, filter_one, filter_three, banded, rows):
    tables = [jnp.asarray(t, BF) for t in one_hot_tables()]
    args = [volume, grad, *swaps, filter_one, filter_three, *banded, *tables]
    far = (8, 9)
    return pl.pallas_call(
        body,
        out_shape=[jax.ShapeDtypeStruct((rows // 2, 128), BF)] * 2,
        in_specs=[FAR if i in far else VMEM for i in range(len(args))],
        out_specs=[VMEM] * 2,
        scratch_shapes=[
            near(512, 576),
            near(320, 1440),
            near(128, 1728),
            near(256, 4608),
            near(192, 38 * 128),
            near(256, 18 * 128),
            near(2304, 1024),
            near(512, 512),
            near(1728, 768),
            near(4608, 256),
            near(512, 1024),
            near(512, 512),
            near(512, 512),
            near(512, 1024),
            near(rows, 128),
            pltpu.SemaphoreType.DMA((2,)),
        ],
        compiler_params=pltpu.CompilerParams(vmem_limit_bytes=LIMIT * 1024 * 1024),
        cost_estimate=pl.CostEstimate(flops=10**10, bytes_accessed=10**7, transcendentals=0),
        name="local_grads",
    )(*args)


def run_finish(mine, other, cells):
    scales = 1.0 / jnp.sqrt(jnp.array([cells, cells / 8.0, cells / 64.0], F32))
    shapes = [(27, 4, 32), (27, 32, 64), (27, 64, 128)]
    outs = pl.pallas_call(
        finish,
        out_shape=[jax.ShapeDtypeStruct(shape, F32) for shape in shapes],
        in_specs=[pl.BlockSpec(memory_space=pltpu.SMEM), VMEM, VMEM],
        out_specs=[VMEM] * 3,
        name="finish",
    )(scales, mine, other)
    return tuple(o.reshape(3, 3, 3, *o.shape[1:]) for o in outs)


def over_sample(pieces):
    return lax.all_to_all(pieces, "sample", 0, 0, tiled=True)


def over_chips(pieces):
    size = lax.axis_size("space")
    groups = [list(range(core, size, 2)) for core in range(2)]
    return lax.all_to_all(pieces, "space", 0, 0, axis_index_groups=groups, tiled=True)


def total_of(got):
    return got.astype(F32).sum(axis=0).astype(BF)


def swap(values, first):
    size = lax.axis_size("space")
    pairs = [(i, i + 1) for i in range(first, size - 1, 2)]
    return lax.ppermute(values, "space", pairs + [(j, i) for i, j in pairs])


def per_device(volume, grad_out, filter_one, filter_two, filter_three):
    spaces, samples = (lax.axis_size("space"), lax.axis_size("sample"))
    own = volume.reshape(512, 128)
    grad = grad_out.reshape(32, 128)
    f1 = filter_one.reshape(27, 4, 32)
    f2 = filter_two.reshape(27, 32, 64)
    f3 = filter_three.reshape(1728, 128)
    core = lax.axis_index("space") % 2

    def second(block, flip=0):
        planes = lax.dynamic_slice(block, (64 * (core ^ flip), 0), (448, 128))
        return jnp.concatenate([planes, grad], axis=0)

    swap_core = swap(own, 0)
    swap_chip = swap(own, 1)
    relay = second(swap_core)
    swap_chip2 = swap(relay, 1)
    f2_later = lax.optimization_barrier((f2, relay))[0]
    banded = run_build(f2_later)
    swap_chip, *banded = lax.optimization_barrier((swap_chip, *banded))
    swap_core2 = swap(second(swap_chip, 1), 0)
    chips = spaces // 2
    keep, send = local_grads(
        own,
        grad,
        (swap_core, swap_chip, swap_chip2, swap_core2),
        f1,
        f3,
        banded,
        spaces * SLOT,
    )
    half = (keep.astype(F32) + swap(send, 0).astype(F32)).astype(BF)
    part = total_of(over_chips(half.reshape(chips, SLOT, 128)))
    part = total_of(over_sample(jnp.broadcast_to(part[None], (samples, SLOT, 128))))
    mine = over_chips(jnp.broadcast_to(part[None], (chips, SLOT, 128))).reshape(-1, 128)
    cells = float(samples * spaces * volume.shape[1] * volume.shape[3] * volume.shape[4])
    return run_finish(mine, swap(mine, 0), cells)


def solution(mesh):
    return jax.shard_map(
        per_device,
        mesh=mesh,
        in_specs=(
            P(("sample", "space"), None, None, None, None),
            P(("sample", "space"), None, None, None, None),
            P(),
            P(),
            P(),
        ),
        out_specs=(P(), P(), P()),
        check_vma=False,
    )
```

```python
import functools

import jax
import jax.numpy as jnp
import numpy as np
from jax import lax
from jax.experimental import pallas as pl
from jax.experimental.pallas import tpu as pltpu
from jax.sharding import PartitionSpec as P

BF = jnp.bfloat16
F32 = jnp.float32
SLOT = 80
LIMIT = 44
G_TWO = 1728
G_ONE = 2160
NT = (((1,), (1,)), ((), ()))
TN = (((0,), (0,)), ((), ()))


def table(rows, cols):
    return np.zeros((rows, cols), np.float32)


def one_hot_tables():
    perm = table(108, 640)
    for kd in range(3):
        for kh in range(3):
            for kw in range(3):
                for c in range(4):
                    row = ((kd * 3 + kh) * 3 + kw) * 4 + c
                    perm[row, ((kd * 3 + kw) * 4 + c) * 16 + kh] = 0.5
    shift = table(128, 256)
    for w in range(128):
        if w >= 1:
            shift[w - 1, w] = 1.0
        if w + 1 < 128:
            shift[w + 1, 128 + w] = 1.0
    pair = table(256, 384)
    odd = table(256, 384)
    even = table(128, 384)
    for a in range(2):
        for kw in range(3):
            for w in range(64):
                src = w + kw - 1
                if 0 <= src < 64:
                    pair[128 * a + 2 * src, 128 * kw + 64 * a + w] = 1.0
                    odd[64 + 64 * a + src, 128 * kw + 64 * a + w] = 1.0
                    even[64 * a + src, 128 * kw + 64 * a + w] = 1.0
    squeeze = table(512, 128)
    spread = table(128, 1152)
    grow_g = table(96, 768)
    grow2 = table(128, 512)
    for h in range(4):
        for w in range(32):
            squeeze[128 * h + 2 * w, 32 * h + w] = 1.0
            for kh in range(3):
                for kw in range(3):
                    if 0 <= h + kh - 1 < 4 and 0 <= w + kw - 1 < 32:
                        src = 32 * (h + kh - 1) + w + kw - 1
                        spread[src, 128 * (3 * kh + kw) + 32 * h + w] = 1.0
            for n in range(6):
                src = 32 * (n // 2) + 16 * (h // 2) + w // 2
                grow_g[src, 128 * n + 32 * h + w] = 1.0 / 16
            for d in range(2):
                for u in range(2):
                    grow2[32 * h + w, 128 * h + 64 * d + 2 * w + u] = 1.0 / 16
    grow1 = table(256, 512)
    for e in range(4):
        for w in range(128):
            grow1[64 * e + w // 2, 128 * e + w] = 1.0 / 16
    return [perm, shift, pair, odd, even, squeeze, spread, grow_g, grow2, grow1]


def dot(a, b):
    return jnp.dot(a, b, preferred_element_type=F32)


def inside(index, count):
    return jnp.logical_and(index >= 0, index < count)


def position():
    return lax.axis_index("space"), lax.axis_size("space")


def taps_of(it):
    kd, kw = (it // 3, it % 3)
    return [kd * 9 + kh * 3 + kw for kh in range(3)]


def taps_back(it):
    kd, kw = (2 - it // 3, 2 - it % 3)
    return [kd * 9 + (2 - kh) * 3 + kw for kh in range(3)]


def band_one(filter_one, perm, t1):
    lane = lax.broadcasted_iota(jnp.int32, (32, 640), 1) % 16
    rows = filter_one[...].astype(F32).reshape(108, 32).astype(BF)
    base = lax.dot_general(rows, perm[...], TN, preferred_element_type=F32)
    for h in range(16):
        moved = pltpu.roll(base, (h - 1) % 640, 1) if h != 1 else base
        if h == 0:
            moved = jnp.where(lane == 15, 0.0, moved)
        if h == 15:
            moved = jnp.where(lane == 0, 0.0, moved)
        t1[32 * h : 32 * h + 32, :] = moved[:, :576].astype(BF)


def band_two(filter_two, t2):
    taps = []
    for kh in range(3):
        rows = jnp.concatenate([filter_two[taps_of(it)[kh]] for it in range(9)], axis=0)
        taps.append(rows.astype(F32).T * 0.5)
    zero = jnp.zeros((64, 288), F32)
    for s in range(5):
        parts = [taps[p - s + 1] if 0 <= p - s + 1 < 3 else zero for p in range(5)]
        t2[64 * s : 64 * s + 64, :] = jnp.concatenate(parts, axis=1).astype(BF)


def band_two_back(filter_two, t2r):
    for it in range(9):
        v2 = [filter_two[k].astype(F32) for k in taps_back(it)]
        zero = jnp.zeros((32, 64), F32)
        for s in range(-6, 8):
            if -1 <= s <= 2:
                parts = [v2[s + j] if 0 <= s + j <= 2 else zero for j in range(2)]
                tile = jnp.concatenate(parts, axis=1).astype(BF)
            else:
                tile = jnp.zeros((32, 128), BF)
            for m in range(4):
                hp = 2 * m + 1 - s
                if 0 <= hp < 8:
                    t2r[32 * hp : 32 * hp + 32, it * 512 + 128 * m : it * 512 + 128 * m + 128] = tile


def with_column_shifts(rows, shift, x1, at):
    moved = dot(rows, shift[...]).astype(BF)
    for p in range(rows.shape[0] // 64):
        lanes = slice(128 * (at + p), 128 * (at + p) + 128)
        x1[0:64, lanes] = moved[64 * p : 64 * p + 64, :128]
        x1[64:128, lanes] = rows[64 * p : 64 * p + 64, :]
        x1[128:192, lanes] = moved[64 * p : 64 * p + 64, 128:]
    return at + rows.shape[0] // 64


def layer_one(t1, x1, at, scale):
    rhs = jnp.concatenate(
        [x1[:, 128 * (at + kd) : 128 * (at + kd) + 256] for kd in range(3)], axis=0
    )
    half = dot(t1[...], rhs)
    t = jnp.tanh(half)
    act = half + half * t
    act = act[:, :128] + act[:, 128:]
    act = act.reshape(8, 2, 32, 128)
    act = (act[:, 0] + act[:, 1]).reshape(256, 128)
    act = act + pltpu.roll(act, 127, 1)
    return half, t, (act * scale).astype(BF)


def either_of(first_core):
    def either(a, b, lo, hi):
        return jnp.where(first_core, a[lo:hi, :], b[lo:hi, :])

    return either


def near_part(
    vol_own,
    swap_core,
    swap_chip,
    filter_one,
    filter_two,
    filter_three,
    perm,
    shift,
    t1_far,
    t2_far,
    w3t_far,
    t2r_far,
    x1_far,
    pp_far,
    sl1_far,
    t1,
    t2,
    w3t,
    t2r,
    pp,
    sl1,
    x1,
    sems,
):
    me, blocks = position()
    either = either_of(me % 2 == 0)
    copies = []

    def leave(near_ref, far_ref):
        copies.append(pltpu.make_async_copy(near_ref, far_ref, sems.at[len(copies)]))
        copies[-1].start()

    band_two_back(filter_two, t2r)
    leave(t2r, t2r_far)
    band_two(filter_two, t2)
    leave(t2, t2_far)
    w3t[...] = (filter_three[...].astype(F32).T * 0.5).astype(BF)
    leave(w3t, w3t_far)
    band_one(filter_one, perm, t1)
    leave(t1, t1_far)
    at = with_column_shifts(either(swap_chip, swap_core, 64, 512), shift, x1, 0)
    at = with_column_shifts(vol_own[...], shift, x1, at)
    at = with_column_shifts(either(swap_core, swap_chip, 0, 448), shift, x1, at)
    leave(x1.at[:, 768:2048], x1_far)
    for j in range(10):
        scale = jnp.where(inside(4 * me - 3 + j, 4 * blocks), 0.125, 0.0)
        half, t, act = layer_one(t1, x1, 2 * j, scale)
        if 3 <= j < 7:
            slope = (1.0 + t) + half * (1.0 - t * t)
            sl1[:, 256 * (j - 3) : 256 * (j - 3) + 256] = slope.astype(BF)
        pp[:, 128 * j : 128 * j + 128] = act
        if j == 6:
            leave(sl1, sl1_far)
    leave(pp, pp_far)
    for copy in copies:
        copy.wait()


def body(
    swap_core,
    swap_chip,
    swap_chip2,
    swap_core2,
    grad_own,
    filter_three,
    t1_far,
    t2_far,
    w3t_far,
    t2r_far,
    x1_far,
    pp_far,
    sl1_far,
    shift,
    pair,
    odd,
    even,
    squeeze,
    spread,
    grow_g,
    grow2,
    grow1,
    kept,
    sent,
    t1,
    t2,
    w3t,
    t2r,
    x1,
    pp,
    sl1,
    xo,
    x2,
    q,
    x3,
    d2c,
    sl2,
    d2,
    d1,
    out,
    sems,
):
    me, blocks = position()
    first_core = me % 2 == 0
    either = either_of(first_core)
    pairs = (
        (t1_far, t1),
        (pp_far, pp.at[:, 512:1792]),
        (t2_far, t2),
        (w3t_far, w3t),
        (t2r_far, t2r),
        (sl1_far, sl1),
        (x1_far, x1),
    )
    copies = [
        pltpu.make_async_copy(far_ref, near_ref, sems.at[i])
        for i, (far_ref, near_ref) in enumerate(pairs)
    ]
    for copy in copies:
        copy.start()

    at = with_column_shifts(either(swap_chip2, swap_core2, 0, 448), shift, xo, 0)
    at = with_column_shifts(either(swap_chip, swap_core, 0, 192), shift, xo, at)
    at = with_column_shifts(either(swap_core, swap_chip, 320, 512), shift, xo, at)
    at = with_column_shifts(either(swap_core2, swap_chip2, 0, 448), shift, xo, at)
    copies[0].wait()
    for j in (0, 1, 2, 3, 14, 15, 16, 17):
        scale = jnp.where(inside(4 * me - 7 + j, 4 * blocks), 0.125, 0.0)
        act = layer_one(t1, xo, 2 * j if j < 4 else 10 + 2 * (j - 14), scale)[2]
        pp[:, 128 * j : 128 * j + 128] = act
    copies[1].wait()

    for first in range(17):
        got = dot(pp[:, first * 128 : first * 128 + 256], pair[...]).astype(BF)
        for kd in range(3):
            m = (first - kd) // 2
            if (first - kd) % 2 == 0 and 0 <= m < 8:
                for kw in range(3):
                    k = 3 * kd + kw
                    x2[256 * k : 256 * k + 256, m * 128 : m * 128 + 128] = got[
                        :, 128 * kw : 128 * kw + 128
                    ]

    copies[2].wait()
    for c in range(4):
        lanes = slice(c * 256, c * 256 + 256)
        for g in range(2):
            rhs = jnp.concatenate(
                [
                    x2[256 * it + 32 * p : 256 * it + 32 * p + 32, lanes]
                    for p in range(3 * g, 3 * g + 5)
                    for it in range(9)
                ],
                axis=0,
            )
            half = dot(t2[64 * g : 64 * g + 256, :], rhs)
            t = jnp.tanh(half)
            if 1 <= c < 3:
                slope = (1.0 + t) + half * (1.0 - t * t)
                sl2[256 * g : 256 * g + 256, c * 256 - 256 : c * 256] = slope.astype(BF)
            act = (half + half * t).reshape(2, 2, 64, 256)
            act = (act[:, 0] + act[:, 1]).reshape(128, 256)
            for u in range(2):
                tile = act[:, 128 * u : 128 * u + 128]
                tile = tile + pltpu.roll(tile, 64, 1)
                tile = tile + pltpu.roll(tile, 127, 1)
                m = 2 * c + u
                scale = jnp.where(inside(2 * me - 3 + m, 2 * blocks), 0.125, 0.0)
                tile = (tile * scale).astype(BF)
                for h in range(2):
                    lo = 128 * (2 * g + h)
                    q[64 * m : 64 * m + 64, lo : lo + 128] = tile[64 * h : 64 * h + 64, :]

    packed = dot(q[...], squeeze[...]).astype(BF)
    got = dot(packed, spread[...]).astype(BF)
    for kd in range(3):
        for s in range(9):
            k = 9 * kd + s
            for n in range(6):
                x3[64 * k : 64 * k + 64, 128 * n : 128 * n + 128] = got[
                    64 * (n + kd) : 64 * (n + kd) + 64, 128 * s : 128 * s + 128
                ]
    rows = jnp.concatenate(
        [
            either(swap_chip2, swap_core2, 448, 480),
            grad_own[...],
            either(swap_core2, swap_chip2, 448, 480),
        ],
        axis=0,
    )
    grown = dot(rows.astype(F32).T.astype(BF), grow_g[...])
    copies[3].wait()
    half = dot(w3t[...], x3[...])
    t = jnp.tanh(half)
    d3 = (grown * ((1.0 + t) + half * (1.0 - t * t))).astype(BF)

    out[:G_TWO, :] = lax.dot_general(
        x3[:, 256:512], d3[:, 256:512], NT, preferred_element_type=F32
    ).astype(BF)

    lane = lax.broadcasted_iota(jnp.int32, (64, 128), 1)
    col, line = (lane % 32, lane // 32)
    masks = []
    for b in range(3):
        for c in range(3):
            keep = inside(col + 1 - c, 32)
            masks.append(jnp.logical_and(keep, inside(line + 1 - b, 4)))
    lhs = jnp.concatenate([filter_three[576 * a : 576 * a + 576, :] for a in range(3)], axis=1)
    grown = []
    for pair_at in range(2):
        rhs = jnp.concatenate(
            [
                d3[:, 128 * (2 * pair_at + 2 - a) : 128 * (2 * pair_at + 2 - a) + 256]
                for a in range(3)
            ],
            axis=0,
        )
        got = dot(lhs, rhs)
        for u in range(2):
            total = None
            for b in range(3):
                for c in range(3):
                    s = 3 * b + c
                    part = got[64 * s : 64 * s + 64, 128 * u : 128 * u + 128]
                    move_by = -(32 * (1 - b) + 1 - c) % 128
                    if move_by:
                        part = jnp.where(masks[s], pltpu.roll(part, move_by, 1), 0.0)
                    total = part if total is None else total + part
            n = 2 * pair_at + u
            scale = jnp.where(inside(2 * me - 1 + n, 2 * blocks), 1.0, 0.0)
            grown.append((total * scale).astype(BF))
    back = dot(jnp.concatenate(grown, axis=0), grow2[...])
    for h in range(8):
        rows = slice(64 * h, 64 * h + 64)
        for n in range(4):
            lanes = slice(128 * n, 128 * n + 128)
            source = back[64 * n : 64 * n + 64, 128 * (h // 2) : 128 * (h // 2) + 128]
            d2[rows, lanes] = (source * sl2[rows, lanes].astype(F32)).astype(BF)

    for start in range(1, 6):
        u = start // 2
        if start % 2:
            got = dot(d2[:, 128 * u : 128 * u + 256], odd[...])
        else:
            got = dot(d2[:, 128 * u : 128 * u + 128], even[...])
        got = got.astype(BF)
        for kd in range(3):
            for m in range(2):
                if 1 + kd + 2 * m == start:
                    for kw in range(3):
                        k = 3 * kd + kw
                        d2c[512 * k : 512 * k + 512, 128 * m : 128 * m + 128] = got[
                            :, 128 * kw : 128 * kw + 128
                        ]
    copies[4].wait()
    back = dot(t2r[...], d2c[...]).astype(BF)
    copies[5].wait()
    back = dot(back, grow1[...])
    for h in range(16):
        rows = slice(32 * h, 32 * h + 32)
        source = back[32 * (h // 2) : 32 * (h // 2) + 32, :]
        for e in range(8):
            lanes = slice(128 * e, 128 * e + 128)
            delta = source[:, 128 * (e // 2) : 128 * (e // 2) + 128] * sl1[rows, lanes].astype(F32)
            d1[rows, lanes] = delta.astype(BF)

    lane16 = lax.broadcasted_iota(jnp.int32, (16, 128), 1)
    all_two = lax.dot_general(
        x2[:, 384:640], d2[:, 128:384], NT, preferred_element_type=F32
    )
    for it in range(9):
        got = all_two[256 * it : 256 * it + 256, :]
        for kh, k in enumerate(taps_of(it)):
            totals = [None, None]
            for h in range(8):
                hp = h + kh - 1
                if 0 <= hp < 8:
                    part = got[32 * hp : 32 * hp + 32, 128 * (h // 2) : 128 * (h // 2) + 128]
                    now = totals[h % 2]
                    totals[h % 2] = part if now is None else now + part
            low = totals[0] + pltpu.roll(totals[1], 64, 1)
            high = pltpu.roll(totals[0], 64, 1) + totals[1]
            out[G_TWO + k * 16 : G_TWO + k * 16 + 16, :] = jnp.where(
                lane16 < 64, low[:16], high[16:]
            ).astype(BF)

    copies[6].wait()
    lhs = jnp.concatenate([x1[:, 128 * kd : 128 * kd + 1024] for kd in range(3)], axis=0)
    got = lax.dot_general(lhs, d1[...], NT, preferred_element_type=F32)
    row = lax.broadcasted_iota(jnp.int32, (576, 128), 0) % 16
    col = lax.broadcasted_iota(jnp.int32, (576, 128), 1) // 32
    lane36 = lax.broadcasted_iota(jnp.int32, (36, 128), 1)
    packed = jnp.zeros((36, 128), F32)
    for kh in range(3):
        total = jnp.zeros((576, 128), F32)
        for u in range(4):
            keep = row == col + (4 * u + kh - 1)
            total = total + jnp.where(keep, got[:, 128 * u : 128 * u + 128], 0.0)
        total = total.reshape(36, 16, 128).sum(axis=1)
        total = total + pltpu.roll(total, 64, 1)
        total = total + pltpu.roll(total, 32, 1)
        packed = packed + jnp.where(lane36 // 32 == kh, total, 0.0)
    out[G_ONE : G_ONE + 48, :] = jnp.concatenate(
        [packed, jnp.zeros((12, 128), F32)], axis=0
    ).astype(BF)
    out[G_ONE + 48 :, :] = jnp.zeros((out.shape[0] - G_ONE - 48, 128), BF)
    half_rows = kept.shape[0]
    mine = pl.multiple_of(me % 2 * half_rows, half_rows)
    kept[...] = out[pl.ds(mine, half_rows), :]
    sent[...] = out[pl.ds(half_rows - mine, half_rows), :]


def finish(scales, mine, other, one_far, two_far, three_far, one, two, three, sems):
    first_core = position()[0] % 2 == 0
    half_rows = mine.shape[0]

    def rows(at, count):
        parts = []
        while count:
            use = min(count, half_rows - at % half_rows)
            here = slice(at % half_rows, at % half_rows + use)
            flag = first_core if at < half_rows else jnp.logical_not(first_core)
            parts.append(jnp.where(flag, mine[here, :], other[here, :]).astype(F32))
            at, count = (at + use, count - use)
        return parts[0] if len(parts) == 1 else jnp.concatenate(parts, axis=0)

    copies = []

    def leave(near_ref, far_ref):
        copies.append(pltpu.make_async_copy(near_ref, far_ref, sems.at[len(copies)]))
        copies[-1].start()

    for k in range(27):
        got = rows(G_TWO + 16 * k, 16) * scales[1]
        two[k, 0:16, :] = got[:, :64]
        two[k, 16:32, :] = got[:, 64:]
    leave(two, two_far)
    got = rows(G_ONE, 48) * scales[0]
    for it in range(9):
        for kh, k in enumerate(taps_of(it)):
            one[k] = got[4 * it : 4 * it + 4, 32 * kh : 32 * kh + 32]
    leave(one, one_far)
    for third in range(3):
        for k in range(9 * third, 9 * third + 9):
            three[k] = rows(64 * k, 64) * scales[2]
        here = slice(9 * third, 9 * third + 9)
        leave(three.at[here], three_far.at[here])
    for copy in copies:
        copy.wait()


VMEM = pl.BlockSpec(memory_space=pltpu.VMEM)


def near(*shape):
    return pltpu.VMEM(shape, BF)


FAR = pl.BlockSpec(memory_space=pl.ANY)
HANDED = (
    (512, 576),
    (320, 1440),
    (128, 1728),
    (256, 4608),
    (192, 1280),
    (256, 1280),
    (512, 1024),
)


def run_near(volume, swap_core, swap_chip, filter_one, filter_two, filter_three):
    tables = [jnp.asarray(t, BF) for t in one_hot_tables()[:2]]
    args = [volume, swap_core, swap_chip, filter_one, filter_two, filter_three, *tables]
    return pl.pallas_call(
        near_part,
        out_shape=[jax.ShapeDtypeStruct(shape, BF) for shape in HANDED],
        in_specs=[VMEM] * len(args),
        out_specs=[FAR] * len(HANDED),
        scratch_shapes=[near(*shape) for shape in HANDED[:4] + HANDED[5:]]
        + [near(192, 22 * 128), pltpu.SemaphoreType.DMA((len(HANDED),))],
        compiler_params=pltpu.CompilerParams(vmem_limit_bytes=20 * 1024 * 1024),
        cost_estimate=pl.CostEstimate(
            flops=3 * 10**9, bytes_accessed=8 * 10**6, transcendentals=0
        ),
        name="near_part",
    )(*args)


def local_grads(swaps, grad, filter_three, handed, rows):
    tables = [jnp.asarray(t, BF) for t in one_hot_tables()[1:]]
    args = [*swaps, grad, filter_three, *handed, *tables]
    far = range(6, 6 + len(HANDED))
    return pl.pallas_call(
        body,
        out_shape=[jax.ShapeDtypeStruct((rows // 2, 128), BF)] * 2,
        in_specs=[FAR if i in far else VMEM for i in range(len(args))],
        out_specs=[VMEM] * 2,
        scratch_shapes=[near(*shape) for shape in HANDED[:5]]
        + [
            near(256, 18 * 128),
            near(512, 1024),
            near(192, 20 * 128),
            near(2304, 1024),
            near(512, 512),
            near(1728, 768),
            near(4608, 256),
            near(512, 512),
            near(512, 512),
            near(512, 1024),
            near(rows, 128),
            pltpu.SemaphoreType.DMA((len(HANDED),)),
        ],
        compiler_params=pltpu.CompilerParams(vmem_limit_bytes=LIMIT * 1024 * 1024),
        cost_estimate=pl.CostEstimate(flops=10**10, bytes_accessed=10**7, transcendentals=0),
        name="local_grads",
    )(*args)


def run_finish(mine, other, cells):
    scales = [float(1.0 / np.sqrt(cells / size)) for size in (1.0, 8.0, 64.0)]
    shapes = [(27, 4, 32), (27, 32, 64), (27, 64, 128)]
    outs = pl.pallas_call(
        functools.partial(finish, scales),
        out_shape=[jax.ShapeDtypeStruct(shape, F32) for shape in shapes],
        in_specs=[VMEM] * 2,
        out_specs=[FAR] * 3,
        scratch_shapes=[pltpu.VMEM(shape, F32) for shape in shapes]
        + [pltpu.SemaphoreType.DMA((5,))],
        name="finish",
    )(mine, other)
    return tuple(o.reshape(3, 3, 3, *o.shape[1:]) for o in outs)


def over_sample(pieces):
    return lax.all_to_all(pieces, "sample", 0, 0, tiled=True)


def over_chips(pieces):
    size = lax.axis_size("space")
    groups = [list(range(core, size, 2)) for core in range(2)]
    return lax.all_to_all(pieces, "space", 0, 0, axis_index_groups=groups, tiled=True)


def total_of(got):
    return got.astype(F32).sum(axis=0).astype(BF)


def swap(values, first):
    size = lax.axis_size("space")
    pairs = [(i, i + 1) for i in range(first, size - 1, 2)]
    return lax.ppermute(values, "space", pairs + [(j, i) for i, j in pairs])


def per_device(volume, grad_out, filter_one, filter_two, filter_three):
    spaces, samples = (lax.axis_size("space"), lax.axis_size("sample"))
    own = volume.reshape(512, 128)
    grad = grad_out.reshape(32, 128)
    f1 = filter_one.reshape(27, 4, 32)
    f2 = filter_two.reshape(27, 32, 64)
    f3 = filter_three.reshape(1728, 128)
    core = lax.axis_index("space") % 2

    def second(block, flip=0):
        planes = lax.dynamic_slice(block, (64 * (core ^ flip), 0), (448, 128))
        return jnp.concatenate([planes, grad], axis=0)

    swap_core = swap(own, 0)
    swap_chip = swap(own, 1)
    relay = second(swap_core)
    swap_chip2 = swap(relay, 1)
    chip_later = lax.optimization_barrier((swap_chip, relay))[0]
    swap_core2 = swap(second(chip_later, 1), 0)
    chips = spaces // 2
    handed = run_near(own, swap_core, swap_chip, f1, f2, f3)
    keep, send = local_grads(
        (swap_core, swap_chip, swap_chip2, swap_core2), grad, f3, handed, spaces * SLOT
    )
    half = (keep.astype(F32) + swap(send, 0).astype(F32)).astype(BF)
    part = total_of(over_chips(half.reshape(chips, SLOT, 128)))
    part = total_of(over_sample(jnp.broadcast_to(part[None], (samples, SLOT, 128))))
    mine = over_chips(jnp.broadcast_to(part[None], (chips, SLOT, 128))).reshape(-1, 128)
    cells = float(samples * spaces * volume.shape[1] * volume.shape[3] * volume.shape[4])
    return run_finish(mine, swap(mine, 0), cells)


def solution(mesh):
    return jax.shard_map(
        per_device,
        mesh=mesh,
        in_specs=(
            P(("sample", "space"), None, None, None, None),
            P(("sample", "space"), None, None, None, None),
            P(),
            P(),
            P(),
        ),
        out_specs=(P(), P(), P()),
        check_vma=False,
    )
```

```python
import functools

import jax
import jax.numpy as jnp
import numpy as np
from jax import lax
from jax.experimental import pallas as pl
from jax.experimental.pallas import tpu as pltpu
from jax.sharding import PartitionSpec as P

BF = jnp.bfloat16
F32 = jnp.float32
SLOT = 80
LIMIT = 44
G_TWO = 1728
G_ONE = 2160
NT = (((1,), (1,)), ((), ()))
TN = (((0,), (0,)), ((), ()))


def table(rows, cols):
    return np.zeros((rows, cols), np.float32)


def one_hot_tables():
    perm = table(108, 640)
    for kd in range(3):
        for kh in range(3):
            for kw in range(3):
                for c in range(4):
                    row = ((kd * 3 + kh) * 3 + kw) * 4 + c
                    perm[row, ((kd * 3 + kw) * 4 + c) * 16 + kh] = 0.5
    shift = table(128, 256)
    for w in range(128):
        if w >= 1:
            shift[w - 1, w] = 1.0
        if w + 1 < 128:
            shift[w + 1, 128 + w] = 1.0
    pair = table(256, 384)
    odd = table(256, 384)
    even = table(128, 384)
    for a in range(2):
        for kw in range(3):
            for w in range(64):
                src = w + kw - 1
                if 0 <= src < 64:
                    pair[128 * a + 2 * src, 128 * kw + 64 * a + w] = 1.0
                    odd[64 + 64 * a + src, 128 * kw + 64 * a + w] = 1.0
                    even[64 * a + src, 128 * kw + 64 * a + w] = 1.0
    squeeze = table(512, 128)
    spread = table(128, 1152)
    grow_g = table(96, 768)
    grow2 = table(128, 512)
    for h in range(4):
        for w in range(32):
            squeeze[128 * h + 2 * w, 32 * h + w] = 1.0
            for kh in range(3):
                for kw in range(3):
                    if 0 <= h + kh - 1 < 4 and 0 <= w + kw - 1 < 32:
                        src = 32 * (h + kh - 1) + w + kw - 1
                        spread[src, 128 * (3 * kh + kw) + 32 * h + w] = 1.0
            for n in range(6):
                src = 32 * (n // 2) + 16 * (h // 2) + w // 2
                grow_g[src, 128 * n + 32 * h + w] = 1.0 / 16
            for d in range(2):
                for u in range(2):
                    grow2[32 * h + w, 128 * h + 64 * d + 2 * w + u] = 1.0 / 16
    grow1 = table(256, 512)
    for e in range(4):
        for w in range(128):
            grow1[64 * e + w // 2, 128 * e + w] = 1.0 / 16
    return [perm, shift, pair, odd, even, squeeze, spread, grow_g, grow2, grow1]


def dot(a, b):
    return jnp.dot(a, b, preferred_element_type=F32)


def inside(index, count):
    return jnp.logical_and(index >= 0, index < count)


def position():
    return lax.axis_index("space"), lax.axis_size("space")


def taps_of(it):
    kd, kw = (it // 3, it % 3)
    return [kd * 9 + kh * 3 + kw for kh in range(3)]


def taps_back(it):
    kd, kw = (2 - it // 3, 2 - it % 3)
    return [kd * 9 + (2 - kh) * 3 + kw for kh in range(3)]


def build(filter_two, t2, t2r):
    for it in range(9):
        v2 = [filter_two[k].astype(F32) for k in taps_back(it)]
        zero = jnp.zeros((32, 64), F32)
        for s in range(-6, 8):
            if -1 <= s <= 2:
                parts = [v2[s + j] if 0 <= s + j <= 2 else zero for j in range(2)]
                tile = jnp.concatenate(parts, axis=1).astype(BF)
            else:
                tile = jnp.zeros((32, 128), BF)
            for m in range(4):
                hp = 2 * m + 1 - s
                if 0 <= hp < 8:
                    t2r[32 * hp : 32 * hp + 32, it * 512 + 128 * m : it * 512 + 128 * m + 128] = tile
    taps = []
    for kh in range(3):
        rows = jnp.concatenate([filter_two[taps_of(it)[kh]] for it in range(9)], axis=0)
        taps.append(rows.astype(F32).T * 0.5)
    zero = jnp.zeros((64, 288), F32)
    for s in range(5):
        parts = [taps[p - s + 1] if 0 <= p - s + 1 < 3 else zero for p in range(5)]
        t2[64 * s : 64 * s + 64, :] = jnp.concatenate(parts, axis=1).astype(BF)


def body(
    vol_own,
    grad_own,
    swap_core,
    swap_chip,
    swap_chip2,
    swap_core2,
    filter_one,
    filter_three,
    t2,
    t2r,
    perm,
    shift,
    pair,
    odd,
    even,
    squeeze,
    spread,
    grow_g,
    grow2,
    grow1,
    kept,
    sent,
    t1,
    w3t,
    x1,
    pp,
    x2,
    q,
    x3,
    d2c,
    sl1,
    sl2,
    d2,
    d1,
    out,
):
    me, blocks = position()
    first_core = me % 2 == 0
    lane = lax.broadcasted_iota(jnp.int32, (32, 640), 1) % 16
    rows = filter_one[...].astype(F32).reshape(108, 32).astype(BF)
    base = lax.dot_general(rows, perm[...], TN, preferred_element_type=F32)
    for h in range(16):
        moved = pltpu.roll(base, (h - 1) % 640, 1) if h != 1 else base
        if h == 0:
            moved = jnp.where(lane == 15, 0.0, moved)
        if h == 15:
            moved = jnp.where(lane == 0, 0.0, moved)
        t1[32 * h : 32 * h + 32, :] = moved[:, :576].astype(BF)
    w3t[...] = (filter_three[...].astype(F32).T * 0.5).astype(BF)

    def either(a, b, lo, hi):
        return jnp.where(first_core, a[lo:hi, :], b[lo:hi, :])

    at = 0
    for rows in (
        either(swap_chip2, swap_core2, 0, 448),
        either(swap_chip, swap_core, 0, 512),
        vol_own[...],
        either(swap_core, swap_chip, 0, 512),
        either(swap_core2, swap_chip2, 0, 448),
    ):
        moved = dot(rows, shift[...]).astype(BF)
        count = rows.shape[0] // 64
        for p in range(count):
            lanes = slice(128 * (at + p), 128 * (at + p) + 128)
            x1[0:64, lanes] = moved[64 * p : 64 * p + 64, :128]
            x1[64:128, lanes] = rows[64 * p : 64 * p + 64, :]
            x1[128:192, lanes] = moved[64 * p : 64 * p + 64, 128:]
        at += count

    for j in range(18):
        rhs = jnp.concatenate(
            [x1[:, (2 * j + kd) * 128 : (2 * j + kd) * 128 + 256] for kd in range(3)], axis=0
        )
        half = dot(t1[...], rhs)
        t = jnp.tanh(half)
        if 7 <= j < 11:
            slope = (1.0 + t) + half * (1.0 - t * t)
            sl1[:, (j - 7) * 256 : (j - 7) * 256 + 256] = slope.astype(BF)
        act = half + half * t
        act = act[:, :128] + act[:, 128:]
        act = act.reshape(8, 2, 32, 128)
        act = (act[:, 0] + act[:, 1]).reshape(256, 128)
        act = act + pltpu.roll(act, 127, 1)
        scale = jnp.where(inside(4 * me - 7 + j, 4 * blocks), 0.125, 0.0)
        pp[:, j * 128 : j * 128 + 128] = (act * scale).astype(BF)

    for first in range(17):
        got = dot(pp[:, first * 128 : first * 128 + 256], pair[...]).astype(BF)
        for kd in range(3):
            m = (first - kd) // 2
            if (first - kd) % 2 == 0 and 0 <= m < 8:
                for kw in range(3):
                    k = 3 * kd + kw
                    x2[256 * k : 256 * k + 256, m * 128 : m * 128 + 128] = got[
                        :, 128 * kw : 128 * kw + 128
                    ]

    for c in range(4):
        lanes = slice(c * 256, c * 256 + 256)
        for g in range(2):
            rhs = jnp.concatenate(
                [
                    x2[256 * it + 32 * p : 256 * it + 32 * p + 32, lanes]
                    for p in range(3 * g, 3 * g + 5)
                    for it in range(9)
                ],
                axis=0,
            )
            half = dot(t2[64 * g : 64 * g + 256, :], rhs)
            t = jnp.tanh(half)
            if 1 <= c < 3:
                slope = (1.0 + t) + half * (1.0 - t * t)
                sl2[256 * g : 256 * g + 256, c * 256 - 256 : c * 256] = slope.astype(BF)
            act = (half + half * t).reshape(2, 2, 64, 256)
            act = (act[:, 0] + act[:, 1]).reshape(128, 256)
            for u in range(2):
                tile = act[:, 128 * u : 128 * u + 128]
                tile = tile + pltpu.roll(tile, 64, 1)
                tile = tile + pltpu.roll(tile, 127, 1)
                m = 2 * c + u
                scale = jnp.where(inside(2 * me - 3 + m, 2 * blocks), 0.125, 0.0)
                tile = (tile * scale).astype(BF)
                for h in range(2):
                    lo = 128 * (2 * g + h)
                    q[64 * m : 64 * m + 64, lo : lo + 128] = tile[64 * h : 64 * h + 64, :]

    packed = dot(q[...], squeeze[...]).astype(BF)
    got = dot(packed, spread[...]).astype(BF)
    for kd in range(3):
        for s in range(9):
            k = 9 * kd + s
            for n in range(6):
                x3[64 * k : 64 * k + 64, 128 * n : 128 * n + 128] = got[
                    64 * (n + kd) : 64 * (n + kd) + 64, 128 * s : 128 * s + 128
                ]
    rows = jnp.concatenate(
        [
            either(swap_chip2, swap_core2, 448, 480),
            grad_own[...],
            either(swap_core2, swap_chip2, 448, 480),
        ],
        axis=0,
    )
    grown = dot(rows.astype(F32).T.astype(BF), grow_g[...])
    half = dot(w3t[...], x3[...])
    t = jnp.tanh(half)
    d3 = (grown * ((1.0 + t) + half * (1.0 - t * t))).astype(BF)

    out[:G_TWO, :] = lax.dot_general(
        x3[:, 256:512], d3[:, 256:512], NT, preferred_element_type=F32
    ).astype(BF)

    lane = lax.broadcasted_iota(jnp.int32, (64, 128), 1)
    col, line = (lane % 32, lane // 32)
    masks = []
    for b in range(3):
        for c in range(3):
            keep = inside(col + 1 - c, 32)
            masks.append(jnp.logical_and(keep, inside(line + 1 - b, 4)))
    lhs = jnp.concatenate([filter_three[576 * a : 576 * a + 576, :] for a in range(3)], axis=1)
    grown = []
    for pair_at in range(2):
        rhs = jnp.concatenate(
            [
                d3[:, 128 * (2 * pair_at + 2 - a) : 128 * (2 * pair_at + 2 - a) + 256]
                for a in range(3)
            ],
            axis=0,
        )
        got = dot(lhs, rhs)
        for u in range(2):
            total = None
            for b in range(3):
                for c in range(3):
                    s = 3 * b + c
                    part = got[64 * s : 64 * s + 64, 128 * u : 128 * u + 128]
                    move_by = -(32 * (1 - b) + 1 - c) % 128
                    if move_by:
                        part = jnp.where(masks[s], pltpu.roll(part, move_by, 1), 0.0)
                    total = part if total is None else total + part
            n = 2 * pair_at + u
            scale = jnp.where(inside(2 * me - 1 + n, 2 * blocks), 1.0, 0.0)
            grown.append((total * scale).astype(BF))
    back = dot(jnp.concatenate(grown, axis=0), grow2[...])
    for h in range(8):
        rows = slice(64 * h, 64 * h + 64)
        for n in range(4):
            lanes = slice(128 * n, 128 * n + 128)
            source = back[64 * n : 64 * n + 64, 128 * (h // 2) : 128 * (h // 2) + 128]
            d2[rows, lanes] = (source * sl2[rows, lanes].astype(F32)).astype(BF)

    for start in range(1, 6):
        u = start // 2
        if start % 2:
            got = dot(d2[:, 128 * u : 128 * u + 256], odd[...])
        else:
            got = dot(d2[:, 128 * u : 128 * u + 128], even[...])
        got = got.astype(BF)
        for kd in range(3):
            for m in range(2):
                if 1 + kd + 2 * m == start:
                    for kw in range(3):
                        k = 3 * kd + kw
                        d2c[512 * k : 512 * k + 512, 128 * m : 128 * m + 128] = got[
                            :, 128 * kw : 128 * kw + 128
                        ]
    back = dot(t2r[...], d2c[...]).astype(BF)
    back = dot(back, grow1[...])
    for h in range(16):
        rows = slice(32 * h, 32 * h + 32)
        source = back[32 * (h // 2) : 32 * (h // 2) + 32, :]
        for e in range(8):
            lanes = slice(128 * e, 128 * e + 128)
            delta = source[:, 128 * (e // 2) : 128 * (e // 2) + 128] * sl1[rows, lanes].astype(F32)
            d1[rows, lanes] = delta.astype(BF)

    lane16 = lax.broadcasted_iota(jnp.int32, (16, 128), 1)
    all_two = lax.dot_general(
        x2[:, 384:640], d2[:, 128:384], NT, preferred_element_type=F32
    )
    for it in range(9):
        got = all_two[256 * it : 256 * it + 256, :]
        for kh, k in enumerate(taps_of(it)):
            totals = [None, None]
            for h in range(8):
                hp = h + kh - 1
                if 0 <= hp < 8:
                    part = got[32 * hp : 32 * hp + 32, 128 * (h // 2) : 128 * (h // 2) + 128]
                    now = totals[h % 2]
                    totals[h % 2] = part if now is None else now + part
            low = totals[0] + pltpu.roll(totals[1], 64, 1)
            high = pltpu.roll(totals[0], 64, 1) + totals[1]
            out[G_TWO + k * 16 : G_TWO + k * 16 + 16, :] = jnp.where(
                lane16 < 64, low[:16], high[16:]
            ).astype(BF)

    lhs = jnp.concatenate([x1[:, 128 * (14 + kd) : 128 * (14 + kd) + 1024] for kd in range(3)], axis=0)
    got = lax.dot_general(lhs, d1[...], NT, preferred_element_type=F32)
    row = lax.broadcasted_iota(jnp.int32, (576, 128), 0) % 16
    col = lax.broadcasted_iota(jnp.int32, (576, 128), 1) // 32
    lane36 = lax.broadcasted_iota(jnp.int32, (36, 128), 1)
    packed = jnp.zeros((36, 128), F32)
    for kh in range(3):
        total = jnp.zeros((576, 128), F32)
        for u in range(4):
            keep = row == col + (4 * u + kh - 1)
            total = total + jnp.where(keep, got[:, 128 * u : 128 * u + 128], 0.0)
        total = total.reshape(36, 16, 128).sum(axis=1)
        total = total + pltpu.roll(total, 64, 1)
        total = total + pltpu.roll(total, 32, 1)
        packed = packed + jnp.where(lane36 // 32 == kh, total, 0.0)
    out[G_ONE : G_ONE + 48, :] = jnp.concatenate(
        [packed, jnp.zeros((12, 128), F32)], axis=0
    ).astype(BF)
    out[G_ONE + 48 :, :] = jnp.zeros((out.shape[0] - G_ONE - 48, 128), BF)
    half_rows = kept.shape[0]
    mine = pl.multiple_of(me % 2 * half_rows, half_rows)
    kept[...] = out[pl.ds(mine, half_rows), :]
    sent[...] = out[pl.ds(half_rows - mine, half_rows), :]


def finish(scales, mine, other, one_far, two_far, three_far, one, two, three, sems):
    first_core = position()[0] % 2 == 0
    half_rows = mine.shape[0]

    def rows(at, count):
        parts = []
        while count:
            use = min(count, half_rows - at % half_rows)
            here = slice(at % half_rows, at % half_rows + use)
            flag = first_core if at < half_rows else jnp.logical_not(first_core)
            parts.append(jnp.where(flag, mine[here, :], other[here, :]).astype(F32))
            at, count = (at + use, count - use)
        return parts[0] if len(parts) == 1 else jnp.concatenate(parts, axis=0)

    copies = []

    def leave(near_ref, far_ref):
        copies.append(pltpu.make_async_copy(near_ref, far_ref, sems.at[len(copies)]))
        copies[-1].start()

    for k in range(27):
        got = rows(G_TWO + 16 * k, 16) * scales[1]
        two[k, 0:16, :] = got[:, :64]
        two[k, 16:32, :] = got[:, 64:]
    leave(two, two_far)
    got = rows(G_ONE, 48) * scales[0]
    for it in range(9):
        for kh, k in enumerate(taps_of(it)):
            one[k] = got[4 * it : 4 * it + 4, 32 * kh : 32 * kh + 32]
    leave(one, one_far)
    for third in range(3):
        for k in range(9 * third, 9 * third + 9):
            three[k] = rows(64 * k, 64) * scales[2]
        here = slice(9 * third, 9 * third + 9)
        leave(three.at[here], three_far.at[here])
    for copy in copies:
        copy.wait()


VMEM = pl.BlockSpec(memory_space=pltpu.VMEM)


def near(*shape):
    return pltpu.VMEM(shape, BF)


FAR = pl.BlockSpec(memory_space=pl.ANY)
BANDED = ((320, 1440), (256, 4608))


def run_build(filter_two):
    return pl.pallas_call(
        build,
        out_shape=[jax.ShapeDtypeStruct(shape, BF) for shape in BANDED],
        in_specs=[VMEM],
        out_specs=[VMEM] * 2,
        compiler_params=pltpu.CompilerParams(vmem_limit_bytes=16 * 1024 * 1024),
        cost_estimate=pl.CostEstimate(flops=10**9, bytes_accessed=6 * 10**6, transcendentals=0),
        name="build",
    )(filter_two)


def local_grads(volume, grad, swaps, filter_one, filter_three, banded, rows):
    tables = [jnp.asarray(t, BF) for t in one_hot_tables()]
    args = [volume, grad, *swaps, filter_one, filter_three, *banded, *tables]
    return pl.pallas_call(
        body,
        out_shape=[jax.ShapeDtypeStruct((rows // 2, 128), BF)] * 2,
        in_specs=[VMEM] * len(args),
        out_specs=[VMEM] * 2,
        scratch_shapes=[
            near(512, 576),
            near(128, 1728),
            near(192, 38 * 128),
            near(256, 18 * 128),
            near(2304, 1024),
            near(512, 512),
            near(1728, 768),
            near(4608, 256),
            near(512, 1024),
            near(512, 512),
            near(512, 512),
            near(512, 1024),
            near(rows, 128),
        ],
        compiler_params=pltpu.CompilerParams(vmem_limit_bytes=LIMIT * 1024 * 1024),
        cost_estimate=pl.CostEstimate(flops=10**10, bytes_accessed=10**7, transcendentals=0),
        name="local_grads",
    )(*args)


def run_finish(mine, other, cells):
    scales = [float(1.0 / np.sqrt(cells / size)) for size in (1.0, 8.0, 64.0)]
    shapes = [(27, 4, 32), (27, 32, 64), (27, 64, 128)]
    outs = pl.pallas_call(
        functools.partial(finish, scales),
        out_shape=[jax.ShapeDtypeStruct(shape, F32) for shape in shapes],
        in_specs=[VMEM] * 2,
        out_specs=[FAR] * 3,
        scratch_shapes=[pltpu.VMEM(shape, F32) for shape in shapes]
        + [pltpu.SemaphoreType.DMA((5,))],
        compiler_params=pltpu.CompilerParams(vmem_limit_bytes=8 * 1024 * 1024),
        name="finish",
    )(mine, other)
    return tuple(o.reshape(3, 3, 3, *o.shape[1:]) for o in outs)


def over_sample(pieces):
    return lax.all_to_all(pieces, "sample", 0, 0, tiled=True)


def over_chips(pieces):
    size = lax.axis_size("space")
    groups = [list(range(core, size, 2)) for core in range(2)]
    return lax.all_to_all(pieces, "space", 0, 0, axis_index_groups=groups, tiled=True)


def total_of(got):
    return got.astype(F32).sum(axis=0).astype(BF)


def swap(values, first):
    size = lax.axis_size("space")
    pairs = [(i, i + 1) for i in range(first, size - 1, 2)]
    return lax.ppermute(values, "space", pairs + [(j, i) for i, j in pairs])


def per_device(volume, grad_out, filter_one, filter_two, filter_three):
    spaces, samples = (lax.axis_size("space"), lax.axis_size("sample"))
    own = volume.reshape(512, 128)
    grad = grad_out.reshape(32, 128)
    f1 = filter_one.reshape(27, 4, 32)
    f2 = filter_two.reshape(27, 32, 64)
    f3 = filter_three.reshape(1728, 128)
    core = lax.axis_index("space") % 2

    def second(block, flip=0):
        planes = lax.dynamic_slice(block, (64 * (core ^ flip), 0), (448, 128))
        return jnp.concatenate([planes, grad], axis=0)

    swap_core = swap(own, 0)
    swap_chip = swap(own, 1)
    relay = second(swap_core)
    swap_chip2 = swap(relay, 1)
    f2_later = lax.optimization_barrier((f2, relay))[0]
    banded = run_build(f2_later)
    swap_chip, *banded = lax.optimization_barrier((swap_chip, *banded))
    swap_core2 = swap(second(swap_chip, 1), 0)
    chips = spaces // 2
    keep, send = local_grads(
        own,
        grad,
        (swap_core, swap_chip, swap_chip2, swap_core2),
        f1,
        f3,
        banded,
        spaces * SLOT,
    )
    half = (keep.astype(F32) + swap(send, 0).astype(F32)).astype(BF)
    part = total_of(over_chips(half.reshape(chips, SLOT, 128)))
    part = total_of(over_sample(jnp.broadcast_to(part[None], (samples, SLOT, 128))))
    mine = over_chips(jnp.broadcast_to(part[None], (chips, SLOT, 128))).reshape(-1, 128)
    cells = float(samples * spaces * volume.shape[1] * volume.shape[3] * volume.shape[4])
    return run_finish(mine, swap(mine, 0), cells)


def solution(mesh):
    return jax.shard_map(
        per_device,
        mesh=mesh,
        in_specs=(
            P(("sample", "space"), None, None, None, None),
            P(("sample", "space"), None, None, None, None),
            P(),
            P(),
            P(),
        ),
        out_specs=(P(), P(), P()),
        check_vma=False,
    )
```

```python
import functools

import jax
import jax.numpy as jnp
import numpy as np
from jax import lax
from jax.experimental import pallas as pl
from jax.experimental.pallas import tpu as pltpu
from jax.sharding import PartitionSpec as P

BF = jnp.bfloat16
F32 = jnp.float32
SLOT = 72
LIMIT = 44
G_TWO = 1728
G_ONE = 2160
NT = (((1,), (1,)), ((), ()))
TN = (((0,), (0,)), ((), ()))


def table(rows, cols):
    return np.zeros((rows, cols), np.float32)


def one_hot_tables():
    perm = table(108, 640)
    for kd in range(3):
        for kh in range(3):
            for kw in range(3):
                for c in range(4):
                    row = ((kd * 3 + kh) * 3 + kw) * 4 + c
                    perm[row, ((kd * 3 + kw) * 4 + c) * 16 + kh] = 0.5
    shift = table(128, 256)
    for w in range(128):
        if w >= 1:
            shift[w - 1, w] = 1.0
        if w + 1 < 128:
            shift[w + 1, 128 + w] = 1.0
    pair = table(256, 128)
    for a in range(2):
        for w in range(64):
            pair[128 * a + 2 * w, 64 * a + w] = 1.0
    squeeze = table(512, 128)
    spread = table(128, 1152)
    grow_g = table(96, 768)
    grow2 = table(128, 512)
    for h in range(4):
        for w in range(32):
            squeeze[128 * h + 2 * w, 32 * h + w] = 1.0
            for kh in range(3):
                for kw in range(3):
                    if 0 <= h + kh - 1 < 4 and 0 <= w + kw - 1 < 32:
                        src = 32 * (h + kh - 1) + w + kw - 1
                        spread[src, 128 * (3 * kh + kw) + 32 * h + w] = 1.0
            for n in range(6):
                src = 32 * (n // 2) + 16 * (h // 2) + w // 2
                grow_g[src, 128 * n + 32 * h + w] = 1.0 / 16
            for d in range(2):
                for u in range(2):
                    grow2[32 * h + w, 128 * h + 64 * d + 2 * w + u] = 1.0 / 16
    grow1 = table(256, 512)
    for e in range(4):
        for w in range(128):
            grow1[64 * e + w // 2, 128 * e + w] = 1.0 / 16
    return [perm, shift, pair, squeeze, spread, grow_g, grow2, grow1]


def dot(a, b):
    return jnp.dot(a, b, preferred_element_type=F32)


def inside(index, count):
    return jnp.logical_and(index >= 0, index < count)


def position():
    return lax.axis_index("space"), lax.axis_size("space")


def taps_of(it):
    kd, kw = (it // 3, it % 3)
    return [kd * 9 + kh * 3 + kw for kh in range(3)]


def taps_back(it):
    kd, kw = (2 - it // 3, 2 - it % 3)
    return [kd * 9 + (2 - kh) * 3 + kw for kh in range(3)]


def build(filter_two, t2, t2r):
    for it in range(9):
        v2 = [filter_two[k].astype(F32) for k in taps_back(it)]
        zero = jnp.zeros((32, 64), F32)
        for s in range(-6, 8):
            if -1 <= s <= 2:
                parts = [v2[s + j] if 0 <= s + j <= 2 else zero for j in range(2)]
                tile = jnp.concatenate(parts, axis=1).astype(BF)
            else:
                tile = jnp.zeros((32, 128), BF)
            for m in range(4):
                hp = 2 * m + 1 - s
                if 0 <= hp < 8:
                    t2r[32 * hp : 32 * hp + 32, it * 512 + 128 * m : it * 512 + 128 * m + 128] = tile
    taps = []
    for kh in range(3):
        rows = jnp.concatenate([filter_two[taps_of(it)[kh]] for it in range(9)], axis=0)
        taps.append(rows.astype(F32).T * 0.5)
    zero = jnp.zeros((64, 288), F32)
    for s in range(5):
        parts = [taps[p - s + 1] if 0 <= p - s + 1 < 3 else zero for p in range(5)]
        t2[64 * s : 64 * s + 64, :] = jnp.concatenate(parts, axis=1).astype(BF)


def body(
    vol_own,
    grad_own,
    swap_core,
    swap_chip,
    swap_chip2,
    swap_core2,
    filter_one,
    filter_three,
    t2,
    t2r,
    perm,
    shift,
    pair,
    squeeze,
    spread,
    grow_g,
    grow2,
    grow1,
    kept,
    sent,
    t1,
    w3t,
    x1,
    pp,
    x2,
    q,
    x3,
    d2c,
    sl1,
    sl2,
    d2,
    d1,
    out,
):
    me, blocks = position()
    first_core = me % 2 == 0
    lane = lax.broadcasted_iota(jnp.int32, (32, 640), 1) % 16
    rows = filter_one[...].astype(F32).reshape(108, 32).astype(BF)
    base = lax.dot_general(rows, perm[...], TN, preferred_element_type=F32)
    for h in range(16):
        moved = pltpu.roll(base, (h - 1) % 640, 1) if h != 1 else base
        if h == 0:
            moved = jnp.where(lane == 15, 0.0, moved)
        if h == 15:
            moved = jnp.where(lane == 0, 0.0, moved)
        t1[32 * h : 32 * h + 32, :] = moved[:, :576].astype(BF)
    w3t[...] = (filter_three[...].astype(F32).T * 0.5).astype(BF)

    def either(a, b, lo, hi):
        return jnp.where(first_core, a[lo:hi, :], b[lo:hi, :])

    at = 0
    for rows in (
        either(swap_chip2, swap_core2, 0, 448),
        either(swap_chip, swap_core, 0, 512),
        vol_own[...],
        either(swap_core, swap_chip, 0, 512),
        either(swap_core2, swap_chip2, 0, 448),
    ):
        moved = dot(rows, shift[...]).astype(BF)
        count = rows.shape[0] // 64
        for p in range(count):
            lanes = slice(128 * (at + p), 128 * (at + p) + 128)
            x1[0:64, lanes] = moved[64 * p : 64 * p + 64, :128]
            x1[64:128, lanes] = rows[64 * p : 64 * p + 64, :]
            x1[128:192, lanes] = moved[64 * p : 64 * p + 64, 128:]
        at += count

    for j in range(18):
        rhs = jnp.concatenate(
            [x1[:, (2 * j + kd) * 128 : (2 * j + kd) * 128 + 256] for kd in range(3)], axis=0
        )
        half = dot(t1[...], rhs)
        t = jnp.tanh(half)
        if 7 <= j < 11:
            slope = (1.0 + t) + half * (1.0 - t * t)
            sl1[:, (j - 7) * 256 : (j - 7) * 256 + 256] = slope.astype(BF)
        act = half + half * t
        act = act[:, :128] + act[:, 128:]
        act = act.reshape(8, 2, 32, 128)
        act = (act[:, 0] + act[:, 1]).reshape(256, 128)
        act = act + pltpu.roll(act, 127, 1)
        scale = jnp.where(inside(4 * me - 7 + j, 4 * blocks), 0.125, 0.0)
        pp[:, j * 128 : j * 128 + 128] = (act * scale).astype(BF)

    col64 = lax.broadcasted_iota(jnp.int32, (256, 128), 1) % 64
    first_col, last_col = (col64 == 0, col64 == 63)
    for first in range(17):
        got = dot(pp[:, first * 128 : first * 128 + 256], pair[...])
        moved = (
            jnp.where(first_col, 0.0, pltpu.roll(got, 1, 1)).astype(BF),
            got.astype(BF),
            jnp.where(last_col, 0.0, pltpu.roll(got, 127, 1)).astype(BF),
        )
        for kd in range(3):
            m = (first - kd) // 2
            if (first - kd) % 2 == 0 and 0 <= m < 8:
                for kw in range(3):
                    k = 3 * kd + kw
                    x2[256 * k : 256 * k + 256, m * 128 : m * 128 + 128] = moved[kw]

    for c in range(4):
        lanes = slice(c * 256, c * 256 + 256)
        for g in range(2):
            rhs = jnp.concatenate(
                [
                    x2[256 * it + 32 * p : 256 * it + 32 * p + 32, lanes]
                    for p in range(3 * g, 3 * g + 5)
                    for it in range(9)
                ],
                axis=0,
            )
            half = dot(t2[64 * g : 64 * g + 256, :], rhs)
            t = jnp.tanh(half)
            if 1 <= c < 3:
                slope = (1.0 + t) + half * (1.0 - t * t)
                sl2[256 * g : 256 * g + 256, c * 256 - 256 : c * 256] = slope.astype(BF)
            act = (half + half * t).reshape(2, 2, 64, 256)
            act = (act[:, 0] + act[:, 1]).reshape(128, 256)
            for u in range(2):
                tile = act[:, 128 * u : 128 * u + 128]
                tile = tile + pltpu.roll(tile, 64, 1)
                tile = tile + pltpu.roll(tile, 127, 1)
                m = 2 * c + u
                scale = jnp.where(inside(2 * me - 3 + m, 2 * blocks), 0.125, 0.0)
                tile = (tile * scale).astype(BF)
                for h in range(2):
                    lo = 128 * (2 * g + h)
                    q[64 * m : 64 * m + 64, lo : lo + 128] = tile[64 * h : 64 * h + 64, :]

    packed = dot(q[...], squeeze[...]).astype(BF)
    got = dot(packed, spread[...]).astype(BF)
    for kd in range(3):
        for s in range(9):
            k = 9 * kd + s
            for n in range(6):
                x3[64 * k : 64 * k + 64, 128 * n : 128 * n + 128] = got[
                    64 * (n + kd) : 64 * (n + kd) + 64, 128 * s : 128 * s + 128
                ]
    rows = jnp.concatenate(
        [
            either(swap_chip2, swap_core2, 448, 480),
            grad_own[...],
            either(swap_core2, swap_chip2, 448, 480),
        ],
        axis=0,
    )
    grown = dot(rows.astype(F32).T.astype(BF), grow_g[...])
    half = dot(w3t[...], x3[...])
    t = jnp.tanh(half)
    d3 = (grown * ((1.0 + t) + half * (1.0 - t * t))).astype(BF)

    out[:G_TWO, :] = lax.dot_general(
        x3[:, 256:512], d3[:, 256:512], NT, preferred_element_type=F32
    ).astype(BF)

    lane = lax.broadcasted_iota(jnp.int32, (64, 128), 1)
    col, line = (lane % 32, lane // 32)
    masks = []
    for b in range(3):
        for c in range(3):
            keep = inside(col + 1 - c, 32)
            masks.append(jnp.logical_and(keep, inside(line + 1 - b, 4)))
    lhs = jnp.concatenate([filter_three[576 * a : 576 * a + 576, :] for a in range(3)], axis=1)
    grown = []
    for pair_at in range(2):
        rhs = jnp.concatenate(
            [
                d3[:, 128 * (2 * pair_at + 2 - a) : 128 * (2 * pair_at + 2 - a) + 256]
                for a in range(3)
            ],
            axis=0,
        )
        got = dot(lhs, rhs)
        for u in range(2):
            total = None
            for b in range(3):
                for c in range(3):
                    s = 3 * b + c
                    part = got[64 * s : 64 * s + 64, 128 * u : 128 * u + 128]
                    move_by = -(32 * (1 - b) + 1 - c) % 128
                    if move_by:
                        part = jnp.where(masks[s], pltpu.roll(part, move_by, 1), 0.0)
                    total = part if total is None else total + part
            n = 2 * pair_at + u
            scale = jnp.where(inside(2 * me - 1 + n, 2 * blocks), 1.0, 0.0)
            grown.append((total * scale).astype(BF))
    back = dot(jnp.concatenate(grown, axis=0), grow2[...])
    for h in range(8):
        rows = slice(64 * h, 64 * h + 64)
        for n in range(4):
            lanes = slice(128 * n, 128 * n + 128)
            source = back[64 * n : 64 * n + 64, 128 * (h // 2) : 128 * (h // 2) + 128]
            d2[rows, lanes] = (source * sl2[rows, lanes].astype(F32)).astype(BF)

    for part in range(2):
        rows = slice(256 * part, 256 * part + 256)
        for start in range(1, 6):
            u = start // 2
            got = d2[rows, 128 * u : 128 * u + 128].astype(F32)
            if start % 2:
                after = d2[rows, 128 * u + 128 : 128 * u + 256].astype(F32)
                lane = lax.broadcasted_iota(jnp.int32, (256, 128), 1)
                got = jnp.where(lane < 64, pltpu.roll(got, 64, 1), pltpu.roll(after, 64, 1))
            moved = (
                jnp.where(first_col, 0.0, pltpu.roll(got, 1, 1)).astype(BF),
                got.astype(BF),
                jnp.where(last_col, 0.0, pltpu.roll(got, 127, 1)).astype(BF),
            )
            for kd in range(3):
                for m in range(2):
                    if 1 + kd + 2 * m == start:
                        for kw in range(3):
                            lo = 512 * (3 * kd + kw) + 256 * part
                            d2c[lo : lo + 256, 128 * m : 128 * m + 128] = moved[kw]
    back = dot(t2r[...], d2c[...]).astype(BF)
    back = dot(back, grow1[...])
    for h in range(16):
        rows = slice(32 * h, 32 * h + 32)
        source = back[32 * (h // 2) : 32 * (h // 2) + 32, :]
        for e in range(8):
            lanes = slice(128 * e, 128 * e + 128)
            delta = source[:, 128 * (e // 2) : 128 * (e // 2) + 128] * sl1[rows, lanes].astype(F32)
            d1[rows, lanes] = delta.astype(BF)

    lane16 = lax.broadcasted_iota(jnp.int32, (16, 128), 1)
    all_two = lax.dot_general(
        x2[:, 384:640], d2[:, 128:384], NT, preferred_element_type=F32
    )
    for it in range(9):
        got = all_two[256 * it : 256 * it + 256, :]
        for kh, k in enumerate(taps_of(it)):
            totals = [None, None]
            for h in range(8):
                hp = h + kh - 1
                if 0 <= hp < 8:
                    part = got[32 * hp : 32 * hp + 32, 128 * (h // 2) : 128 * (h // 2) + 128]
                    now = totals[h % 2]
                    totals[h % 2] = part if now is None else now + part
            low = totals[0] + pltpu.roll(totals[1], 64, 1)
            high = pltpu.roll(totals[0], 64, 1) + totals[1]
            out[G_TWO + k * 16 : G_TWO + k * 16 + 16, :] = jnp.where(
                lane16 < 64, low[:16], high[16:]
            ).astype(BF)

    lhs = jnp.concatenate([x1[:, 128 * (14 + kd) : 128 * (14 + kd) + 1024] for kd in range(3)], axis=0)
    got = lax.dot_general(lhs, d1[...], NT, preferred_element_type=F32)
    row = lax.broadcasted_iota(jnp.int32, (576, 128), 0) % 16
    col = lax.broadcasted_iota(jnp.int32, (576, 128), 1) // 32
    lane36 = lax.broadcasted_iota(jnp.int32, (36, 128), 1)
    packed = jnp.zeros((36, 128), F32)
    for kh in range(3):
        total = jnp.zeros((576, 128), F32)
        for u in range(4):
            keep = row == col + (4 * u + kh - 1)
            total = total + jnp.where(keep, got[:, 128 * u : 128 * u + 128], 0.0)
        total = total.reshape(36, 16, 128).sum(axis=1)
        total = total + pltpu.roll(total, 64, 1)
        total = total + pltpu.roll(total, 32, 1)
        packed = packed + jnp.where(lane36 // 32 == kh, total, 0.0)
    out[G_ONE : G_ONE + 48, :] = jnp.concatenate(
        [packed, jnp.zeros((12, 128), F32)], axis=0
    ).astype(BF)
    out[G_ONE + 48 :, :] = jnp.zeros((out.shape[0] - G_ONE - 48, 128), BF)
    half_rows = kept.shape[0]
    mine = pl.multiple_of(me % 2 * half_rows, half_rows)
    kept[...] = out[pl.ds(mine, half_rows), :]
    sent[...] = out[pl.ds(half_rows - mine, half_rows), :]


def finish(scales, mine, other, one_far, two_far, three_far, one, two, three, sems):
    first_core = position()[0] % 2 == 0
    half_rows = mine.shape[0]

    def rows(at, count):
        parts = []
        while count:
            use = min(count, half_rows - at % half_rows)
            here = slice(at % half_rows, at % half_rows + use)
            flag = first_core if at < half_rows else jnp.logical_not(first_core)
            parts.append(jnp.where(flag, mine[here, :], other[here, :]).astype(F32))
            at, count = (at + use, count - use)
        return parts[0] if len(parts) == 1 else jnp.concatenate(parts, axis=0)

    copies = []

    def leave(near_ref, far_ref):
        copies.append(pltpu.make_async_copy(near_ref, far_ref, sems.at[len(copies)]))
        copies[-1].start()

    for k in range(27):
        got = rows(G_TWO + 16 * k, 16) * scales[1]
        two[k, 0:16, :] = got[:, :64]
        two[k, 16:32, :] = got[:, 64:]
    leave(two, two_far)
    got = rows(G_ONE, 48) * scales[0]
    for it in range(9):
        for kh, k in enumerate(taps_of(it)):
            one[k] = got[4 * it : 4 * it + 4, 32 * kh : 32 * kh + 32]
    leave(one, one_far)
    for third in range(3):
        for k in range(9 * third, 9 * third + 9):
            three[k] = rows(64 * k, 64) * scales[2]
        here = slice(9 * third, 9 * third + 9)
        leave(three.at[here], three_far.at[here])
    for copy in copies:
        copy.wait()


VMEM = pl.BlockSpec(memory_space=pltpu.VMEM)


def near(*shape):
    return pltpu.VMEM(shape, BF)


FAR = pl.BlockSpec(memory_space=pl.ANY)
BANDED = ((320, 1440), (256, 4608))


def run_build(filter_two):
    return pl.pallas_call(
        build,
        out_shape=[jax.ShapeDtypeStruct(shape, BF) for shape in BANDED],
        in_specs=[VMEM],
        out_specs=[VMEM] * 2,
        compiler_params=pltpu.CompilerParams(vmem_limit_bytes=16 * 1024 * 1024),
        cost_estimate=pl.CostEstimate(flops=10**9, bytes_accessed=6 * 10**6, transcendentals=0),
        name="build",
    )(filter_two)


def local_grads(volume, grad, swaps, filter_one, filter_three, banded, rows):
    tables = [jnp.asarray(t, BF) for t in one_hot_tables()]
    args = [volume, grad, *swaps, filter_one, filter_three, *banded, *tables]
    return pl.pallas_call(
        body,
        out_shape=[jax.ShapeDtypeStruct((rows // 2, 128), BF)] * 2,
        in_specs=[VMEM] * len(args),
        out_specs=[VMEM] * 2,
        scratch_shapes=[
            near(512, 576),
            near(128, 1728),
            near(192, 38 * 128),
            near(256, 18 * 128),
            near(2304, 1024),
            near(512, 512),
            near(1728, 768),
            near(4608, 256),
            near(512, 1024),
            near(512, 512),
            near(512, 512),
            near(512, 1024),
            near(rows, 128),
        ],
        compiler_params=pltpu.CompilerParams(vmem_limit_bytes=LIMIT * 1024 * 1024),
        cost_estimate=pl.CostEstimate(flops=10**10, bytes_accessed=10**7, transcendentals=0),
        name="local_grads",
    )(*args)


def run_finish(mine, other, cells):
    scales = [float(1.0 / np.sqrt(cells / size)) for size in (1.0, 8.0, 64.0)]
    shapes = [(27, 4, 32), (27, 32, 64), (27, 64, 128)]
    outs = pl.pallas_call(
        functools.partial(finish, scales),
        out_shape=[jax.ShapeDtypeStruct(shape, F32) for shape in shapes],
        in_specs=[VMEM] * 2,
        out_specs=[FAR] * 3,
        scratch_shapes=[pltpu.VMEM(shape, F32) for shape in shapes]
        + [pltpu.SemaphoreType.DMA((5,))],
        compiler_params=pltpu.CompilerParams(vmem_limit_bytes=8 * 1024 * 1024),
        name="finish",
    )(mine, other)
    return tuple(o.reshape(3, 3, 3, *o.shape[1:]) for o in outs)


def over_sample(pieces):
    return lax.all_to_all(pieces, "sample", 0, 0, tiled=True)


def over_chips(pieces):
    size = lax.axis_size("space")
    groups = [list(range(core, size, 2)) for core in range(2)]
    return lax.all_to_all(pieces, "space", 0, 0, axis_index_groups=groups, tiled=True)


def total_of(got):
    return got.astype(F32).sum(axis=0).astype(BF)


def swap(values, first):
    size = lax.axis_size("space")
    pairs = [(i, i + 1) for i in range(first, size - 1, 2)]
    return lax.ppermute(values, "space", pairs + [(j, i) for i, j in pairs])


def per_device(volume, grad_out, filter_one, filter_two, filter_three):
    spaces, samples = (lax.axis_size("space"), lax.axis_size("sample"))
    own = volume.reshape(512, 128)
    grad = grad_out.reshape(32, 128)
    f1 = filter_one.reshape(27, 4, 32)
    f2 = filter_two.reshape(27, 32, 64)
    f3 = filter_three.reshape(1728, 128)
    core = lax.axis_index("space") % 2

    def second(block, flip=0):
        planes = lax.dynamic_slice(block, (64 * (core ^ flip), 0), (448, 128))
        return jnp.concatenate([planes, grad], axis=0)

    swap_core = swap(own, 0)
    swap_chip = swap(own, 1)
    relay = second(swap_core)
    swap_chip2 = swap(relay, 1)
    f2_later = lax.optimization_barrier((f2, relay))[0]
    banded = run_build(f2_later)
    swap_chip, *banded = lax.optimization_barrier((swap_chip, *banded))
    swap_core2 = swap(second(swap_chip, 1), 0)
    chips = spaces // 2
    keep, send = local_grads(
        own,
        grad,
        (swap_core, swap_chip, swap_chip2, swap_core2),
        f1,
        f3,
        banded,
        spaces * SLOT,
    )
    half = (keep.astype(F32) + swap(send, 0).astype(F32)).astype(BF)
    part = total_of(over_chips(half.reshape(chips, SLOT, 128)))
    part = total_of(over_sample(jnp.broadcast_to(part[None], (samples, SLOT, 128))))
    mine = over_chips(jnp.broadcast_to(part[None], (chips, SLOT, 128))).reshape(-1, 128)
    cells = float(samples * spaces * volume.shape[1] * volume.shape[3] * volume.shape[4])
    return run_finish(mine, swap(mine, 0), cells)


def solution(mesh):
    return jax.shard_map(
        per_device,
        mesh=mesh,
        in_specs=(
            P(("sample", "space"), None, None, None, None),
            P(("sample", "space"), None, None, None, None),
            P(),
            P(),
            P(),
        ),
        out_specs=(P(), P(), P()),
        check_vma=False,
    )
```

```python
import functools

import jax
import jax.numpy as jnp
import numpy as np
from jax import lax
from jax.experimental import pallas as pl
from jax.experimental.pallas import tpu as pltpu
from jax.sharding import PartitionSpec as P

BF = jnp.bfloat16
F32 = jnp.float32
SLOT = 72
LIMIT = 44
G_TWO = 1728
G_ONE = 2160
NT = (((1,), (1,)), ((), ()))
TN = (((0,), (0,)), ((), ()))


def table(rows, cols):
    return np.zeros((rows, cols), np.float32)


def one_hot_tables():
    pair = table(256, 128)
    for a in range(2):
        for w in range(64):
            pair[128 * a + 2 * w, 64 * a + w] = 1.0
    squeeze = table(512, 128)
    spread = table(128, 1152)
    grow_g = table(96, 768)
    grow2 = table(128, 512)
    for h in range(4):
        for w in range(32):
            squeeze[128 * h + 2 * w, 32 * h + w] = 1.0
            for kh in range(3):
                for kw in range(3):
                    if 0 <= h + kh - 1 < 4 and 0 <= w + kw - 1 < 32:
                        src = 32 * (h + kh - 1) + w + kw - 1
                        spread[src, 128 * (3 * kh + kw) + 32 * h + w] = 1.0
            for n in range(6):
                src = 32 * (n // 2) + 16 * (h // 2) + w // 2
                grow_g[src, 128 * n + 32 * h + w] = 1.0 / 16
            for d in range(2):
                for u in range(2):
                    grow2[32 * h + w, 128 * h + 64 * d + 2 * w + u] = 1.0 / 16
    grow1 = table(256, 512)
    for e in range(4):
        for w in range(128):
            grow1[64 * e + w // 2, 128 * e + w] = 1.0 / 16
    return [pair, squeeze, spread, grow_g, grow2, grow1]


def dot(a, b):
    return jnp.dot(a, b, preferred_element_type=F32)


def inside(index, count):
    return jnp.logical_and(index >= 0, index < count)


def position():
    return lax.axis_index("space"), lax.axis_size("space")


def taps_of(it):
    kd, kw = (it // 3, it % 3)
    return [kd * 9 + kh * 3 + kw for kh in range(3)]


def taps_back(it):
    kd, kw = (2 - it // 3, 2 - it % 3)
    return [kd * 9 + (2 - kh) * 3 + kw for kh in range(3)]


def band_one(filter_one, t1):
    lane = lax.broadcasted_iota(jnp.int32, (32, 640), 1) % 16
    rows = filter_one[...].astype(F32).reshape(108, 32).astype(BF)
    at = lax.broadcasted_iota(jnp.int32, (108, 640), 1)
    kd = (at >= 192).astype(jnp.int32) + (at >= 384).astype(jnp.int32)
    rest = at - 192 * kd
    kw = (rest >= 64).astype(jnp.int32) + (rest >= 128).astype(jnp.int32)
    c = (rest - 64 * kw) // 16
    kh = rest % 16
    place = 36 * kd + 12 * kh + 4 * kw + c
    here = lax.broadcasted_iota(jnp.int32, (108, 640), 0) == place
    here = jnp.logical_and(here, jnp.logical_and(kh < 3, at < 576))
    perm = jnp.where(here, 0.5, 0.0).astype(BF)
    base = lax.dot_general(rows, perm, TN, preferred_element_type=F32)
    for h in range(16):
        moved = pltpu.roll(base, (h - 1) % 640, 1) if h != 1 else base
        if h == 0:
            moved = jnp.where(lane == 15, 0.0, moved)
        if h == 15:
            moved = jnp.where(lane == 0, 0.0, moved)
        t1[32 * h : 32 * h + 32, :] = moved[:, :576].astype(BF)


def band_two(filter_two, t2):
    taps = []
    for kh in range(3):
        rows = jnp.concatenate([filter_two[taps_of(it)[kh]] for it in range(9)], axis=0)
        taps.append(rows.astype(F32).T * 0.5)
    zero = jnp.zeros((64, 288), F32)
    for s in range(5):
        parts = [taps[p - s + 1] if 0 <= p - s + 1 < 3 else zero for p in range(5)]
        t2[64 * s : 64 * s + 64, :] = jnp.concatenate(parts, axis=1).astype(BF)


def band_two_back(filter_two, t2r):
    for it in range(9):
        v2 = [filter_two[k].astype(F32) for k in taps_back(it)]
        zero = jnp.zeros((32, 64), F32)
        for s in range(-6, 8):
            if -1 <= s <= 2:
                parts = [v2[s + j] if 0 <= s + j <= 2 else zero for j in range(2)]
                tile = jnp.concatenate(parts, axis=1).astype(BF)
            else:
                tile = jnp.zeros((32, 128), BF)
            for m in range(4):
                hp = 2 * m + 1 - s
                if 0 <= hp < 8:
                    t2r[32 * hp : 32 * hp + 32, it * 512 + 128 * m : it * 512 + 128 * m + 128] = tile


def with_column_shifts(rows, x1, at):
    lane = lax.broadcasted_iota(jnp.int32, (64, 128), 1)
    for p in range(rows.shape[0] // 64):
        lanes = slice(128 * (at + p), 128 * (at + p) + 128)
        plane = rows[64 * p : 64 * p + 64, :]
        wide = plane.astype(F32)
        x1[0:64, lanes] = jnp.where(lane == 0, 0.0, pltpu.roll(wide, 1, 1)).astype(BF)
        x1[64:128, lanes] = plane
        x1[128:192, lanes] = jnp.where(lane == 127, 0.0, pltpu.roll(wide, 127, 1)).astype(BF)
    return at + rows.shape[0] // 64


def layer_one(t1, x1, at, scale):
    rhs = jnp.concatenate(
        [x1[:, 128 * (at + kd) : 128 * (at + kd) + 256] for kd in range(3)], axis=0
    )
    half = dot(t1[...], rhs)
    t = jnp.tanh(half)
    act = half + half * t
    act = act[:, :128] + act[:, 128:]
    act = act.reshape(8, 2, 32, 128)
    act = (act[:, 0] + act[:, 1]).reshape(256, 128)
    act = act + pltpu.roll(act, 127, 1)
    return half, t, (act * scale).astype(BF)


def either_of(first_core):
    def either(a, b, lo, hi):
        return jnp.where(first_core, a[lo:hi, :], b[lo:hi, :])

    return either


def near_part(
    vol_own,
    swap_core,
    swap_chip,
    filter_one,
    filter_two,
    t1,
    t2,
    t2r,
    x1_own,
    pp,
    sl1,
    x1,
):
    me, blocks = position()
    either = either_of(me % 2 == 0)
    band_two_back(filter_two, t2r)
    band_two(filter_two, t2)
    band_one(filter_one, t1)
    at = with_column_shifts(either(swap_chip, swap_core, 64, 512), x1, 0)
    at = with_column_shifts(vol_own[...], x1, at)
    at = with_column_shifts(either(swap_core, swap_chip, 0, 448), x1, at)
    x1_own[...] = x1[:, 768:2048]
    for j in range(10):
        scale = jnp.where(inside(4 * me - 3 + j, 4 * blocks), 0.125, 0.0)
        half, t, act = layer_one(t1, x1, 2 * j, scale)
        if 3 <= j < 7:
            slope = (1.0 + t) + half * (1.0 - t * t)
            sl1[:, 256 * (j - 3) : 256 * (j - 3) + 256] = slope.astype(BF)
        pp[:, 128 * j : 128 * j + 128] = act


def body(
    swap_core,
    swap_chip,
    swap_chip2,
    swap_core2,
    grad_own,
    filter_three,
    t1,
    t2,
    t2r,
    x1,
    pp_near,
    sl1,
    pair,
    squeeze,
    spread,
    grow_g,
    grow2,
    grow1,
    kept,
    sent,
    w3t,
    pp,
    xo,
    x2,
    q,
    x3,
    d2c,
    sl2,
    d2,
    d1,
    out,
):
    me, blocks = position()
    either = either_of(me % 2 == 0)
    w3t[...] = (filter_three[...].astype(F32).T * 0.5).astype(BF)

    at = with_column_shifts(either(swap_chip2, swap_core2, 0, 448), xo, 0)
    at = with_column_shifts(either(swap_chip, swap_core, 0, 192), xo, at)
    at = with_column_shifts(either(swap_core, swap_chip, 320, 512), xo, at)
    at = with_column_shifts(either(swap_core2, swap_chip2, 0, 448), xo, at)
    for j in (0, 1, 2, 3, 14, 15, 16, 17):
        scale = jnp.where(inside(4 * me - 7 + j, 4 * blocks), 0.125, 0.0)
        act = layer_one(t1, xo, 2 * j if j < 4 else 10 + 2 * (j - 14), scale)[2]
        lo = 128 * (j if j < 4 else j - 10)
        pp[:, lo : lo + 128] = act

    def pooled_plane(j):
        if 4 <= j < 14:
            return pp_near[:, 128 * (j - 4) : 128 * (j - 4) + 128]
        lo = 128 * (j if j < 4 else j - 10)
        return pp[:, lo : lo + 128]

    col64 = lax.broadcasted_iota(jnp.int32, (256, 128), 1) % 64
    first_col, last_col = (col64 == 0, col64 == 63)
    for first in range(17):
        both = jnp.concatenate([pooled_plane(first), pooled_plane(first + 1)], axis=1)
        got = dot(both, pair[...])
        moved = (
            jnp.where(first_col, 0.0, pltpu.roll(got, 1, 1)).astype(BF),
            got.astype(BF),
            jnp.where(last_col, 0.0, pltpu.roll(got, 127, 1)).astype(BF),
        )
        for kd in range(3):
            m = (first - kd) // 2
            if (first - kd) % 2 == 0 and 0 <= m < 8:
                for kw in range(3):
                    k = 3 * kd + kw
                    x2[256 * k : 256 * k + 256, m * 128 : m * 128 + 128] = moved[kw]

    for c in range(4):
        lanes = slice(c * 256, c * 256 + 256)
        for g in range(2):
            rhs = jnp.concatenate(
                [
                    x2[256 * it + 32 * p : 256 * it + 32 * p + 32, lanes]
                    for p in range(3 * g, 3 * g + 5)
                    for it in range(9)
                ],
                axis=0,
            )
            half = dot(t2[64 * g : 64 * g + 256, :], rhs)
            t = jnp.tanh(half)
            if 1 <= c < 3:
                slope = (1.0 + t) + half * (1.0 - t * t)
                sl2[256 * g : 256 * g + 256, c * 256 - 256 : c * 256] = slope.astype(BF)
            act = (half + half * t).reshape(2, 2, 64, 256)
            act = (act[:, 0] + act[:, 1]).reshape(128, 256)
            for u in range(2):
                tile = act[:, 128 * u : 128 * u + 128]
                tile = tile + pltpu.roll(tile, 64, 1)
                tile = tile + pltpu.roll(tile, 127, 1)
                m = 2 * c + u
                scale = jnp.where(inside(2 * me - 3 + m, 2 * blocks), 0.125, 0.0)
                tile = (tile * scale).astype(BF)
                for h in range(2):
                    lo = 128 * (2 * g + h)
                    q[64 * m : 64 * m + 64, lo : lo + 128] = tile[64 * h : 64 * h + 64, :]

    packed = dot(q[...], squeeze[...]).astype(BF)
    got = dot(packed, spread[...]).astype(BF)
    for kd in range(3):
        for s in range(9):
            k = 9 * kd + s
            for n in range(6):
                x3[64 * k : 64 * k + 64, 128 * n : 128 * n + 128] = got[
                    64 * (n + kd) : 64 * (n + kd) + 64, 128 * s : 128 * s + 128
                ]
    rows = jnp.concatenate(
        [
            either(swap_chip2, swap_core2, 448, 480),
            grad_own[...],
            either(swap_core2, swap_chip2, 448, 480),
        ],
        axis=0,
    )
    grown = dot(rows.astype(F32).T.astype(BF), grow_g[...])
    half = dot(w3t[...], x3[...])
    t = jnp.tanh(half)
    d3 = (grown * ((1.0 + t) + half * (1.0 - t * t))).astype(BF)

    out[:G_TWO, :] = lax.dot_general(
        x3[:, 256:512], d3[:, 256:512], NT, preferred_element_type=F32
    ).astype(BF)

    lane = lax.broadcasted_iota(jnp.int32, (64, 128), 1)
    col, line = (lane % 32, lane // 32)
    masks = []
    for b in range(3):
        for c in range(3):
            keep = inside(col + 1 - c, 32)
            masks.append(jnp.logical_and(keep, inside(line + 1 - b, 4)))
    lhs = jnp.concatenate([filter_three[576 * a : 576 * a + 576, :] for a in range(3)], axis=1)
    grown = []
    for pair_at in range(2):
        rhs = jnp.concatenate(
            [
                d3[:, 128 * (2 * pair_at + 2 - a) : 128 * (2 * pair_at + 2 - a) + 256]
                for a in range(3)
            ],
            axis=0,
        )
        got = dot(lhs, rhs)
        for u in range(2):
            total = None
            for b in range(3):
                for c in range(3):
                    s = 3 * b + c
                    part = got[64 * s : 64 * s + 64, 128 * u : 128 * u + 128]
                    move_by = -(32 * (1 - b) + 1 - c) % 128
                    if move_by:
                        part = jnp.where(masks[s], pltpu.roll(part, move_by, 1), 0.0)
                    total = part if total is None else total + part
            n = 2 * pair_at + u
            scale = jnp.where(inside(2 * me - 1 + n, 2 * blocks), 1.0, 0.0)
            grown.append((total * scale).astype(BF))
    back = dot(jnp.concatenate(grown, axis=0), grow2[...])
    for h in range(8):
        rows = slice(64 * h, 64 * h + 64)
        for n in range(4):
            lanes = slice(128 * n, 128 * n + 128)
            source = back[64 * n : 64 * n + 64, 128 * (h // 2) : 128 * (h // 2) + 128]
            d2[rows, lanes] = (source * sl2[rows, lanes].astype(F32)).astype(BF)

    for part in range(2):
        rows = slice(256 * part, 256 * part + 256)
        for start in range(1, 6):
            u = start // 2
            got = d2[rows, 128 * u : 128 * u + 128].astype(F32)
            if start % 2:
                after = d2[rows, 128 * u + 128 : 128 * u + 256].astype(F32)
                lane = lax.broadcasted_iota(jnp.int32, (256, 128), 1)
                got = jnp.where(lane < 64, pltpu.roll(got, 64, 1), pltpu.roll(after, 64, 1))
            moved = (
                jnp.where(first_col, 0.0, pltpu.roll(got, 1, 1)).astype(BF),
                got.astype(BF),
                jnp.where(last_col, 0.0, pltpu.roll(got, 127, 1)).astype(BF),
            )
            for kd in range(3):
                for m in range(2):
                    if 1 + kd + 2 * m == start:
                        for kw in range(3):
                            lo = 512 * (3 * kd + kw) + 256 * part
                            d2c[lo : lo + 256, 128 * m : 128 * m + 128] = moved[kw]
    back = dot(t2r[...], d2c[...]).astype(BF)
    back = dot(back, grow1[...])
    for h in range(16):
        rows = slice(32 * h, 32 * h + 32)
        source = back[32 * (h // 2) : 32 * (h // 2) + 32, :]
        for e in range(8):
            lanes = slice(128 * e, 128 * e + 128)
            delta = source[:, 128 * (e // 2) : 128 * (e // 2) + 128] * sl1[rows, lanes].astype(F32)
            d1[rows, lanes] = delta.astype(BF)

    lane16 = lax.broadcasted_iota(jnp.int32, (16, 128), 1)
    all_two = lax.dot_general(
        x2[:, 384:640], d2[:, 128:384], NT, preferred_element_type=F32
    )
    for it in range(9):
        got = all_two[256 * it : 256 * it + 256, :]
        for kh, k in enumerate(taps_of(it)):
            totals = [None, None]
            for h in range(8):
                hp = h + kh - 1
                if 0 <= hp < 8:
                    part = got[32 * hp : 32 * hp + 32, 128 * (h // 2) : 128 * (h // 2) + 128]
                    now = totals[h % 2]
                    totals[h % 2] = part if now is None else now + part
            low = totals[0] + pltpu.roll(totals[1], 64, 1)
            high = pltpu.roll(totals[0], 64, 1) + totals[1]
            out[G_TWO + k * 16 : G_TWO + k * 16 + 16, :] = jnp.where(
                lane16 < 64, low[:16], high[16:]
            ).astype(BF)

    lhs = jnp.concatenate([x1[:, 128 * kd : 128 * kd + 1024] for kd in range(3)], axis=0)
    got = lax.dot_general(lhs, d1[...], NT, preferred_element_type=F32)
    row = lax.broadcasted_iota(jnp.int32, (576, 128), 0) % 16
    col = lax.broadcasted_iota(jnp.int32, (576, 128), 1) // 32
    lane36 = lax.broadcasted_iota(jnp.int32, (36, 128), 1)
    packed = jnp.zeros((36, 128), F32)
    for kh in range(3):
        total = jnp.zeros((576, 128), F32)
        for u in range(4):
            keep = row == col + (4 * u + kh - 1)
            total = total + jnp.where(keep, got[:, 128 * u : 128 * u + 128], 0.0)
        total = total.reshape(36, 16, 128).sum(axis=1)
        total = total + pltpu.roll(total, 64, 1)
        total = total + pltpu.roll(total, 32, 1)
        packed = packed + jnp.where(lane36 // 32 == kh, total, 0.0)
    out[G_ONE : G_ONE + 48, :] = jnp.concatenate(
        [packed, jnp.zeros((12, 128), F32)], axis=0
    ).astype(BF)
    out[G_ONE + 48 :, :] = jnp.zeros((out.shape[0] - G_ONE - 48, 128), BF)
    half_rows = kept.shape[0]
    mine = pl.multiple_of(me % 2 * half_rows, half_rows)
    kept[...] = out[pl.ds(mine, half_rows), :]
    sent[...] = out[pl.ds(half_rows - mine, half_rows), :]


def finish(scales, mine, other, one_far, two_far, three_far, one, two, three, sems):
    first_core = position()[0] % 2 == 0
    half_rows = mine.shape[0]

    def rows(at, count):
        parts = []
        while count:
            use = min(count, half_rows - at % half_rows)
            here = slice(at % half_rows, at % half_rows + use)
            flag = first_core if at < half_rows else jnp.logical_not(first_core)
            parts.append(jnp.where(flag, mine[here, :], other[here, :]).astype(F32))
            at, count = (at + use, count - use)
        return parts[0] if len(parts) == 1 else jnp.concatenate(parts, axis=0)

    copies = []

    def leave(near_ref, far_ref):
        copies.append(pltpu.make_async_copy(near_ref, far_ref, sems.at[len(copies)]))
        copies[-1].start()

    for k in range(27):
        got = rows(G_TWO + 16 * k, 16) * scales[1]
        two[k, 0:16, :] = got[:, :64]
        two[k, 16:32, :] = got[:, 64:]
    leave(two, two_far)
    got = rows(G_ONE, 48) * scales[0]
    for it in range(9):
        for kh, k in enumerate(taps_of(it)):
            one[k] = got[4 * it : 4 * it + 4, 32 * kh : 32 * kh + 32]
    leave(one, one_far)
    for third in range(3):
        for k in range(9 * third, 9 * third + 9):
            three[k] = rows(64 * k, 64) * scales[2]
        here = slice(9 * third, 9 * third + 9)
        leave(three.at[here], three_far.at[here])
    for copy in copies:
        copy.wait()


VMEM = pl.BlockSpec(memory_space=pltpu.VMEM)


def near(*shape):
    return pltpu.VMEM(shape, BF)


FAR = pl.BlockSpec(memory_space=pl.ANY)
HANDED = ((512, 576), (320, 1440), (256, 4608), (192, 1280), (256, 1280), (512, 1024))


def run_near(volume, swap_core, swap_chip, filter_one, filter_two):
    args = [volume, swap_core, swap_chip, filter_one, filter_two]
    return pl.pallas_call(
        near_part,
        out_shape=[jax.ShapeDtypeStruct(shape, BF) for shape in HANDED],
        in_specs=[VMEM] * len(args),
        out_specs=[VMEM] * len(HANDED),
        scratch_shapes=[near(192, 22 * 128)],
        compiler_params=pltpu.CompilerParams(vmem_limit_bytes=20 * 1024 * 1024),
        cost_estimate=pl.CostEstimate(
            flops=3 * 10**9, bytes_accessed=8 * 10**6, transcendentals=0
        ),
        name="near_part",
    )(*args)


def local_grads(swaps, grad, filter_three, handed, rows):
    tables = [jnp.asarray(t, BF) for t in one_hot_tables()]
    args = [*swaps, grad, filter_three, *handed, *tables]
    return pl.pallas_call(
        body,
        out_shape=[jax.ShapeDtypeStruct((rows // 2, 128), BF)] * 2,
        in_specs=[VMEM] * len(args),
        out_specs=[VMEM] * 2,
        scratch_shapes=[
            near(128, 1728),
            near(256, 8 * 128),
            near(192, 20 * 128),
            near(2304, 1024),
            near(512, 512),
            near(1728, 768),
            near(4608, 256),
            near(512, 512),
            near(512, 512),
            near(512, 1024),
            near(rows, 128),
        ],
        compiler_params=pltpu.CompilerParams(vmem_limit_bytes=LIMIT * 1024 * 1024),
        cost_estimate=pl.CostEstimate(flops=10**10, bytes_accessed=10**7, transcendentals=0),
        name="local_grads",
    )(*args)


def run_finish(mine, other, cells):
    scales = [float(1.0 / np.sqrt(cells / size)) for size in (1.0, 8.0, 64.0)]
    shapes = [(27, 4, 32), (27, 32, 64), (27, 64, 128)]
    outs = pl.pallas_call(
        functools.partial(finish, scales),
        out_shape=[jax.ShapeDtypeStruct(shape, F32) for shape in shapes],
        in_specs=[VMEM] * 2,
        out_specs=[FAR] * 3,
        scratch_shapes=[pltpu.VMEM(shape, F32) for shape in shapes]
        + [pltpu.SemaphoreType.DMA((5,))],
        compiler_params=pltpu.CompilerParams(vmem_limit_bytes=8 * 1024 * 1024),
        name="finish",
    )(mine, other)
    return tuple(o.reshape(3, 3, 3, *o.shape[1:]) for o in outs)


def over_sample(pieces):
    return lax.all_to_all(pieces, "sample", 0, 0, tiled=True)


def over_chips(pieces):
    size = lax.axis_size("space")
    groups = [list(range(core, size, 2)) for core in range(2)]
    return lax.all_to_all(pieces, "space", 0, 0, axis_index_groups=groups, tiled=True)


def total_of(got):
    return got.astype(F32).sum(axis=0).astype(BF)


def swap(values, first):
    size = lax.axis_size("space")
    pairs = [(i, i + 1) for i in range(first, size - 1, 2)]
    return lax.ppermute(values, "space", pairs + [(j, i) for i, j in pairs])


def per_device(volume, grad_out, filter_one, filter_two, filter_three):
    spaces, samples = (lax.axis_size("space"), lax.axis_size("sample"))
    own = volume.reshape(512, 128)
    grad = grad_out.reshape(32, 128)
    f1 = filter_one.reshape(27, 4, 32)
    f2 = filter_two.reshape(27, 32, 64)
    f3 = filter_three.reshape(1728, 128)
    core = lax.axis_index("space") % 2

    def second(block, flip=0):
        planes = lax.dynamic_slice(block, (64 * (core ^ flip), 0), (448, 128))
        return jnp.concatenate([planes, grad], axis=0)

    swap_core = swap(own, 0)
    swap_chip = swap(own, 1)
    relay = second(swap_core)
    swap_chip2 = swap(relay, 1)
    chip_later = lax.optimization_barrier((swap_chip, relay))[0]
    swap_core2 = swap(second(chip_later, 1), 0)
    chips = spaces // 2
    handed = run_near(own, swap_core, swap_chip, f1, f2)
    keep, send = local_grads(
        (swap_core, swap_chip, swap_chip2, swap_core2), grad, f3, handed, spaces * SLOT
    )
    half = (keep.astype(F32) + swap(send, 0).astype(F32)).astype(BF)
    part = total_of(over_chips(half.reshape(chips, SLOT, 128)))
    part = total_of(over_sample(jnp.broadcast_to(part[None], (samples, SLOT, 128))))
    mine = over_chips(jnp.broadcast_to(part[None], (chips, SLOT, 128))).reshape(-1, 128)
    cells = float(samples * spaces * volume.shape[1] * volume.shape[3] * volume.shape[4])
    return run_finish(mine, swap(mine, 0), cells)


def solution(mesh):
    return jax.shard_map(
        per_device,
        mesh=mesh,
        in_specs=(
            P(("sample", "space"), None, None, None, None),
            P(("sample", "space"), None, None, None, None),
            P(),
            P(),
            P(),
        ),
        out_specs=(P(), P(), P()),
        check_vma=False,
    )
```

```python
import functools

import jax
import jax.numpy as jnp
import numpy as np
from jax import lax
from jax.experimental import pallas as pl
from jax.experimental.pallas import tpu as pltpu
from jax.sharding import PartitionSpec as P

BF = jnp.bfloat16
F32 = jnp.float32
SLOT = 72
LIMIT = 44
G_TWO = 1728
G_ONE = 2160
NT = (((1,), (1,)), ((), ()))
TN = (((0,), (0,)), ((), ()))


def table(rows, cols):
    return np.zeros((rows, cols), np.float32)


def one_hot_tables():
    pair = table(256, 128)
    for a in range(2):
        for w in range(64):
            pair[128 * a + 2 * w, 64 * a + w] = 1.0
    squeeze = table(512, 128)
    spread = table(128, 1152)
    grow_g = table(96, 768)
    grow2 = table(128, 512)
    for h in range(4):
        for w in range(32):
            squeeze[128 * h + 2 * w, 32 * h + w] = 1.0
            for kh in range(3):
                for kw in range(3):
                    if 0 <= h + kh - 1 < 4 and 0 <= w + kw - 1 < 32:
                        src = 32 * (h + kh - 1) + w + kw - 1
                        spread[src, 128 * (3 * kh + kw) + 32 * h + w] = 1.0
            for n in range(6):
                src = 32 * (n // 2) + 16 * (h // 2) + w // 2
                grow_g[src, 128 * n + 32 * h + w] = 1.0 / 16
            for d in range(2):
                for u in range(2):
                    grow2[32 * h + w, 128 * h + 64 * d + 2 * w + u] = 1.0 / 16
    grow1 = table(256, 512)
    for e in range(4):
        for w in range(128):
            grow1[64 * e + w // 2, 128 * e + w] = 1.0 / 16
    return [pair, squeeze, spread, grow_g, grow2, grow1]


def dot(a, b):
    return jnp.dot(a, b, preferred_element_type=F32)


def inside(index, count):
    return jnp.logical_and(index >= 0, index < count)


def position():
    return lax.axis_index("space"), lax.axis_size("space")


def taps_of(it):
    kd, kw = (it // 3, it % 3)
    return [kd * 9 + kh * 3 + kw for kh in range(3)]


def taps_back(it):
    kd, kw = (2 - it // 3, 2 - it % 3)
    return [kd * 9 + (2 - kh) * 3 + kw for kh in range(3)]


def band_one(filter_one, t1):
    lane = lax.broadcasted_iota(jnp.int32, (32, 640), 1) % 16
    rows = filter_one[...].astype(F32).reshape(108, 32).astype(BF)
    at = lax.broadcasted_iota(jnp.int32, (108, 640), 1)
    kd = (at >= 192).astype(jnp.int32) + (at >= 384).astype(jnp.int32)
    rest = at - 192 * kd
    kw = (rest >= 64).astype(jnp.int32) + (rest >= 128).astype(jnp.int32)
    c = (rest - 64 * kw) // 16
    kh = rest % 16
    place = 36 * kd + 12 * kh + 4 * kw + c
    here = lax.broadcasted_iota(jnp.int32, (108, 640), 0) == place
    here = jnp.logical_and(here, jnp.logical_and(kh < 3, at < 576))
    perm = jnp.where(here, 0.5, 0.0).astype(BF)
    base = lax.dot_general(rows, perm, TN, preferred_element_type=F32)
    for h in range(16):
        moved = pltpu.roll(base, (h - 1) % 640, 1) if h != 1 else base
        if h == 0:
            moved = jnp.where(lane == 15, 0.0, moved)
        if h == 15:
            moved = jnp.where(lane == 0, 0.0, moved)
        t1[32 * h : 32 * h + 32, :] = moved[:, :576].astype(BF)


def band_two(filter_two, t2):
    taps = []
    for kh in range(3):
        rows = jnp.concatenate([filter_two[taps_of(it)[kh]] for it in range(9)], axis=0)
        taps.append(rows.astype(F32).T * 0.5)
    zero = jnp.zeros((64, 288), F32)
    for s in range(5):
        parts = [taps[p - s + 1] if 0 <= p - s + 1 < 3 else zero for p in range(5)]
        t2[64 * s : 64 * s + 64, :] = jnp.concatenate(parts, axis=1).astype(BF)


def band_two_back(filter_two, t2r):
    for it in range(9):
        v2 = [filter_two[k].astype(F32) for k in taps_back(it)]
        zero = jnp.zeros((32, 64), F32)
        for s in range(-6, 8):
            if -1 <= s <= 2:
                parts = [v2[s + j] if 0 <= s + j <= 2 else zero for j in range(2)]
                tile = jnp.concatenate(parts, axis=1).astype(BF)
            else:
                tile = jnp.zeros((32, 128), BF)
            for m in range(4):
                hp = 2 * m + 1 - s
                if 0 <= hp < 8:
                    t2r[32 * hp : 32 * hp + 32, it * 512 + 128 * m : it * 512 + 128 * m + 128] = tile


def with_column_shifts(rows, x1, at):
    lane = lax.broadcasted_iota(jnp.int32, (64, 128), 1)
    for p in range(rows.shape[0] // 64):
        lanes = slice(128 * (at + p), 128 * (at + p) + 128)
        plane = rows[64 * p : 64 * p + 64, :]
        wide = plane.astype(F32)
        x1[0:64, lanes] = jnp.where(lane == 0, 0.0, pltpu.roll(wide, 1, 1)).astype(BF)
        x1[64:128, lanes] = plane
        x1[128:192, lanes] = jnp.where(lane == 127, 0.0, pltpu.roll(wide, 127, 1)).astype(BF)
    return at + rows.shape[0] // 64


def layer_one(t1, x1, at, scale):
    rhs = jnp.concatenate(
        [x1[:, 128 * (at + kd) : 128 * (at + kd) + 256] for kd in range(3)], axis=0
    )
    half = dot(t1[...], rhs)
    t = jnp.tanh(half)
    act = half + half * t
    act = act[:, :128] + act[:, 128:]
    act = act.reshape(8, 2, 32, 128)
    act = (act[:, 0] + act[:, 1]).reshape(256, 128)
    act = act + pltpu.roll(act, 127, 1)
    return half, t, (act * scale).astype(BF)


def either_of(first_core):
    def either(a, b, lo, hi):
        return jnp.where(first_core, a[lo:hi, :], b[lo:hi, :])

    return either


def near_part(
    vol_own,
    swap_core,
    swap_chip,
    filter_one,
    filter_two,
    t1,
    t2,
    t2r,
    x1_own,
    pp,
    sl1,
    x1,
):
    me, blocks = position()
    either = either_of(me % 2 == 0)
    band_two_back(filter_two, t2r)
    band_two(filter_two, t2)
    band_one(filter_one, t1)
    at = with_column_shifts(either(swap_chip, swap_core, 64, 512), x1, 0)
    at = with_column_shifts(vol_own[...], x1, at)
    at = with_column_shifts(either(swap_core, swap_chip, 0, 448), x1, at)
    x1_own[...] = x1[:, 768:2048]
    for j in range(10):
        scale = jnp.where(inside(4 * me - 3 + j, 4 * blocks), 0.125, 0.0)
        half, t, act = layer_one(t1, x1, 2 * j, scale)
        if 3 <= j < 7:
            slope = (1.0 + t) + half * (1.0 - t * t)
            sl1[:, 256 * (j - 3) : 256 * (j - 3) + 256] = slope.astype(BF)
        pp[:, 128 * j : 128 * j + 128] = act


def body(
    swap_core,
    swap_chip,
    swap_chip2,
    swap_core2,
    grad_own,
    filter_three,
    t1,
    t2,
    t2r,
    x1,
    pp_near,
    sl1,
    pair,
    squeeze,
    spread,
    grow_g,
    grow2,
    grow1,
    kept,
    sent,
    w3t,
    pp,
    xo,
    x2,
    q,
    x3,
    d2c,
    sl2,
    d2,
    d1,
    out,
):
    me, blocks = position()
    either = either_of(me % 2 == 0)
    w3t[...] = (filter_three[...].astype(F32).T * 0.5).astype(BF)

    at = with_column_shifts(either(swap_chip2, swap_core2, 0, 448), xo, 0)
    at = with_column_shifts(either(swap_chip, swap_core, 0, 192), xo, at)
    at = with_column_shifts(either(swap_core, swap_chip, 320, 512), xo, at)
    at = with_column_shifts(either(swap_core2, swap_chip2, 0, 448), xo, at)
    for j in (0, 1, 2, 3, 14, 15, 16, 17):
        scale = jnp.where(inside(4 * me - 7 + j, 4 * blocks), 0.125, 0.0)
        act = layer_one(t1, xo, 2 * j if j < 4 else 10 + 2 * (j - 14), scale)[2]
        lo = 128 * (j if j < 4 else j - 10)
        pp[:, lo : lo + 128] = act

    def pooled_plane(j):
        if 4 <= j < 14:
            return pp_near[:, 128 * (j - 4) : 128 * (j - 4) + 128]
        lo = 128 * (j if j < 4 else j - 10)
        return pp[:, lo : lo + 128]

    col64 = lax.broadcasted_iota(jnp.int32, (256, 128), 1) % 64
    first_col, last_col = (col64 == 0, col64 == 63)
    for first in range(17):
        both = jnp.concatenate([pooled_plane(first), pooled_plane(first + 1)], axis=1)
        got = dot(both, pair[...])
        moved = (
            jnp.where(first_col, 0.0, pltpu.roll(got, 1, 1)).astype(BF),
            got.astype(BF),
            jnp.where(last_col, 0.0, pltpu.roll(got, 127, 1)).astype(BF),
        )
        for kd in range(3):
            m = (first - kd) // 2
            if (first - kd) % 2 == 0 and 0 <= m < 8:
                for kw in range(3):
                    k = 3 * kd + kw
                    x2[256 * k : 256 * k + 256, m * 128 : m * 128 + 128] = moved[kw]

    for c in range(4):
        lanes = slice(c * 256, c * 256 + 256)
        for g in range(2):
            rhs = jnp.concatenate(
                [
                    x2[256 * it + 32 * p : 256 * it + 32 * p + 32, lanes]
                    for p in range(3 * g, 3 * g + 5)
                    for it in range(9)
                ],
                axis=0,
            )
            half = dot(t2[64 * g : 64 * g + 256, :], rhs)
            t = jnp.tanh(half)
            if 1 <= c < 3:
                slope = (1.0 + t) + half * (1.0 - t * t)
                sl2[256 * g : 256 * g + 256, c * 256 - 256 : c * 256] = slope.astype(BF)
            act = (half + half * t).reshape(2, 2, 64, 256)
            act = (act[:, 0] + act[:, 1]).reshape(128, 256)
            for u in range(2):
                tile = act[:, 128 * u : 128 * u + 128]
                tile = tile + pltpu.roll(tile, 64, 1)
                tile = tile + pltpu.roll(tile, 127, 1)
                m = 2 * c + u
                scale = jnp.where(inside(2 * me - 3 + m, 2 * blocks), 0.125, 0.0)
                tile = (tile * scale).astype(BF)
                for h in range(2):
                    lo = 128 * (2 * g + h)
                    q[64 * m : 64 * m + 64, lo : lo + 128] = tile[64 * h : 64 * h + 64, :]

    packed = dot(q[...], squeeze[...]).astype(BF)
    got = dot(packed, spread[...]).astype(BF)
    for kd in range(3):
        for s in range(9):
            k = 9 * kd + s
            for n in range(6):
                x3[64 * k : 64 * k + 64, 128 * n : 128 * n + 128] = got[
                    64 * (n + kd) : 64 * (n + kd) + 64, 128 * s : 128 * s + 128
                ]
    rows = jnp.concatenate(
        [
            either(swap_chip2, swap_core2, 448, 480),
            grad_own[...],
            either(swap_core2, swap_chip2, 448, 480),
        ],
        axis=0,
    )
    grown = dot(rows.astype(F32).T.astype(BF), grow_g[...])
    half = dot(w3t[...], x3[...])
    t = jnp.tanh(half)
    d3 = (grown * ((1.0 + t) + half * (1.0 - t * t))).astype(BF)

    out[:G_TWO, :] = lax.dot_general(
        x3[:, 256:512], d3[:, 256:512], NT, preferred_element_type=F32
    ).astype(BF)

    lane = lax.broadcasted_iota(jnp.int32, (64, 128), 1)
    col, line = (lane % 32, lane // 32)
    masks = []
    for b in range(3):
        for c in range(3):
            keep = inside(col + 1 - c, 32)
            masks.append(jnp.logical_and(keep, inside(line + 1 - b, 4)))
    lhs = jnp.concatenate([filter_three[576 * a : 576 * a + 576, :] for a in range(3)], axis=1)
    grown = []
    for pair_at in range(2):
        rhs = jnp.concatenate(
            [
                d3[:, 128 * (2 * pair_at + 2 - a) : 128 * (2 * pair_at + 2 - a) + 256]
                for a in range(3)
            ],
            axis=0,
        )
        got = dot(lhs, rhs)
        for u in range(2):
            total = None
            for b in range(3):
                for c in range(3):
                    s = 3 * b + c
                    part = got[64 * s : 64 * s + 64, 128 * u : 128 * u + 128]
                    move_by = -(32 * (1 - b) + 1 - c) % 128
                    if move_by:
                        part = jnp.where(masks[s], pltpu.roll(part, move_by, 1), 0.0)
                    total = part if total is None else total + part
            n = 2 * pair_at + u
            scale = jnp.where(inside(2 * me - 1 + n, 2 * blocks), 1.0, 0.0)
            grown.append((total * scale).astype(BF))
    back = dot(jnp.concatenate(grown, axis=0), grow2[...])
    for h in range(8):
        rows = slice(64 * h, 64 * h + 64)
        for n in range(4):
            lanes = slice(128 * n, 128 * n + 128)
            source = back[64 * n : 64 * n + 64, 128 * (h // 2) : 128 * (h // 2) + 128]
            d2[rows, lanes] = (source * sl2[rows, lanes].astype(F32)).astype(BF)

    for part in range(2):
        rows = slice(256 * part, 256 * part + 256)
        for start in range(1, 6):
            u = start // 2
            got = d2[rows, 128 * u : 128 * u + 128].astype(F32)
            if start % 2:
                after = d2[rows, 128 * u + 128 : 128 * u + 256].astype(F32)
                lane = lax.broadcasted_iota(jnp.int32, (256, 128), 1)
                got = jnp.where(lane < 64, pltpu.roll(got, 64, 1), pltpu.roll(after, 64, 1))
            moved = (
                jnp.where(first_col, 0.0, pltpu.roll(got, 1, 1)).astype(BF),
                got.astype(BF),
                jnp.where(last_col, 0.0, pltpu.roll(got, 127, 1)).astype(BF),
            )
            for kd in range(3):
                for m in range(2):
                    if 1 + kd + 2 * m == start:
                        for kw in range(3):
                            lo = 512 * (3 * kd + kw) + 256 * part
                            d2c[lo : lo + 256, 128 * m : 128 * m + 128] = moved[kw]
    back = dot(t2r[...], d2c[...]).astype(BF)
    back = dot(back, grow1[...])
    for h in range(16):
        rows = slice(32 * h, 32 * h + 32)
        source = back[32 * (h // 2) : 32 * (h // 2) + 32, :]
        for e in range(8):
            lanes = slice(128 * e, 128 * e + 128)
            delta = source[:, 128 * (e // 2) : 128 * (e // 2) + 128] * sl1[rows, lanes].astype(F32)
            d1[rows, lanes] = delta.astype(BF)

    lane16 = lax.broadcasted_iota(jnp.int32, (16, 128), 1)
    all_two = lax.dot_general(
        x2[:, 384:640], d2[:, 128:384], NT, preferred_element_type=F32
    )
    for it in range(9):
        got = all_two[256 * it : 256 * it + 256, :]
        for kh, k in enumerate(taps_of(it)):
            totals = [None, None]
            for h in range(8):
                hp = h + kh - 1
                if 0 <= hp < 8:
                    part = got[32 * hp : 32 * hp + 32, 128 * (h // 2) : 128 * (h // 2) + 128]
                    now = totals[h % 2]
                    totals[h % 2] = part if now is None else now + part
            low = totals[0] + pltpu.roll(totals[1], 64, 1)
            high = pltpu.roll(totals[0], 64, 1) + totals[1]
            out[G_TWO + k * 16 : G_TWO + k * 16 + 16, :] = jnp.where(
                lane16 < 64, low[:16], high[16:]
            ).astype(BF)

    lhs = jnp.concatenate([x1[:, 128 * kd : 128 * kd + 1024] for kd in range(3)], axis=0)
    got = lax.dot_general(lhs, d1[...], NT, preferred_element_type=F32)
    row = lax.broadcasted_iota(jnp.int32, (576, 128), 0) % 16
    col = lax.broadcasted_iota(jnp.int32, (576, 128), 1) // 32
    lane36 = lax.broadcasted_iota(jnp.int32, (36, 128), 1)
    packed = jnp.zeros((36, 128), F32)
    for kh in range(3):
        total = jnp.zeros((576, 128), F32)
        for u in range(4):
            keep = row == col + (4 * u + kh - 1)
            total = total + jnp.where(keep, got[:, 128 * u : 128 * u + 128], 0.0)
        total = total.reshape(36, 16, 128).sum(axis=1)
        total = total + pltpu.roll(total, 64, 1)
        total = total + pltpu.roll(total, 32, 1)
        packed = packed + jnp.where(lane36 // 32 == kh, total, 0.0)
    out[G_ONE : G_ONE + 48, :] = jnp.concatenate(
        [packed, jnp.zeros((12, 128), F32)], axis=0
    ).astype(BF)
    out[G_ONE + 48 :, :] = jnp.zeros((out.shape[0] - G_ONE - 48, 128), BF)
    half_rows = kept.shape[0]
    mine = pl.multiple_of(me % 2 * half_rows, half_rows)
    kept[...] = out[pl.ds(mine, half_rows), :]
    sent[...] = out[pl.ds(half_rows - mine, half_rows), :]


def finish(scales, mine, other, one_far, two_far, three_far, one, two, three, sems):
    first_core = position()[0] % 2 == 0
    half_rows = mine.shape[0]

    def rows(at, count):
        parts = []
        while count:
            use = min(count, half_rows - at % half_rows)
            here = slice(at % half_rows, at % half_rows + use)
            flag = first_core if at < half_rows else jnp.logical_not(first_core)
            parts.append(jnp.where(flag, mine[here, :], other[here, :]).astype(F32))
            at, count = (at + use, count - use)
        return parts[0] if len(parts) == 1 else jnp.concatenate(parts, axis=0)

    copies = []

    def leave(near_ref, far_ref):
        copies.append(pltpu.make_async_copy(near_ref, far_ref, sems.at[len(copies)]))
        copies[-1].start()

    for k in range(27):
        got = rows(G_TWO + 16 * k, 16) * scales[1]
        two[k, 0:16, :] = got[:, :64]
        two[k, 16:32, :] = got[:, 64:]
    leave(two, two_far)
    got = rows(G_ONE, 48) * scales[0]
    for it in range(9):
        for kh, k in enumerate(taps_of(it)):
            one[k] = got[4 * it : 4 * it + 4, 32 * kh : 32 * kh + 32]
    leave(one, one_far)
    for third in range(3):
        for k in range(9 * third, 9 * third + 9):
            three[k] = rows(64 * k, 64) * scales[2]
        here = slice(9 * third, 9 * third + 9)
        leave(three.at[here], three_far.at[here])
    for copy in copies:
        copy.wait()


VMEM = pl.BlockSpec(memory_space=pltpu.VMEM)


def near(*shape):
    return pltpu.VMEM(shape, BF)


FAR = pl.BlockSpec(memory_space=pl.ANY)
def relay_planes(block, grad, out):
    first_core = position()[0] % 2 == 0
    out[:448, :] = jnp.where(first_core, block[64:, :], block[:448, :])
    out[448:, :] = grad[...]


def run_relay(block, grad):
    return pl.pallas_call(
        relay_planes,
        out_shape=jax.ShapeDtypeStruct((480, 128), BF),
        in_specs=[VMEM] * 2,
        out_specs=VMEM,
        compiler_params=pltpu.CompilerParams(vmem_limit_bytes=4 * 1024 * 1024),
        cost_estimate=pl.CostEstimate(
            flops=4 * 10**9, bytes_accessed=12 * 10**6, transcendentals=0
        ),
        name="relay",
    )(block, grad)


HANDED = ((512, 576), (320, 1440), (256, 4608), (192, 1280), (256, 1280), (512, 1024))


def run_near(volume, swap_core, swap_chip, filter_one, filter_two):
    args = [volume, swap_core, swap_chip, filter_one, filter_two]
    return pl.pallas_call(
        near_part,
        out_shape=[jax.ShapeDtypeStruct(shape, BF) for shape in HANDED],
        in_specs=[VMEM] * len(args),
        out_specs=[VMEM] * len(HANDED),
        scratch_shapes=[near(192, 22 * 128)],
        compiler_params=pltpu.CompilerParams(vmem_limit_bytes=20 * 1024 * 1024),
        cost_estimate=pl.CostEstimate(
            flops=3 * 10**9, bytes_accessed=8 * 10**6, transcendentals=0
        ),
        name="near_part",
    )(*args)


def local_grads(swaps, grad, filter_three, handed, rows):
    tables = [jnp.asarray(t, BF) for t in one_hot_tables()]
    args = [*swaps, grad, filter_three, *handed, *tables]
    return pl.pallas_call(
        body,
        out_shape=[jax.ShapeDtypeStruct((rows // 2, 128), BF)] * 2,
        in_specs=[VMEM] * len(args),
        out_specs=[VMEM] * 2,
        scratch_shapes=[
            near(128, 1728),
            near(256, 8 * 128),
            near(192, 20 * 128),
            near(2304, 1024),
            near(512, 512),
            near(1728, 768),
            near(4608, 256),
            near(512, 512),
            near(512, 512),
            near(512, 1024),
            near(rows, 128),
        ],
        compiler_params=pltpu.CompilerParams(vmem_limit_bytes=LIMIT * 1024 * 1024),
        cost_estimate=pl.CostEstimate(flops=10**10, bytes_accessed=10**7, transcendentals=0),
        name="local_grads",
    )(*args)


def run_finish(mine, other, cells):
    scales = [float(1.0 / np.sqrt(cells / size)) for size in (1.0, 8.0, 64.0)]
    shapes = [(27, 4, 32), (27, 32, 64), (27, 64, 128)]
    outs = pl.pallas_call(
        functools.partial(finish, scales),
        out_shape=[jax.ShapeDtypeStruct(shape, F32) for shape in shapes],
        in_specs=[VMEM] * 2,
        out_specs=[FAR] * 3,
        scratch_shapes=[pltpu.VMEM(shape, F32) for shape in shapes]
        + [pltpu.SemaphoreType.DMA((5,))],
        compiler_params=pltpu.CompilerParams(vmem_limit_bytes=8 * 1024 * 1024),
        name="finish",
    )(mine, other)
    return tuple(o.reshape(3, 3, 3, *o.shape[1:]) for o in outs)


def over_sample(pieces):
    return lax.all_to_all(pieces, "sample", 0, 0, tiled=True)


def over_chips(pieces):
    size = lax.axis_size("space")
    groups = [list(range(core, size, 2)) for core in range(2)]
    return lax.all_to_all(pieces, "space", 0, 0, axis_index_groups=groups, tiled=True)


def total_of(got):
    return got.astype(F32).sum(axis=0).astype(BF)


def swap(values, first):
    size = lax.axis_size("space")
    pairs = [(i, i + 1) for i in range(first, size - 1, 2)]
    return lax.ppermute(values, "space", pairs + [(j, i) for i, j in pairs])


def per_device(volume, grad_out, filter_one, filter_two, filter_three):
    spaces, samples = (lax.axis_size("space"), lax.axis_size("sample"))
    own = volume.reshape(512, 128)
    grad = grad_out.reshape(32, 128)
    f1 = filter_one.reshape(27, 4, 32)
    f2 = filter_two.reshape(27, 32, 64)
    f3 = filter_three.reshape(1728, 128)
    core = lax.axis_index("space") % 2

    def second(block):
        planes = lax.dynamic_slice(block, (64 * core, 0), (448, 128))
        return jnp.concatenate([planes, grad], axis=0)

    swap_core = swap(own, 0)
    swap_chip = swap(own, 1)
    relay = second(swap_core)
    swap_chip2 = swap(relay, 1)
    chip_later = lax.optimization_barrier((swap_chip, relay))[0]
    swap_core2 = swap(run_relay(chip_later, grad), 0)
    chips = spaces // 2
    handed = run_near(own, swap_core, swap_chip, f1, f2)
    keep, send = local_grads(
        (swap_core, swap_chip, swap_chip2, swap_core2), grad, f3, handed, spaces * SLOT
    )
    half = (keep.astype(F32) + swap(send, 0).astype(F32)).astype(BF)
    part = total_of(over_chips(half.reshape(chips, SLOT, 128)))
    part = total_of(over_sample(jnp.broadcast_to(part[None], (samples, SLOT, 128))))
    mine = over_chips(jnp.broadcast_to(part[None], (chips, SLOT, 128))).reshape(-1, 128)
    cells = float(samples * spaces * volume.shape[1] * volume.shape[3] * volume.shape[4])
    return run_finish(mine, swap(mine, 0), cells)


def solution(mesh):
    return jax.shard_map(
        per_device,
        mesh=mesh,
        in_specs=(
            P(("sample", "space"), None, None, None, None),
            P(("sample", "space"), None, None, None, None),
            P(),
            P(),
            P(),
        ),
        out_specs=(P(), P(), P()),
        check_vma=False,
    )
```

```python
import functools

import jax
import jax.numpy as jnp
import numpy as np
from jax import lax
from jax.experimental import pallas as pl
from jax.experimental.pallas import tpu as pltpu
from jax.sharding import PartitionSpec as P

BF = jnp.bfloat16
F32 = jnp.float32
SLOT = 72
LIMIT = 44
G_TWO = 1728
G_ONE = 2160
NT = (((1,), (1,)), ((), ()))
TN = (((0,), (0,)), ((), ()))


def table(rows, cols):
    return np.zeros((rows, cols), np.float32)


def one_hot_tables():
    pair = table(256, 128)
    for a in range(2):
        for w in range(64):
            pair[128 * a + 2 * w, 64 * a + w] = 1.0
    squeeze = table(512, 128)
    spread = table(128, 1152)
    grow_g = table(96, 768)
    grow2 = table(128, 512)
    for h in range(4):
        for w in range(32):
            squeeze[128 * h + 2 * w, 32 * h + w] = 1.0
            for kh in range(3):
                for kw in range(3):
                    if 0 <= h + kh - 1 < 4 and 0 <= w + kw - 1 < 32:
                        src = 32 * (h + kh - 1) + w + kw - 1
                        spread[src, 128 * (3 * kh + kw) + 32 * h + w] = 1.0
            for n in range(6):
                src = 32 * (n // 2) + 16 * (h // 2) + w // 2
                grow_g[src, 128 * n + 32 * h + w] = 1.0 / 16
            for d in range(2):
                for u in range(2):
                    grow2[32 * h + w, 128 * h + 64 * d + 2 * w + u] = 1.0 / 16
    grow1 = table(256, 512)
    for e in range(4):
        for w in range(128):
            grow1[64 * e + w // 2, 128 * e + w] = 1.0 / 16
    return [pair, squeeze, spread, grow_g, grow2, grow1]


def dot(a, b):
    return jnp.dot(a, b, preferred_element_type=F32)


def inside(index, count):
    return jnp.logical_and(index >= 0, index < count)


def position():
    return lax.axis_index("space"), lax.axis_size("space")


def taps_of(it):
    kd, kw = (it // 3, it % 3)
    return [kd * 9 + kh * 3 + kw for kh in range(3)]


def taps_back(it):
    kd, kw = (2 - it // 3, 2 - it % 3)
    return [kd * 9 + (2 - kh) * 3 + kw for kh in range(3)]


def band_one(filter_one, t1):
    lane = lax.broadcasted_iota(jnp.int32, (32, 640), 1) % 16
    rows = filter_one[...].astype(F32).reshape(108, 32).astype(BF)
    at = lax.broadcasted_iota(jnp.int32, (108, 640), 1)
    kd = (at >= 192).astype(jnp.int32) + (at >= 384).astype(jnp.int32)
    rest = at - 192 * kd
    kw = (rest >= 64).astype(jnp.int32) + (rest >= 128).astype(jnp.int32)
    c = (rest - 64 * kw) // 16
    kh = rest % 16
    place = 36 * kd + 12 * kh + 4 * kw + c
    here = lax.broadcasted_iota(jnp.int32, (108, 640), 0) == place
    here = jnp.logical_and(here, jnp.logical_and(kh < 3, at < 576))
    perm = jnp.where(here, 0.5, 0.0).astype(BF)
    base = lax.dot_general(rows, perm, TN, preferred_element_type=F32)
    for h in range(16):
        moved = pltpu.roll(base, (h - 1) % 640, 1) if h != 1 else base
        if h == 0:
            moved = jnp.where(lane == 15, 0.0, moved)
        if h == 15:
            moved = jnp.where(lane == 0, 0.0, moved)
        t1[32 * h : 32 * h + 32, :] = moved[:, :576].astype(BF)


def band_two(filter_two, t2):
    taps = []
    for kh in range(3):
        rows = jnp.concatenate([filter_two[taps_of(it)[kh]] for it in range(9)], axis=0)
        taps.append(rows.astype(F32).T * 0.5)
    zero = jnp.zeros((64, 288), F32)
    for s in range(5):
        parts = [taps[p - s + 1] if 0 <= p - s + 1 < 3 else zero for p in range(5)]
        t2[64 * s : 64 * s + 64, :] = jnp.concatenate(parts, axis=1).astype(BF)


def band_two_back(filter_two, t2r):
    for it in range(9):
        v2 = [filter_two[k].astype(F32) for k in taps_back(it)]
        zero = jnp.zeros((32, 64), F32)
        for s in range(-6, 8):
            if -1 <= s <= 2:
                parts = [v2[s + j] if 0 <= s + j <= 2 else zero for j in range(2)]
                tile = jnp.concatenate(parts, axis=1).astype(BF)
            else:
                tile = jnp.zeros((32, 128), BF)
            for m in range(4):
                hp = 2 * m + 1 - s
                if 0 <= hp < 8:
                    t2r[32 * hp : 32 * hp + 32, it * 512 + 128 * m : it * 512 + 128 * m + 128] = tile


def with_column_shifts(rows, x1, at):
    lane = lax.broadcasted_iota(jnp.int32, (64, 128), 1)
    for p in range(rows.shape[0] // 64):
        lanes = slice(128 * (at + p), 128 * (at + p) + 128)
        plane = rows[64 * p : 64 * p + 64, :]
        wide = plane.astype(F32)
        x1[0:64, lanes] = jnp.where(lane == 0, 0.0, pltpu.roll(wide, 1, 1)).astype(BF)
        x1[64:128, lanes] = plane
        x1[128:192, lanes] = jnp.where(lane == 127, 0.0, pltpu.roll(wide, 127, 1)).astype(BF)
    return at + rows.shape[0] // 64


def layer_one(t1, x1, at, scale):
    rhs = jnp.concatenate(
        [x1[:, 128 * (at + kd) : 128 * (at + kd) + 256] for kd in range(3)], axis=0
    )
    half = dot(t1[...], rhs)
    t = jnp.tanh(half)
    act = half + half * t
    act = act[:, :128] + act[:, 128:]
    act = act.reshape(8, 2, 32, 128)
    act = (act[:, 0] + act[:, 1]).reshape(256, 128)
    act = act + pltpu.roll(act, 127, 1)
    return half, t, (act * scale).astype(BF)


def either_of(first_core):
    def either(a, b, lo, hi):
        return jnp.where(first_core, a[lo:hi, :], b[lo:hi, :])

    return either


def near_part(
    vol_own,
    swap_core,
    swap_chip,
    filter_one,
    filter_two,
    t1,
    t2,
    t2r,
    x1_own,
    pp,
    sl1,
    x1,
):
    me, blocks = position()
    either = either_of(me % 2 == 0)
    band_two_back(filter_two, t2r)
    band_two(filter_two, t2)
    band_one(filter_one, t1)
    at = with_column_shifts(either(swap_chip, swap_core, 64, 512), x1, 0)
    at = with_column_shifts(vol_own[...], x1, at)
    at = with_column_shifts(either(swap_core, swap_chip, 0, 448), x1, at)
    x1_own[...] = x1[:, 768:2048]
    for j in range(10):
        scale = jnp.where(inside(4 * me - 3 + j, 4 * blocks), 0.125, 0.0)
        half, t, act = layer_one(t1, x1, 2 * j, scale)
        if 3 <= j < 7:
            slope = (1.0 + t) + half * (1.0 - t * t)
            sl1[:, 256 * (j - 3) : 256 * (j - 3) + 256] = slope.astype(BF)
        pp[:, 128 * j : 128 * j + 128] = act


def body(
    swap_core,
    swap_chip,
    swap_chip2,
    swap_core2,
    grad_own,
    filter_three,
    t1,
    t2,
    t2r,
    x1,
    pp_near,
    sl1,
    pair,
    squeeze,
    spread,
    grow_g,
    grow2,
    grow1,
    kept,
    sent,
    w3t,
    pp,
    xo,
    x2,
    q,
    x3,
    d2c,
    sl2,
    d2,
    d1,
    out,
):
    me, blocks = position()
    either = either_of(me % 2 == 0)
    w3t[...] = (filter_three[...].astype(F32).T * 0.5).astype(BF)

    at = with_column_shifts(either(swap_chip2, swap_core2, 0, 448), xo, 0)
    at = with_column_shifts(either(swap_chip, swap_core, 0, 192), xo, at)
    at = with_column_shifts(either(swap_core, swap_chip, 320, 512), xo, at)
    at = with_column_shifts(either(swap_core2, swap_chip2, 0, 448), xo, at)
    for j in (0, 1, 2, 3, 14, 15, 16, 17):
        scale = jnp.where(inside(4 * me - 7 + j, 4 * blocks), 0.125, 0.0)
        act = layer_one(t1, xo, 2 * j if j < 4 else 10 + 2 * (j - 14), scale)[2]
        lo = 128 * (j if j < 4 else j - 10)
        pp[:, lo : lo + 128] = act

    def pooled_plane(j):
        if 4 <= j < 14:
            return pp_near[:, 128 * (j - 4) : 128 * (j - 4) + 128]
        lo = 128 * (j if j < 4 else j - 10)
        return pp[:, lo : lo + 128]

    col64 = lax.broadcasted_iota(jnp.int32, (256, 128), 1) % 64
    first_col, last_col = (col64 == 0, col64 == 63)
    for first in range(17):
        both = jnp.concatenate([pooled_plane(first), pooled_plane(first + 1)], axis=1)
        got = dot(both, pair[...])
        moved = (
            jnp.where(first_col, 0.0, pltpu.roll(got, 1, 1)).astype(BF),
            got.astype(BF),
            jnp.where(last_col, 0.0, pltpu.roll(got, 127, 1)).astype(BF),
        )
        for kd in range(3):
            m = (first - kd) // 2
            if (first - kd) % 2 == 0 and 0 <= m < 8:
                for kw in range(3):
                    k = 3 * kd + kw
                    x2[256 * k : 256 * k + 256, m * 128 : m * 128 + 128] = moved[kw]

    for c in range(4):
        lanes = slice(c * 256, c * 256 + 256)
        for g in range(2):
            rhs = jnp.concatenate(
                [
                    x2[256 * it + 32 * p : 256 * it + 32 * p + 32, lanes]
                    for p in range(3 * g, 3 * g + 5)
                    for it in range(9)
                ],
                axis=0,
            )
            half = dot(t2[64 * g : 64 * g + 256, :], rhs)
            t = jnp.tanh(half)
            if 1 <= c < 3:
                slope = (1.0 + t) + half * (1.0 - t * t)
                sl2[256 * g : 256 * g + 256, c * 256 - 256 : c * 256] = slope.astype(BF)
            act = (half + half * t).reshape(2, 2, 64, 256)
            act = (act[:, 0] + act[:, 1]).reshape(128, 256)
            for u in range(2):
                tile = act[:, 128 * u : 128 * u + 128]
                tile = tile + pltpu.roll(tile, 64, 1)
                tile = tile + pltpu.roll(tile, 127, 1)
                m = 2 * c + u
                scale = jnp.where(inside(2 * me - 3 + m, 2 * blocks), 0.125, 0.0)
                tile = (tile * scale).astype(BF)
                for h in range(2):
                    lo = 128 * (2 * g + h)
                    q[64 * m : 64 * m + 64, lo : lo + 128] = tile[64 * h : 64 * h + 64, :]

    packed = dot(q[...], squeeze[...]).astype(BF)
    got = dot(packed, spread[...]).astype(BF)
    for kd in range(3):
        for s in range(9):
            k = 9 * kd + s
            for n in range(6):
                x3[64 * k : 64 * k + 64, 128 * n : 128 * n + 128] = got[
                    64 * (n + kd) : 64 * (n + kd) + 64, 128 * s : 128 * s + 128
                ]
    rows = jnp.concatenate(
        [
            either(swap_chip2, swap_core2, 448, 480),
            grad_own[...],
            either(swap_core2, swap_chip2, 448, 480),
        ],
        axis=0,
    )
    grown = dot(rows.astype(F32).T.astype(BF), grow_g[...])
    half = dot(w3t[...], x3[...])
    t = jnp.tanh(half)
    d3 = (grown * ((1.0 + t) + half * (1.0 - t * t))).astype(BF)

    out[:G_TWO, :] = lax.dot_general(
        x3[:, 256:512], d3[:, 256:512], NT, preferred_element_type=F32
    ).astype(BF)

    lane = lax.broadcasted_iota(jnp.int32, (64, 128), 1)
    col, line = (lane % 32, lane // 32)
    masks = []
    for b in range(3):
        for c in range(3):
            keep = inside(col + 1 - c, 32)
            masks.append(jnp.logical_and(keep, inside(line + 1 - b, 4)))
    lhs = jnp.concatenate([filter_three[576 * a : 576 * a + 576, :] for a in range(3)], axis=1)
    grown = []
    for pair_at in range(2):
        rhs = jnp.concatenate(
            [
                d3[:, 128 * (2 * pair_at + 2 - a) : 128 * (2 * pair_at + 2 - a) + 256]
                for a in range(3)
            ],
            axis=0,
        )
        got = dot(lhs, rhs)
        for u in range(2):
            total = None
            for b in range(3):
                for c in range(3):
                    s = 3 * b + c
                    part = got[64 * s : 64 * s + 64, 128 * u : 128 * u + 128]
                    move_by = -(32 * (1 - b) + 1 - c) % 128
                    if move_by:
                        part = jnp.where(masks[s], pltpu.roll(part, move_by, 1), 0.0)
                    total = part if total is None else total + part
            n = 2 * pair_at + u
            scale = jnp.where(inside(2 * me - 1 + n, 2 * blocks), 1.0, 0.0)
            grown.append((total * scale).astype(BF))
    back = dot(jnp.concatenate(grown, axis=0), grow2[...])
    for h in range(8):
        rows = slice(64 * h, 64 * h + 64)
        for n in range(4):
            lanes = slice(128 * n, 128 * n + 128)
            source = back[64 * n : 64 * n + 64, 128 * (h // 2) : 128 * (h // 2) + 128]
            d2[rows, lanes] = (source * sl2[rows, lanes].astype(F32)).astype(BF)

    for part in range(2):
        rows = slice(256 * part, 256 * part + 256)
        for start in range(1, 6):
            u = start // 2
            got = d2[rows, 128 * u : 128 * u + 128].astype(F32)
            if start % 2:
                after = d2[rows, 128 * u + 128 : 128 * u + 256].astype(F32)
                lane = lax.broadcasted_iota(jnp.int32, (256, 128), 1)
                got = jnp.where(lane < 64, pltpu.roll(got, 64, 1), pltpu.roll(after, 64, 1))
            moved = (
                jnp.where(first_col, 0.0, pltpu.roll(got, 1, 1)).astype(BF),
                got.astype(BF),
                jnp.where(last_col, 0.0, pltpu.roll(got, 127, 1)).astype(BF),
            )
            for kd in range(3):
                for m in range(2):
                    if 1 + kd + 2 * m == start:
                        for kw in range(3):
                            lo = 512 * (3 * kd + kw) + 256 * part
                            d2c[lo : lo + 256, 128 * m : 128 * m + 128] = moved[kw]
    back = dot(t2r[...], d2c[...]).astype(BF)
    back = dot(back, grow1[...])
    for h in range(16):
        rows = slice(32 * h, 32 * h + 32)
        source = back[32 * (h // 2) : 32 * (h // 2) + 32, :]
        for e in range(8):
            lanes = slice(128 * e, 128 * e + 128)
            delta = source[:, 128 * (e // 2) : 128 * (e // 2) + 128] * sl1[rows, lanes].astype(F32)
            d1[rows, lanes] = delta.astype(BF)

    lane16 = lax.broadcasted_iota(jnp.int32, (16, 128), 1)
    all_two = lax.dot_general(
        x2[:, 384:640], d2[:, 128:384], NT, preferred_element_type=F32
    )
    for it in range(9):
        got = all_two[256 * it : 256 * it + 256, :]
        for kh, k in enumerate(taps_of(it)):
            totals = [None, None]
            for h in range(8):
                hp = h + kh - 1
                if 0 <= hp < 8:
                    part = got[32 * hp : 32 * hp + 32, 128 * (h // 2) : 128 * (h // 2) + 128]
                    now = totals[h % 2]
                    totals[h % 2] = part if now is None else now + part
            low = totals[0] + pltpu.roll(totals[1], 64, 1)
            high = pltpu.roll(totals[0], 64, 1) + totals[1]
            out[G_TWO + k * 16 : G_TWO + k * 16 + 16, :] = jnp.where(
                lane16 < 64, low[:16], high[16:]
            ).astype(BF)

    lhs = jnp.concatenate([x1[:, 128 * kd : 128 * kd + 1024] for kd in range(3)], axis=0)
    got = lax.dot_general(lhs, d1[...], NT, preferred_element_type=F32)
    row = lax.broadcasted_iota(jnp.int32, (576, 128), 0) % 16
    col = lax.broadcasted_iota(jnp.int32, (576, 128), 1) // 32
    lane36 = lax.broadcasted_iota(jnp.int32, (36, 128), 1)
    packed = jnp.zeros((36, 128), F32)
    for kh in range(3):
        total = jnp.zeros((576, 128), F32)
        for u in range(4):
            keep = row == col + (4 * u + kh - 1)
            total = total + jnp.where(keep, got[:, 128 * u : 128 * u + 128], 0.0)
        total = total.reshape(36, 16, 128).sum(axis=1)
        total = total + pltpu.roll(total, 64, 1)
        total = total + pltpu.roll(total, 32, 1)
        packed = packed + jnp.where(lane36 // 32 == kh, total, 0.0)
    out[G_ONE : G_ONE + 48, :] = jnp.concatenate(
        [packed, jnp.zeros((12, 128), F32)], axis=0
    ).astype(BF)
    out[G_ONE + 48 :, :] = jnp.zeros((out.shape[0] - G_ONE - 48, 128), BF)
    half_rows = kept.shape[0]
    mine = pl.multiple_of(me % 2 * half_rows, half_rows)
    kept[...] = out[pl.ds(mine, half_rows), :]
    sent[...] = out[pl.ds(half_rows - mine, half_rows), :]


def finish(scales, mine, other, one_far, two_far, three_far, one, two, three, sems):
    first_core = position()[0] % 2 == 0
    half_rows = mine.shape[0]

    def rows(at, count):
        parts = []
        while count:
            use = min(count, half_rows - at % half_rows)
            here = slice(at % half_rows, at % half_rows + use)
            flag = first_core if at < half_rows else jnp.logical_not(first_core)
            parts.append(jnp.where(flag, mine[here, :], other[here, :]).astype(F32))
            at, count = (at + use, count - use)
        return parts[0] if len(parts) == 1 else jnp.concatenate(parts, axis=0)

    copies = []

    def leave(near_ref, far_ref):
        copies.append(pltpu.make_async_copy(near_ref, far_ref, sems.at[len(copies)]))
        copies[-1].start()

    for k in range(27):
        got = rows(G_TWO + 16 * k, 16) * scales[1]
        two[k, 0:16, :] = got[:, :64]
        two[k, 16:32, :] = got[:, 64:]
    leave(two, two_far)
    got = rows(G_ONE, 48) * scales[0]
    for it in range(9):
        for kh, k in enumerate(taps_of(it)):
            one[k] = got[4 * it : 4 * it + 4, 32 * kh : 32 * kh + 32]
    leave(one, one_far)
    for third in range(3):
        for k in range(9 * third, 9 * third + 9):
            three[k] = rows(64 * k, 64) * scales[2]
        here = slice(9 * third, 9 * third + 9)
        leave(three.at[here], three_far.at[here])
    for copy in copies:
        copy.wait()


VMEM = pl.BlockSpec(memory_space=pltpu.VMEM)


def near(*shape):
    return pltpu.VMEM(shape, BF)


FAR = pl.BlockSpec(memory_space=pl.ANY)
def relay_planes(last_seven, block, grad, out):
    flag = position()[0] % 2 == last_seven
    out[:448, :] = jnp.where(flag, block[64:, :], block[:448, :])
    out[448:, :] = grad[...]


def run_relay(last_seven, block, grad):
    return pl.pallas_call(
        functools.partial(relay_planes, last_seven),
        out_shape=jax.ShapeDtypeStruct((480, 128), BF),
        in_specs=[VMEM] * 2,
        out_specs=VMEM,
        compiler_params=pltpu.CompilerParams(vmem_limit_bytes=4 * 1024 * 1024),
        cost_estimate=pl.CostEstimate(
            flops=4 * 10**9, bytes_accessed=12 * 10**6, transcendentals=0
        ),
        name="relay",
    )(block, grad)


HANDED = ((512, 576), (320, 1440), (256, 4608), (192, 1280), (256, 1280), (512, 1024))


def run_near(volume, swap_core, swap_chip, filter_one, filter_two):
    args = [volume, swap_core, swap_chip, filter_one, filter_two]
    return pl.pallas_call(
        near_part,
        out_shape=[jax.ShapeDtypeStruct(shape, BF) for shape in HANDED],
        in_specs=[VMEM] * len(args),
        out_specs=[VMEM] * len(HANDED),
        scratch_shapes=[near(192, 22 * 128)],
        compiler_params=pltpu.CompilerParams(vmem_limit_bytes=20 * 1024 * 1024),
        cost_estimate=pl.CostEstimate(
            flops=3 * 10**9, bytes_accessed=8 * 10**6, transcendentals=0
        ),
        name="near_part",
    )(*args)


def local_grads(swaps, grad, filter_three, handed, rows):
    tables = [jnp.asarray(t, BF) for t in one_hot_tables()]
    args = [*swaps, grad, filter_three, *handed, *tables]
    return pl.pallas_call(
        body,
        out_shape=[jax.ShapeDtypeStruct((rows // 2, 128), BF)] * 2,
        in_specs=[VMEM] * len(args),
        out_specs=[VMEM] * 2,
        scratch_shapes=[
            near(128, 1728),
            near(256, 8 * 128),
            near(192, 20 * 128),
            near(2304, 1024),
            near(512, 512),
            near(1728, 768),
            near(4608, 256),
            near(512, 512),
            near(512, 512),
            near(512, 1024),
            near(rows, 128),
        ],
        compiler_params=pltpu.CompilerParams(vmem_limit_bytes=LIMIT * 1024 * 1024),
        cost_estimate=pl.CostEstimate(flops=10**10, bytes_accessed=10**7, transcendentals=0),
        name="local_grads",
    )(*args)


def run_finish(mine, other, cells):
    scales = [float(1.0 / np.sqrt(cells / size)) for size in (1.0, 8.0, 64.0)]
    shapes = [(27, 4, 32), (27, 32, 64), (27, 64, 128)]
    outs = pl.pallas_call(
        functools.partial(finish, scales),
        out_shape=[jax.ShapeDtypeStruct(shape, F32) for shape in shapes],
        in_specs=[VMEM] * 2,
        out_specs=[FAR] * 3,
        scratch_shapes=[pltpu.VMEM(shape, F32) for shape in shapes]
        + [pltpu.SemaphoreType.DMA((5,))],
        compiler_params=pltpu.CompilerParams(vmem_limit_bytes=8 * 1024 * 1024),
        name="finish",
    )(mine, other)
    return tuple(o.reshape(3, 3, 3, *o.shape[1:]) for o in outs)


def over_sample(pieces):
    return lax.all_to_all(pieces, "sample", 0, 0, tiled=True)


def over_chips(pieces):
    size = lax.axis_size("space")
    groups = [list(range(core, size, 2)) for core in range(2)]
    return lax.all_to_all(pieces, "space", 0, 0, axis_index_groups=groups, tiled=True)


def total_of(got):
    return got.astype(F32).sum(axis=0).astype(BF)


def swap(values, first):
    size = lax.axis_size("space")
    pairs = [(i, i + 1) for i in range(first, size - 1, 2)]
    return lax.ppermute(values, "space", pairs + [(j, i) for i, j in pairs])


def per_device(volume, grad_out, filter_one, filter_two, filter_three):
    spaces, samples = (lax.axis_size("space"), lax.axis_size("sample"))
    own = volume.reshape(512, 128)
    grad = grad_out.reshape(32, 128)
    f1 = filter_one.reshape(27, 4, 32)
    f2 = filter_two.reshape(27, 32, 64)
    f3 = filter_three.reshape(1728, 128)
    swap_core = swap(own, 0)
    swap_chip = swap(own, 1)
    relay = run_relay(1, swap_core, grad)
    swap_chip2 = swap(relay, 1)
    chip_later = lax.optimization_barrier((swap_chip, relay))[0]
    swap_core2 = swap(run_relay(0, chip_later, grad), 0)
    chips = spaces // 2
    handed = run_near(own, swap_core, swap_chip, f1, f2)
    keep, send = local_grads(
        (swap_core, swap_chip, swap_chip2, swap_core2), grad, f3, handed, spaces * SLOT
    )
    half = (keep.astype(F32) + swap(send, 0).astype(F32)).astype(BF)
    part = total_of(over_chips(half.reshape(chips, SLOT, 128)))
    part = total_of(over_sample(jnp.broadcast_to(part[None], (samples, SLOT, 128))))
    mine = over_chips(jnp.broadcast_to(part[None], (chips, SLOT, 128))).reshape(-1, 128)
    cells = float(samples * spaces * volume.shape[1] * volume.shape[3] * volume.shape[4])
    return run_finish(mine, swap(mine, 0), cells)


def solution(mesh):
    return jax.shard_map(
        per_device,
        mesh=mesh,
        in_specs=(
            P(("sample", "space"), None, None, None, None),
            P(("sample", "space"), None, None, None, None),
            P(),
            P(),
            P(),
        ),
        out_specs=(P(), P(), P()),
        check_vma=False,
    )
```

```python
import functools

import jax
import jax.numpy as jnp
import numpy as np
from jax import lax
from jax.experimental import pallas as pl
from jax.experimental.pallas import tpu as pltpu
from jax.sharding import PartitionSpec as P

BF = jnp.bfloat16
F32 = jnp.float32
SLOT = 72
LIMIT = 44
G_TWO = 1728
G_ONE = 2160
NT = (((1,), (1,)), ((), ()))
TN = (((0,), (0,)), ((), ()))


def table(rows, cols):
    return np.zeros((rows, cols), np.float32)


def one_hot_tables():
    pair = table(256, 128)
    for a in range(2):
        for w in range(64):
            pair[128 * a + 2 * w, 64 * a + w] = 1.0
    squeeze = table(512, 128)
    spread = table(128, 1152)
    grow_g = table(96, 768)
    grow2 = table(128, 512)
    for h in range(4):
        for w in range(32):
            squeeze[128 * h + 2 * w, 32 * h + w] = 1.0
            for kh in range(3):
                for kw in range(3):
                    if 0 <= h + kh - 1 < 4 and 0 <= w + kw - 1 < 32:
                        src = 32 * (h + kh - 1) + w + kw - 1
                        spread[src, 128 * (3 * kh + kw) + 32 * h + w] = 1.0
            for n in range(6):
                src = 32 * (n // 2) + 16 * (h // 2) + w // 2
                grow_g[src, 128 * n + 32 * h + w] = 1.0 / 16
            for d in range(2):
                for u in range(2):
                    grow2[32 * h + w, 128 * h + 64 * d + 2 * w + u] = 1.0 / 16
    grow1 = table(256, 512)
    for e in range(4):
        for w in range(128):
            grow1[64 * e + w // 2, 128 * e + w] = 1.0 / 16
    return [pair, squeeze, spread, grow_g, grow2, grow1]


def dot(a, b):
    return jnp.dot(a, b, preferred_element_type=F32)


def inside(index, count):
    return jnp.logical_and(index >= 0, index < count)


def position():
    return lax.axis_index("space"), lax.axis_size("space")


def taps_of(it):
    kd, kw = (it // 3, it % 3)
    return [kd * 9 + kh * 3 + kw for kh in range(3)]


def taps_back(it):
    kd, kw = (2 - it // 3, 2 - it % 3)
    return [kd * 9 + (2 - kh) * 3 + kw for kh in range(3)]


def band_one(filter_one, t1):
    lane = lax.broadcasted_iota(jnp.int32, (32, 640), 1) % 16
    rows = filter_one[...].astype(F32).reshape(108, 32).astype(BF)
    at = lax.broadcasted_iota(jnp.int32, (108, 640), 1)
    kd = (at >= 192).astype(jnp.int32) + (at >= 384).astype(jnp.int32)
    rest = at - 192 * kd
    kw = (rest >= 64).astype(jnp.int32) + (rest >= 128).astype(jnp.int32)
    c = (rest - 64 * kw) // 16
    kh = rest % 16
    place = 36 * kd + 12 * kh + 4 * kw + c
    here = lax.broadcasted_iota(jnp.int32, (108, 640), 0) == place
    here = jnp.logical_and(here, jnp.logical_and(kh < 3, at < 576))
    perm = jnp.where(here, 0.5, 0.0).astype(BF)
    base = lax.dot_general(rows, perm, TN, preferred_element_type=F32)
    for h in range(16):
        moved = pltpu.roll(base, (h - 1) % 640, 1) if h != 1 else base
        if h == 0:
            moved = jnp.where(lane == 15, 0.0, moved)
        if h == 15:
            moved = jnp.where(lane == 0, 0.0, moved)
        t1[32 * h : 32 * h + 32, :] = moved[:, :576].astype(BF)


def band_two(filter_two, t2):
    taps = []
    for kh in range(3):
        rows = jnp.concatenate([filter_two[taps_of(it)[kh]] for it in range(9)], axis=0)
        taps.append(rows.astype(F32).T * 0.5)
    zero = jnp.zeros((64, 288), F32)
    for s in range(5):
        parts = [taps[p - s + 1] if 0 <= p - s + 1 < 3 else zero for p in range(5)]
        t2[64 * s : 64 * s + 64, :] = jnp.concatenate(parts, axis=1).astype(BF)


def band_two_back(filter_two, t2r):
    for it in range(9):
        v2 = [filter_two[k].astype(F32) for k in taps_back(it)]
        zero = jnp.zeros((32, 64), F32)
        for s in range(-6, 8):
            if -1 <= s <= 2:
                parts = [v2[s + j] if 0 <= s + j <= 2 else zero for j in range(2)]
                tile = jnp.concatenate(parts, axis=1).astype(BF)
            else:
                tile = jnp.zeros((32, 128), BF)
            for m in range(4):
                hp = 2 * m + 1 - s
                if 0 <= hp < 8:
                    t2r[32 * hp : 32 * hp + 32, it * 512 + 128 * m : it * 512 + 128 * m + 128] = tile


def with_column_shifts(rows, x1, at):
    lane = lax.broadcasted_iota(jnp.int32, (64, 128), 1)
    for p in range(rows.shape[0] // 64):
        lanes = slice(128 * (at + p), 128 * (at + p) + 128)
        plane = rows[64 * p : 64 * p + 64, :]
        wide = plane.astype(F32)
        x1[0:64, lanes] = jnp.where(lane == 0, 0.0, pltpu.roll(wide, 1, 1)).astype(BF)
        x1[64:128, lanes] = plane
        x1[128:192, lanes] = jnp.where(lane == 127, 0.0, pltpu.roll(wide, 127, 1)).astype(BF)
    return at + rows.shape[0] // 64


def layer_one(t1, x1, at, scale):
    rhs = jnp.concatenate(
        [x1[:, 128 * (at + kd) : 128 * (at + kd) + 256] for kd in range(3)], axis=0
    )
    half = dot(t1[...], rhs)
    t = jnp.tanh(half)
    act = half + half * t
    act = act[:, :128] + act[:, 128:]
    act = act.reshape(8, 2, 32, 128)
    act = (act[:, 0] + act[:, 1]).reshape(256, 128)
    act = act + pltpu.roll(act, 127, 1)
    return half, t, (act * scale).astype(BF)


def either_of(first_core):
    def either(a, b, lo, hi):
        return jnp.where(first_core, a[lo:hi, :], b[lo:hi, :])

    return either


def near_part(
    vol_own,
    swap_core,
    swap_chip,
    filter_one,
    filter_two,
    filter_three,
    t1,
    t2,
    t2r,
    x1_own,
    pp,
    sl1,
    w3t,
    x1,
):
    me, blocks = position()
    either = either_of(me % 2 == 0)
    w3t[...] = (filter_three[...].astype(F32).T * 0.5).astype(BF)
    band_two_back(filter_two, t2r)
    band_two(filter_two, t2)
    band_one(filter_one, t1)
    at = with_column_shifts(either(swap_chip, swap_core, 64, 512), x1, 0)
    at = with_column_shifts(vol_own[...], x1, at)
    at = with_column_shifts(either(swap_core, swap_chip, 0, 448), x1, at)
    x1_own[...] = x1[:, 768:2048]
    for j in range(10):
        scale = jnp.where(inside(4 * me - 3 + j, 4 * blocks), 0.125, 0.0)
        half, t, act = layer_one(t1, x1, 2 * j, scale)
        if 3 <= j < 7:
            slope = (1.0 + t) + half * (1.0 - t * t)
            sl1[:, 256 * (j - 3) : 256 * (j - 3) + 256] = slope.astype(BF)
        pp[:, 128 * j : 128 * j + 128] = act


def body(
    swap_core,
    swap_chip,
    swap_chip2,
    swap_core2,
    grad_own,
    filter_three,
    t1,
    t2,
    t2r,
    x1,
    pp_near,
    sl1,
    w3t,
    pair,
    squeeze,
    spread,
    grow_g,
    grow2,
    grow1,
    kept,
    sent,
    pp,
    xo,
    x2,
    q,
    x3,
    d2c,
    sl2,
    d2,
    d1,
    out,
):
    me, blocks = position()
    either = either_of(me % 2 == 0)

    at = with_column_shifts(either(swap_chip2, swap_core2, 0, 448), xo, 0)
    at = with_column_shifts(either(swap_chip, swap_core, 0, 192), xo, at)
    at = with_column_shifts(either(swap_core, swap_chip, 320, 512), xo, at)
    at = with_column_shifts(either(swap_core2, swap_chip2, 0, 448), xo, at)
    for j in (0, 1, 2, 3, 14, 15, 16, 17):
        scale = jnp.where(inside(4 * me - 7 + j, 4 * blocks), 0.125, 0.0)
        act = layer_one(t1, xo, 2 * j if j < 4 else 10 + 2 * (j - 14), scale)[2]
        lo = 128 * (j if j < 4 else j - 10)
        pp[:, lo : lo + 128] = act

    def pooled_plane(j):
        if 4 <= j < 14:
            return pp_near[:, 128 * (j - 4) : 128 * (j - 4) + 128]
        lo = 128 * (j if j < 4 else j - 10)
        return pp[:, lo : lo + 128]

    col64 = lax.broadcasted_iota(jnp.int32, (256, 128), 1) % 64
    first_col, last_col = (col64 == 0, col64 == 63)
    for first in range(17):
        both = jnp.concatenate([pooled_plane(first), pooled_plane(first + 1)], axis=1)
        got = dot(both, pair[...])
        moved = (
            jnp.where(first_col, 0.0, pltpu.roll(got, 1, 1)).astype(BF),
            got.astype(BF),
            jnp.where(last_col, 0.0, pltpu.roll(got, 127, 1)).astype(BF),
        )
        for kd in range(3):
            m = (first - kd) // 2
            if (first - kd) % 2 == 0 and 0 <= m < 8:
                for kw in range(3):
                    k = 3 * kd + kw
                    x2[256 * k : 256 * k + 256, m * 128 : m * 128 + 128] = moved[kw]

    for c in range(4):
        lanes = slice(c * 256, c * 256 + 256)
        for g in range(2):
            rhs = jnp.concatenate(
                [
                    x2[256 * it + 32 * p : 256 * it + 32 * p + 32, lanes]
                    for p in range(3 * g, 3 * g + 5)
                    for it in range(9)
                ],
                axis=0,
            )
            half = dot(t2[64 * g : 64 * g + 256, :], rhs)
            t = jnp.tanh(half)
            if 1 <= c < 3:
                slope = (1.0 + t) + half * (1.0 - t * t)
                sl2[256 * g : 256 * g + 256, c * 256 - 256 : c * 256] = slope.astype(BF)
            act = (half + half * t).reshape(2, 2, 64, 256)
            act = (act[:, 0] + act[:, 1]).reshape(128, 256)
            for u in range(2):
                tile = act[:, 128 * u : 128 * u + 128]
                tile = tile + pltpu.roll(tile, 64, 1)
                tile = tile + pltpu.roll(tile, 127, 1)
                m = 2 * c + u
                scale = jnp.where(inside(2 * me - 3 + m, 2 * blocks), 0.125, 0.0)
                tile = (tile * scale).astype(BF)
                for h in range(2):
                    lo = 128 * (2 * g + h)
                    q[64 * m : 64 * m + 64, lo : lo + 128] = tile[64 * h : 64 * h + 64, :]

    packed = dot(q[...], squeeze[...]).astype(BF)
    got = dot(packed, spread[...]).astype(BF)
    for kd in range(3):
        for s in range(9):
            k = 9 * kd + s
            for n in range(6):
                x3[64 * k : 64 * k + 64, 128 * n : 128 * n + 128] = got[
                    64 * (n + kd) : 64 * (n + kd) + 64, 128 * s : 128 * s + 128
                ]
    rows = jnp.concatenate(
        [
            either(swap_chip2, swap_core2, 448, 480),
            grad_own[...],
            either(swap_core2, swap_chip2, 448, 480),
        ],
        axis=0,
    )
    grown = dot(rows.astype(F32).T.astype(BF), grow_g[...])
    half = dot(w3t[...], x3[...])
    t = jnp.tanh(half)
    d3 = (grown * ((1.0 + t) + half * (1.0 - t * t))).astype(BF)

    out[:G_TWO, :] = lax.dot_general(
        x3[:, 256:512], d3[:, 256:512], NT, preferred_element_type=F32
    ).astype(BF)

    lane = lax.broadcasted_iota(jnp.int32, (64, 128), 1)
    col, line = (lane % 32, lane // 32)
    masks = []
    for b in range(3):
        for c in range(3):
            keep = inside(col + 1 - c, 32)
            masks.append(jnp.logical_and(keep, inside(line + 1 - b, 4)))
    lhs = jnp.concatenate([filter_three[576 * a : 576 * a + 576, :] for a in range(3)], axis=1)
    grown = []
    for pair_at in range(2):
        rhs = jnp.concatenate(
            [
                d3[:, 128 * (2 * pair_at + 2 - a) : 128 * (2 * pair_at + 2 - a) + 256]
                for a in range(3)
            ],
            axis=0,
        )
        got = dot(lhs, rhs)
        for u in range(2):
            total = None
            for b in range(3):
                for c in range(3):
                    s = 3 * b + c
                    part = got[64 * s : 64 * s + 64, 128 * u : 128 * u + 128]
                    move_by = -(32 * (1 - b) + 1 - c) % 128
                    if move_by:
                        part = jnp.where(masks[s], pltpu.roll(part, move_by, 1), 0.0)
                    total = part if total is None else total + part
            n = 2 * pair_at + u
            scale = jnp.where(inside(2 * me - 1 + n, 2 * blocks), 1.0, 0.0)
            grown.append((total * scale).astype(BF))
    back = dot(jnp.concatenate(grown, axis=0), grow2[...])
    for h in range(8):
        rows = slice(64 * h, 64 * h + 64)
        for n in range(4):
            lanes = slice(128 * n, 128 * n + 128)
            source = back[64 * n : 64 * n + 64, 128 * (h // 2) : 128 * (h // 2) + 128]
            d2[rows, lanes] = (source * sl2[rows, lanes].astype(F32)).astype(BF)

    for part in range(2):
        rows = slice(256 * part, 256 * part + 256)
        for start in range(1, 6):
            u = start // 2
            got = d2[rows, 128 * u : 128 * u + 128].astype(F32)
            if start % 2:
                after = d2[rows, 128 * u + 128 : 128 * u + 256].astype(F32)
                lane = lax.broadcasted_iota(jnp.int32, (256, 128), 1)
                got = jnp.where(lane < 64, pltpu.roll(got, 64, 1), pltpu.roll(after, 64, 1))
            moved = (
                jnp.where(first_col, 0.0, pltpu.roll(got, 1, 1)).astype(BF),
                got.astype(BF),
                jnp.where(last_col, 0.0, pltpu.roll(got, 127, 1)).astype(BF),
            )
            for kd in range(3):
                for m in range(2):
                    if 1 + kd + 2 * m == start:
                        for kw in range(3):
                            lo = 512 * (3 * kd + kw) + 256 * part
                            d2c[lo : lo + 256, 128 * m : 128 * m + 128] = moved[kw]
    back = dot(t2r[...], d2c[...]).astype(BF)
    back = dot(back, grow1[...])
    for h in range(16):
        rows = slice(32 * h, 32 * h + 32)
        source = back[32 * (h // 2) : 32 * (h // 2) + 32, :]
        for e in range(8):
            lanes = slice(128 * e, 128 * e + 128)
            delta = source[:, 128 * (e // 2) : 128 * (e // 2) + 128] * sl1[rows, lanes].astype(F32)
            d1[rows, lanes] = delta.astype(BF)

    lane16 = lax.broadcasted_iota(jnp.int32, (16, 128), 1)
    all_two = lax.dot_general(
        x2[:, 384:640], d2[:, 128:384], NT, preferred_element_type=F32
    )
    for it in range(9):
        got = all_two[256 * it : 256 * it + 256, :]
        for kh, k in enumerate(taps_of(it)):
            totals = [None, None]
            for h in range(8):
                hp = h + kh - 1
                if 0 <= hp < 8:
                    part = got[32 * hp : 32 * hp + 32, 128 * (h // 2) : 128 * (h // 2) + 128]
                    now = totals[h % 2]
                    totals[h % 2] = part if now is None else now + part
            low = totals[0] + pltpu.roll(totals[1], 64, 1)
            high = pltpu.roll(totals[0], 64, 1) + totals[1]
            out[G_TWO + k * 16 : G_TWO + k * 16 + 16, :] = jnp.where(
                lane16 < 64, low[:16], high[16:]
            ).astype(BF)

    lhs = jnp.concatenate([x1[:, 128 * kd : 128 * kd + 1024] for kd in range(3)], axis=0)
    got = lax.dot_general(lhs, d1[...], NT, preferred_element_type=F32)
    row = lax.broadcasted_iota(jnp.int32, (576, 128), 0) % 16
    col = lax.broadcasted_iota(jnp.int32, (576, 128), 1) // 32
    lane36 = lax.broadcasted_iota(jnp.int32, (36, 128), 1)
    packed = jnp.zeros((36, 128), F32)
    for kh in range(3):
        total = jnp.zeros((576, 128), F32)
        for u in range(4):
            keep = row == col + (4 * u + kh - 1)
            total = total + jnp.where(keep, got[:, 128 * u : 128 * u + 128], 0.0)
        total = total.reshape(36, 16, 128).sum(axis=1)
        total = total + pltpu.roll(total, 64, 1)
        total = total + pltpu.roll(total, 32, 1)
        packed = packed + jnp.where(lane36 // 32 == kh, total, 0.0)
    out[G_ONE : G_ONE + 48, :] = jnp.concatenate(
        [packed, jnp.zeros((12, 128), F32)], axis=0
    ).astype(BF)
    out[G_ONE + 48 :, :] = jnp.zeros((out.shape[0] - G_ONE - 48, 128), BF)
    half_rows = kept.shape[0]
    mine = pl.multiple_of(me % 2 * half_rows, half_rows)
    kept[...] = out[pl.ds(mine, half_rows), :]
    sent[...] = out[pl.ds(half_rows - mine, half_rows), :]


def finish(scales, mine, other, one_far, two_far, three_far, one, two, three, sems):
    first_core = position()[0] % 2 == 0
    half_rows = mine.shape[0]

    def rows(at, count):
        parts = []
        while count:
            use = min(count, half_rows - at % half_rows)
            here = slice(at % half_rows, at % half_rows + use)
            flag = first_core if at < half_rows else jnp.logical_not(first_core)
            parts.append(jnp.where(flag, mine[here, :], other[here, :]).astype(F32))
            at, count = (at + use, count - use)
        return parts[0] if len(parts) == 1 else jnp.concatenate(parts, axis=0)

    copies = []

    def leave(near_ref, far_ref):
        copies.append(pltpu.make_async_copy(near_ref, far_ref, sems.at[len(copies)]))
        copies[-1].start()

    for k in range(27):
        got = rows(G_TWO + 16 * k, 16) * scales[1]
        two[k, 0:16, :] = got[:, :64]
        two[k, 16:32, :] = got[:, 64:]
    leave(two, two_far)
    got = rows(G_ONE, 48) * scales[0]
    for it in range(9):
        for kh, k in enumerate(taps_of(it)):
            one[k] = got[4 * it : 4 * it + 4, 32 * kh : 32 * kh + 32]
    leave(one, one_far)
    for third in range(3):
        for k in range(9 * third, 9 * third + 9):
            three[k] = rows(64 * k, 64) * scales[2]
        here = slice(9 * third, 9 * third + 9)
        leave(three.at[here], three_far.at[here])
    for copy in copies:
        copy.wait()


VMEM = pl.BlockSpec(memory_space=pltpu.VMEM)


def near(*shape):
    return pltpu.VMEM(shape, BF)


FAR = pl.BlockSpec(memory_space=pl.ANY)
def relay_planes(last_seven, block, grad, out):
    flag = position()[0] % 2 == last_seven
    out[:448, :] = jnp.where(flag, block[64:, :], block[:448, :])
    out[448:, :] = grad[...]


def run_relay(last_seven, block, grad):
    return pl.pallas_call(
        functools.partial(relay_planes, last_seven),
        out_shape=jax.ShapeDtypeStruct((480, 128), BF),
        in_specs=[VMEM] * 2,
        out_specs=VMEM,
        compiler_params=pltpu.CompilerParams(vmem_limit_bytes=4 * 1024 * 1024),
        cost_estimate=pl.CostEstimate(
            flops=4 * 10**9, bytes_accessed=12 * 10**6, transcendentals=0
        ),
        name="relay",
    )(block, grad)


HANDED = ((512, 576), (320, 1440), (256, 4608), (192, 1280), (256, 1280), (512, 1024), (128, 1728))


def run_near(volume, swap_core, swap_chip, filter_one, filter_two, filter_three):
    args = [volume, swap_core, swap_chip, filter_one, filter_two, filter_three]
    return pl.pallas_call(
        near_part,
        out_shape=[jax.ShapeDtypeStruct(shape, BF) for shape in HANDED],
        in_specs=[VMEM] * len(args),
        out_specs=[VMEM] * len(HANDED),
        scratch_shapes=[near(192, 22 * 128)],
        compiler_params=pltpu.CompilerParams(vmem_limit_bytes=20 * 1024 * 1024),
        cost_estimate=pl.CostEstimate(
            flops=3 * 10**9, bytes_accessed=8 * 10**6, transcendentals=0
        ),
        name="near_part",
    )(*args)


def local_grads(swaps, grad, filter_three, handed, rows):
    tables = [jnp.asarray(t, BF) for t in one_hot_tables()]
    args = [*swaps, grad, filter_three, *handed, *tables]
    return pl.pallas_call(
        body,
        out_shape=[jax.ShapeDtypeStruct((rows // 2, 128), BF)] * 2,
        in_specs=[VMEM] * len(args),
        out_specs=[VMEM] * 2,
        scratch_shapes=[
            near(256, 8 * 128),
            near(192, 20 * 128),
            near(2304, 1024),
            near(512, 512),
            near(1728, 768),
            near(4608, 256),
            near(512, 512),
            near(512, 512),
            near(512, 1024),
            near(rows, 128),
        ],
        compiler_params=pltpu.CompilerParams(vmem_limit_bytes=LIMIT * 1024 * 1024),
        cost_estimate=pl.CostEstimate(flops=10**10, bytes_accessed=10**7, transcendentals=0),
        name="local_grads",
    )(*args)


def run_finish(mine, other, cells):
    scales = [float(1.0 / np.sqrt(cells / size)) for size in (1.0, 8.0, 64.0)]
    shapes = [(27, 4, 32), (27, 32, 64), (27, 64, 128)]
    outs = pl.pallas_call(
        functools.partial(finish, scales),
        out_shape=[jax.ShapeDtypeStruct(shape, F32) for shape in shapes],
        in_specs=[VMEM] * 2,
        out_specs=[FAR] * 3,
        scratch_shapes=[pltpu.VMEM(shape, F32) for shape in shapes]
        + [pltpu.SemaphoreType.DMA((5,))],
        compiler_params=pltpu.CompilerParams(vmem_limit_bytes=8 * 1024 * 1024),
        name="finish",
    )(mine, other)
    return tuple(o.reshape(3, 3, 3, *o.shape[1:]) for o in outs)


def over_sample(pieces):
    return lax.all_to_all(pieces, "sample", 0, 0, tiled=True)


def over_chips(pieces):
    size = lax.axis_size("space")
    groups = [list(range(core, size, 2)) for core in range(2)]
    return lax.all_to_all(pieces, "space", 0, 0, axis_index_groups=groups, tiled=True)


def total_of(got):
    return got.astype(F32).sum(axis=0).astype(BF)


def swap(values, first):
    size = lax.axis_size("space")
    pairs = [(i, i + 1) for i in range(first, size - 1, 2)]
    return lax.ppermute(values, "space", pairs + [(j, i) for i, j in pairs])


def per_device(volume, grad_out, filter_one, filter_two, filter_three):
    spaces, samples = (lax.axis_size("space"), lax.axis_size("sample"))
    own = volume.reshape(512, 128)
    grad = grad_out.reshape(32, 128)
    f1 = filter_one.reshape(27, 4, 32)
    f2 = filter_two.reshape(27, 32, 64)
    f3 = filter_three.reshape(1728, 128)
    swap_core = swap(own, 0)
    swap_chip = swap(own, 1)
    relay = run_relay(1, swap_core, grad)
    swap_chip2 = swap(relay, 1)
    chip_later = lax.optimization_barrier((swap_chip, relay))[0]
    swap_core2 = swap(run_relay(0, chip_later, grad), 0)
    chips = spaces // 2
    handed = run_near(own, swap_core, swap_chip, f1, f2, f3)
    keep, send = local_grads(
        (swap_core, swap_chip, swap_chip2, swap_core2), grad, f3, handed, spaces * SLOT
    )
    half = (keep.astype(F32) + swap(send, 0).astype(F32)).astype(BF)
    part = total_of(over_chips(half.reshape(chips, SLOT, 128)))
    part = total_of(over_sample(jnp.broadcast_to(part[None], (samples, SLOT, 128))))
    mine = over_chips(jnp.broadcast_to(part[None], (chips, SLOT, 128))).reshape(-1, 128)
    cells = float(samples * spaces * volume.shape[1] * volume.shape[3] * volume.shape[4])
    return run_finish(mine, swap(mine, 0), cells)


def solution(mesh):
    return jax.shard_map(
        per_device,
        mesh=mesh,
        in_specs=(
            P(("sample", "space"), None, None, None, None),
            P(("sample", "space"), None, None, None, None),
            P(),
            P(),
            P(),
        ),
        out_specs=(P(), P(), P()),
        check_vma=False,
    )
```
